32 devices in a mesh: frame: 4 (over z), height: 8 (over y, x, core).
Axes of the slice: x: 2, y: 2, z: 4, core: 2. Of those that a mesh axis runs over, the one named last changes fastest.
Arguments:
- video: bfloat16 [33, 16, 32, 256], P(None, 'height', 'frame'), may hold values from -48 to 48
- frame_counts: int32 [4], replicated, may hold values from 1 to 18, 33 in all
- temporal_weight: bfloat16 [6912, 256], replicated, may hold values from -0.125 to 0.125
- temporal_bias: float32 [256], replicated, may hold values from -4 to 4
- first_gain: float32 [256], replicated, may hold values from 0.1 to 1.9
- first_shift: float32 [256], replicated, may hold values from -3 to 3
- first_weight: bfloat16 [2304, 256], P('height'), may hold values from -0.125 to 0.125
- first_bias: float32 [256], replicated, may hold values from -4 to 4
- second_gain: float32 [256], replicated, may hold values from 0.1 to 1.9
- second_shift: float32 [256], replicated, may hold values from -3 to 3
- second_weight: bfloat16 [2304, 256], P('height'), may hold values from -0.125 to 0.125
- second_bias: float32 [256], replicated, may hold values from -4 to 4
Outputs:
- owned: bfloat16 [72, 16, 32, 256], P('frame', 'height')
The draws below stay inside these ranges and needn't reach their ends.
Inputs may be any that keep to these rules, and one draw needn't show every extreme that they name: frame_counts[k] consecutive frames belong to index k of frame; the counts add up to 33 and the largest is exactly 18.
All inputs are finite; a program needn't handle non-finite values.
Results may differ from the reference program's by a relative error of at most 0.0055.
Values may be sent and summed in bfloat16 or wider, within the bound.
No kernel may reach another device: no remote copies, remote signals or barrier semaphores. Data moves between devices by JAX's collectives and lax.ppermute only.
A program may use at most 64 MiB of HBM per device.

```python
import math
import jax
import jax.numpy as jnp
import numpy as np
from jax import lax

C = 256
GROUPS = 32
FRAMES = 33
H = 16
W = 32
MOST = 18
SLOTS = 72
N_FRAME = 4


def draw_video(key, part):
    key_base, key_rows, key_cols = jax.random.split(key, 3)
    position = jnp.arange(H, dtype=jnp.float32) / max(H - 1, 1)
    row_log = math.log(3.0) * (position - 0.5) + jax.random.uniform(key_rows, (H,), jnp.float32, -0.6, 0.6)
    col_log = jax.random.uniform(key_cols, (W,), jnp.float32, -0.8, 0.8)
    base = jnp.clip(jax.random.normal(key_base, (FRAMES, H, W, C), jnp.float32), -6.0, 6.0)
    scaled = base * jnp.exp(row_log)[None, :, None, None] * jnp.exp(col_log)[None, None, :, None]
    return jnp.clip(scaled, -48.0, 48.0).astype(jnp.bfloat16)


def shard_levels(stream_key, shape, cuts, least, high):
    factor_of = 1.0
    for dim, shards_of in cuts:
        draws = jax.random.uniform(jax.random.fold_in(jax.random.fold_in(stream_key, 6), dim), (shards_of,), jnp.float32, least / len(cuts), high / len(cuts))
        factor_of = factor_of * jnp.repeat(jnp.exp(draws), shape[dim] // shards_of).reshape((-1,) + (1,) * (len(shape) - 1 - dim))
    return factor_of


def split_up(number_of, total, limit, slope):
    weights = [(1 << 20) // math.isqrt(standing ** slope) + 1 for standing in range(2, number_of + 1)]
    surplus, given = total - limit - (number_of - 1), [1] * (number_of - 1)
    while surplus > 0:
        movable = [i for i in range(number_of - 1) if given[i] < limit]
        mass, budget = sum([weights[i] for i in movable]), surplus
        for i in movable:
            addition = min(limit - given[i], max(1, budget * weights[i] // mass), surplus)
            given[i] = given[i] + addition
            surplus = surplus - addition
    return np.array([limit] + given)


def ragged(key, number_of, total, most, lean):
    if number_of == 2:
        one = jax.random.randint(key, (), max(1, total - most), min(most, total - 1) + 1)
        return jnp.stack([one, total - one])
    sizes = jnp.asarray(split_up(number_of, total, most, lean), jnp.int32)
    pairs = (number_of - 1) // 2
    giver, taker = sizes[1:1 + 2 * pairs:2], sizes[2:2 + 2 * pairs:2]
    margin = jnp.minimum(giver - 1, most - taker)
    shifted = jax.random.randint(jax.random.fold_in(key, 1), (pairs,), 0, 1 << 20) % (margin + 1)
    sizes = sizes.at[1:1 + 2 * pairs:2].set(giver - shifted).at[2:2 + 2 * pairs:2].set(taker + shifted)
    return sizes[jax.random.permutation(jax.random.fold_in(key, 2), number_of)]


def normal_values(stream_key, extent, deviation, reach, cuts=(), kind=jnp.bfloat16):
    gain = shard_levels(stream_key, extent, cuts, -0.22, 0.18) if cuts else 1.0
    drawn = jax.random.normal(stream_key, extent, jnp.float32) * deviation * gain
    return jnp.minimum(jnp.maximum(drawn, -reach), reach).astype(kind)


def setup_inputs(seed: int = 0) -> dict:
    streams_of = jax.random.split(jax.random.key(seed), 13)
    video = draw_video(jax.random.fold_in(streams_of[12], 71), 0)
    frame_counts = ragged(streams_of[1], N_FRAME, FRAMES, MOST, 2).astype(jnp.int32)
    temporal_weight = normal_values(streams_of[2], (27 * C, C), (9 * C) ** -0.5, 0.125)
    temporal_bias = normal_values(streams_of[3], (C,), 1.0, 4.0, (), jnp.float32)
    first_gain = jnp.clip(1.0 + 0.18 * jax.random.normal(streams_of[4], (C,), jnp.float32), 0.1, 1.9)
    first_shift = normal_values(streams_of[5], (C,), 0.5, 3.0, (), jnp.float32)
    first_weight = normal_values(streams_of[6], (9 * C, C), (9 * C) ** -0.5, 0.125, ((0, 8),))
    first_bias = normal_values(streams_of[7], (C,), 1.0, 4.0, (), jnp.float32)
    second_gain = jnp.clip(1.0 + 0.18 * jax.random.normal(streams_of[8], (C,), jnp.float32), 0.1, 1.9)
    second_shift = normal_values(streams_of[9], (C,), 0.5, 3.0, (), jnp.float32)
    second_weight = normal_values(streams_of[10], (9 * C, C), (9 * C) ** -0.5, 0.125, ((0, 8),))
    second_bias = normal_values(streams_of[11], (C,), 1.0, 4.0, (), jnp.float32)
    return {"video": video, "frame_counts": frame_counts, "temporal_weight": temporal_weight, "temporal_bias": temporal_bias, "first_gain": first_gain, "first_shift": first_shift, "first_weight": first_weight, "first_bias": first_bias, "second_gain": second_gain, "second_shift": second_shift, "second_weight": second_weight, "second_bias": second_bias}


def spatial_patches(padded, row_count, col_count):
    pieces = []
    for row_tap in range(3):
        for col_tap in range(3):
            pieces.append(padded[..., row_tap:row_tap + row_count, col_tap:col_tap + col_count, :])
    return jnp.concatenate(pieces, axis=-1)

def group_act(values, gain_row, shift_row):
    grouped = values.reshape(H, W, GROUPS, C // GROUPS)
    group_mean = lax.optimization_barrier(jnp.mean(grouped, axis=(0, 1, 3), keepdims=True))
    centered = grouped - group_mean
    group_var = lax.optimization_barrier(jnp.mean(centered * centered, axis=(0, 1, 3), keepdims=True))
    normed = (centered * lax.rsqrt(group_var + 1e-06)).reshape(H, W, C) * gain_row + shift_row
    return jax.nn.silu(normed).astype(jnp.bfloat16)

def conv_frame(inputs, weight, offset_bias):
    padded = jnp.pad(inputs, ((1, 1), (1, 1), (0, 0)))
    patches = spatial_patches(padded, H, W).reshape(H * W, 9 * C)
    summed = jnp.dot(patches, weight, preferred_element_type=jnp.float32) + offset_bias
    return summed.reshape(H, W, C)

def reference(video, frame_counts, temporal_weight, temporal_bias, first_gain, first_shift, first_weight, first_bias, second_gain, second_shift, second_weight, second_bias):
    activated = jax.nn.silu(video.astype(jnp.float32)).astype(jnp.bfloat16)
    causal = jnp.pad(activated, ((2, 0), (1, 1), (1, 1), (0, 0)))

    def one_frame(frame_idx):
        window = lax.dynamic_slice_in_dim(causal, frame_idx, 3, 0)
        accumulated = jnp.zeros((H * W, C), jnp.float32)
        for tap_time in range(3):
            patches = spatial_patches(window[tap_time], H, W).reshape(H * W, 9 * C)
            accumulated = accumulated + jnp.dot(patches, temporal_weight[tap_time * 9 * C:(tap_time + 1) * 9 * C], preferred_element_type=jnp.float32)
        source = lax.dynamic_index_in_dim(video, frame_idx, 0, keepdims=False)
        blended = (source.astype(jnp.float32) + accumulated.reshape(H, W, C) + temporal_bias).astype(jnp.bfloat16)
        first_in = group_act(blended.astype(jnp.float32), first_gain, first_shift)
        first_out = conv_frame(first_in, first_weight, first_bias).astype(jnp.bfloat16)
        second_in = group_act(first_out.astype(jnp.float32), second_gain, second_shift)
        return (blended.astype(jnp.float32) + conv_frame(second_in, second_weight, second_bias)).astype(jnp.bfloat16)
    decoded = lax.map(one_frame, jnp.arange(FRAMES, dtype=jnp.int32))
    offsets = jnp.cumsum(frame_counts) - frame_counts
    slot_ids = jnp.arange(SLOTS, dtype=jnp.int32)
    owner_idx = slot_ids // MOST
    within = slot_ids - owner_idx * MOST
    first_frame = jnp.take(offsets, owner_idx)
    frame_total = jnp.take(frame_counts, owner_idx)
    source_idx = jnp.clip(first_frame + within, 0, FRAMES - 1).astype(jnp.int32)
    picked = jnp.take(decoded, source_idx, axis=0)
    return jnp.where((within < frame_total)[:, None, None, None], picked, jnp.zeros_like(picked))
```

```python
import functools

import jax
import jax.numpy as jnp
from jax import lax
from jax.experimental import pallas as pl
from jax.experimental.pallas import tpu as pltpu
from jax.sharding import Mesh, PartitionSpec as P

GROUPS = 32
EPS = 1e-06
VMEM = pl.BlockSpec(memory_space=pltpu.VMEM)
SMEM = pl.BlockSpec(memory_space=pltpu.SMEM)
F32, BF16 = jnp.float32, jnp.bfloat16


def up_to(number, multiple):
    return -(-number // multiple) * multiple


def silu(values):
    half = 0.5 * values
    return half + half * jnp.tanh(half)


def with_column_taps(values):
    axis, width = values.ndim - 2, values.shape[-2]
    column = lax.broadcasted_iota(jnp.int32, values.shape, axis)
    before = jnp.where(column == 0, 0.0, pltpu.roll(values, 1, axis))
    after = jnp.where(column == width - 1, 0.0, pltpu.roll(values, width - 1, axis))
    return jnp.concatenate([before.astype(BF16), values.astype(BF16), after.astype(BF16)], axis=-1)


def frame_offset(counts_ref, owner):
    offset = jnp.int32(0)
    for index in range(counts_ref.shape[0]):
        offset = offset + jnp.where(index < owner, counts_ref[index], 0)
    return offset


def pick_body(halves, frames_each, counts_ref, video_ref, out_ref):
    frames = video_ref.shape[0]
    slots = out_ref.shape[1]
    for owner in range(counts_ref.shape[0]):
        offset = frame_offset(counts_ref, owner)
        for half in range(halves):
            for slot in range(slots):
                frame = offset + (half * frames_each + slot - 2)
                values = video_ref[jnp.clip(frame, 0, frames - 1)]
                out_ref[owner * halves + half, slot] = jnp.where(
                    frame >= 0, values, jnp.zeros_like(values)
                )


def temporal_body(halves, rows, part_ref, weight_ref, bias_ref, total_ref, taps_ref):
    peers, slots, cells, channels = part_ref.shape
    columns = cells // rows
    frames_each, all_rows, width = total_ref.shape[:3]

    def place(slot, _):
        for half in range(halves):
            for row in range(rows):
                values = jnp.concatenate(
                    [
                        part_ref[peer * halves + half, slot].astype(F32)[
                            row * columns : (row + 1) * columns
                        ]
                        for peer in range(peers // halves)
                    ],
                    axis=0,
                )
                at = half * rows + row
                taps_ref[slot, at] = with_column_taps(silu(values))

                @pl.when(slot >= 2)
                def _():
                    total_ref[slot - 2, at] = values + bias_ref[...]

        return 0

    lax.fori_loop(0, slots, place, 0)
    depth = 3 * channels
    for row_tap in range(3):
        low, high = max(0, 1 - row_tap), min(all_rows, all_rows + 1 - row_tap)
        for time_tap in range(3):
            patches = taps_ref[
                time_tap : time_tap + frames_each, low + row_tap - 1 : high + row_tap - 1
            ]
            start = (time_tap * 3 + row_tap) * depth
            product = jnp.dot(
                patches.reshape(frames_each * (high - low) * width, depth),
                weight_ref[start : start + depth],
                preferred_element_type=F32,
            )
            total_ref[:, low:high] += product.reshape(frames_each, high - low, width, channels)


def write_stats(field_ref, stats_ref):
    frames_each, rows, width, channels = field_ref.shape
    span = stats_ref.shape[0] // 3
    sums, squares = [], []
    for frame in range(frames_each):
        values = field_ref[frame].astype(F32).reshape(rows * width, channels)
        part_sum = jnp.sum(values, axis=0, keepdims=True)
        centered = values - part_sum * (1.0 / (rows * width))
        sums.append(part_sum)
        squares.append(jnp.sum(centered * centered, axis=0, keepdims=True))
    pad = [jnp.zeros((span - 2 * frames_each, channels), F32)] if span > 2 * frames_each else []
    rest = jnp.concatenate(sums + squares + pad, axis=0)
    for piece in range(3):
        rounded = rest.astype(BF16)
        stats_ref[piece * span : (piece + 1) * span] = rounded
        rest = rest - rounded.astype(F32)


def write_messages(field_ref, down_ref, up_ref, stats_ref):
    frames_each, rows, width, channels = field_ref.shape
    write_stats(field_ref, stats_ref)
    edge = frames_each * width
    down_ref[:edge] = field_ref[:, rows - 1].reshape(edge, channels)
    up_ref[:edge] = field_ref[:, 0].reshape(edge, channels)
    down_ref[edge:] = stats_ref[...]
    up_ref[edge:] = stats_ref[...]


def borders_body(
    n_pair,
    total_ref,
    above_ref,
    below_ref,
    weight_ref,
    blended_ref,
    down_ref,
    up_ref,
    stats_ref,
    taps_ref,
):
    frames_each, rows, width, channels = total_ref.shape
    slots = above_ref.shape[0]
    depth = 3 * channels

    def place(slot, _):
        taps_ref[0, slot] = with_column_taps(silu(above_ref[slot].astype(F32)))
        taps_ref[1, slot] = with_column_taps(silu(below_ref[slot].astype(F32)))
        return 0

    lax.fori_loop(0, slots, place, 0)
    for side, row, row_tap in ((0, 0, 0), (1, rows - 1, 2)):
        summed = total_ref[:, row].reshape(frames_each * width, channels)
        for time_tap in range(3):
            patches = taps_ref[side, time_tap : time_tap + frames_each]
            start = (time_tap * 3 + row_tap) * depth
            summed = summed + jnp.dot(
                patches.reshape(frames_each * width, depth),
                weight_ref[start : start + depth],
                preferred_element_type=F32,
            )
        blended_ref[:, row] = summed.reshape(frames_each, width, channels).astype(BF16)
    blended_ref[:, 1 : rows - 1] = total_ref[:, 1 : rows - 1].astype(BF16)
    write_messages(blended_ref, down_ref, up_ref, stats_ref)


def group_total(values, width_group):
    lane = lax.broadcasted_iota(jnp.int32, values.shape, 1)
    size, step = values.shape[1], 1
    while step < width_group:
        upper = (lane // step) % 2 == 1
        values = values + jnp.where(
            upper, pltpu.roll(values, step, 1), pltpu.roll(values, size - step, 1)
        )
        step *= 2
    return values


def scale_and_offset(frames_each, cells, stats, gain_ref, shift_ref):
    channels = stats[0].shape[1]
    width_group = channels // GROUPS
    span = stats[0].shape[0] // 3
    parts = []
    for packed in stats:
        pieces = [packed[i * span : (i + 1) * span].astype(F32) for i in range(3)]
        parts.append(pieces[0] + (pieces[1] + pieces[2]))
    sums = [part[:frames_each] for part in parts]
    squares = [part[frames_each : 2 * frames_each] for part in parts]
    sample = float(cells * len(parts) * width_group)
    mean = group_total(functools.reduce(jnp.add, sums), width_group) * (1.0 / sample)
    spread = functools.reduce(jnp.add, squares)
    for part_sum in sums:
        apart = part_sum * (1.0 / cells) - mean
        spread = spread + float(cells) * apart * apart
    variance = group_total(spread, width_group) * (1.0 / sample)
    scale = lax.rsqrt(variance + EPS) * gain_ref[...]
    return scale, shift_ref[...] - mean * scale


def normed_taps(
    n_pair, index_ref, field_ref, above_ref, below_ref, stats, gain_ref, shift_ref, taps_ref,
    scale_ref, offset_ref,
):
    frames_each, rows, width, channels = field_ref.shape
    scale, offset = scale_and_offset(frames_each, rows * width, stats, gain_ref, shift_ref)
    for frame in range(frames_each):
        scale_ref[frame] = scale[frame : frame + 1]
        offset_ref[frame] = offset[frame : frame + 1]
    pair = index_ref[0]
    top = jnp.where(pair > 0, 1.0, 0.0)
    bottom = jnp.where(pair < n_pair - 1, 1.0, 0.0)

    def place(frame, _):
        scale_row, offset_row = scale_ref[frame], offset_ref[frame]
        for row in range(rows):
            values = field_ref[frame, row].astype(F32) * scale_row + offset_row
            taps_ref[frame, row + 1] = with_column_taps(silu(values))
        edge = pl.ds(pl.multiple_of(frame * width, width), width)
        values = silu(above_ref[edge].astype(F32) * scale_row + offset_row) * top
        taps_ref[frame, 0] = with_column_taps(values)
        values = silu(below_ref[edge].astype(F32) * scale_row + offset_row) * bottom
        taps_ref[frame, rows + 1] = with_column_taps(values)
        return 0

    lax.fori_loop(0, frames_each, place, 0)


def gather_weight(n_pair, which, index_ref, same_ref, other_ref, weight_ref):
    depth = weight_ref.shape[0] // (2 * n_pair)
    if same_ref.shape[0] != n_pair:
        weight_ref[...] = same_ref[which]
        return
    pair, core = index_ref[0], index_ref[1]
    for step in range(n_pair):
        source = lax.rem(pair - step + n_pair, n_pair)
        for parts_ref, of_core in ((same_ref, core), (other_ref, 1 - core)):
            shard = source * 2 + of_core
            rows = pl.ds(pl.multiple_of(shard * depth, depth), depth)
            weight_ref[rows] = parts_ref[step, which * depth : (which + 1) * depth]


def convolved(rows, row, taps_ref, weight_ref):
    frames_each, _, width, depth = taps_ref.shape
    summed = None
    for row_tap in range(3):
        patches = taps_ref[:, row + row_tap : row + row_tap + rows]
        product = jnp.dot(
            patches.reshape(frames_each * rows * width, depth),
            weight_ref[row_tap * depth : (row_tap + 1) * depth],
            preferred_element_type=F32,
        )
        summed = product if summed is None else summed + product
    return summed


def first_body(
    n_pair,
    n_others,
    index_ref,
    blended_ref,
    from_above_ref,
    from_below_ref,
    own_ref,
    *refs,
):
    others, refs = refs[:n_others], refs[n_others:]
    (
        same_ref, other_ref, gain_ref, shift_ref, bias_ref,
        out_ref, down_ref, up_ref, stats_ref,
        taps_ref, weight_ref, scale_ref, offset_ref,
    ) = refs
    frames_each, rows, width, channels = blended_ref.shape
    edge = frames_each * width
    stats = [own_ref[...], from_above_ref[edge:]]
    if n_pair > 2:
        stats.append(from_below_ref[edge:])
    stats = stats + [ref[...] for ref in others]
    normed_taps(
        n_pair, index_ref, blended_ref, from_above_ref, from_below_ref, stats,
        gain_ref, shift_ref, taps_ref, scale_ref, offset_ref,
    )
    gather_weight(n_pair, 0, index_ref, same_ref, other_ref, weight_ref)
    summed = convolved(rows, 0, taps_ref, weight_ref) + bias_ref[...]
    out_ref[...] = summed.astype(BF16).reshape(frames_each, rows, width, channels)
    write_messages(out_ref, down_ref, up_ref, stats_ref)


def second_body(
    n_pair,
    n_others,
    index_ref,
    field_ref,
    from_above_ref,
    from_below_ref,
    own_ref,
    *refs,
):
    others, refs = refs[:n_others], refs[n_others:]
    (
        same_ref, other_ref, gain_ref, shift_ref, bias_ref, blended_ref,
        kept_ref, sent_ref,
        taps_ref, weight_ref, scale_ref, offset_ref, whole_ref,
    ) = refs
    frames_each, rows, width, channels = field_ref.shape
    edge = frames_each * width
    stats = [own_ref[...], from_above_ref[edge:]]
    if n_pair > 2:
        stats.append(from_below_ref[edge:])
    stats = stats + [ref[...] for ref in others]
    normed_taps(
        n_pair, index_ref, field_ref, from_above_ref, from_below_ref, stats,
        gain_ref, shift_ref, taps_ref, scale_ref, offset_ref,
    )
    gather_weight(n_pair, 1, index_ref, same_ref, other_ref, weight_ref)
    core, count = index_ref[1], index_ref[2]
    summed = convolved(rows, 0, taps_ref, weight_ref) + bias_ref[...]
    summed = summed.reshape(frames_each, rows, width, channels) + blended_ref[...].astype(F32)
    half = rows // 2
    for frame in range(frames_each):
        live = core * frames_each + frame < count
        whole_ref[frame] = jnp.where(live, summed[frame], 0.0).astype(BF16)
    kept_ref[...] = whole_ref[:, pl.ds(core * half, half)]
    sent_ref[...] = whole_ref[:, pl.ds((1 - core) * half, half)]


def per_device(
    video,
    frame_counts,
    temporal_weight,
    temporal_bias,
    first_gain,
    first_shift,
    first_weight,
    first_bias,
    second_gain,
    second_shift,
    second_weight,
    second_bias,
):
    frames, rows, columns, channels = video.shape
    n_frame, n_pair = lax.axis_size("frame"), lax.axis_size("pair")
    width = columns * n_frame
    capacity = min(2 * ((frames + n_frame - 1) // n_frame), frames - n_frame + 1)
    frames_each = up_to(capacity, 2) // 2
    slots = frames_each + 2
    all_rows = 2 * rows
    edge = frames_each * width
    span = up_to(2 * frames_each, 16)
    params = pltpu.CompilerParams(vmem_limit_bytes=48 * 1024 * 1024)

    def ring(step):
        return [(i, (i + step) % n_pair) for i in range(n_pair)]

    def line(step):
        return [(i, i + step) for i in range(n_pair) if 0 <= i + step < n_pair]

    def struct(shape, dtype=BF16):
        return jax.ShapeDtypeStruct(shape, dtype)

    def row_of(vector):
        return vector.reshape(1, channels)

    pair, core = lax.axis_index("pair"), lax.axis_index("core")
    owner = lax.axis_index("frame")
    my_count = lax.dynamic_index_in_dim(frame_counts, owner, keepdims=False)
    index = jnp.stack([pair, core, my_count]).astype(jnp.int32)

    picked = pl.pallas_call(
        functools.partial(pick_body, 2, frames_each),
        out_shape=struct((n_frame * 2, slots, rows * columns, channels)),
        in_specs=[SMEM, VMEM],
        out_specs=VMEM,
        compiler_params=params,
        name="pick",
    )(frame_counts, video.reshape(frames, rows * columns, channels))
    parts = lax.all_to_all(picked, ("frame", "core"), split_axis=0, concat_axis=0)

    if first_weight.shape[0] % 16 == 0 and n_pair > 2:
        own_weights = jnp.concatenate([first_weight, second_weight], axis=0)
        same = jnp.stack(
            [own_weights]
            + [lax.ppermute(own_weights, "pair", ring(step)) for step in range(1, n_pair)]
        )
        other = lax.ppermute(same, "core", [(0, 1), (1, 0)])
    else:
        both = (first_weight, second_weight)
        same = jnp.stack([lax.all_gather(w, ("pair", "core"), tiled=True) for w in both])
        other = jnp.zeros((16, channels), BF16)

    by_place = parts.reshape(n_frame, 2, slots, rows, columns, channels)

    def edge_row(array):
        return array.transpose(1, 0, 2, 3).reshape(slots, width, channels)

    above = lax.ppermute(edge_row(by_place[:, 1, :, rows - 1]), "pair", line(1))
    below = lax.ppermute(edge_row(by_place[:, 0, :, 0]), "pair", line(-1))

    total = pl.pallas_call(
        functools.partial(temporal_body, 2, rows),
        out_shape=struct((frames_each, all_rows, width, channels), F32),
        in_specs=[VMEM] * 3,
        out_specs=VMEM,
        scratch_shapes=[pltpu.VMEM((slots, all_rows, width, 3 * channels), BF16)],
        compiler_params=params,
        name="temporal",
    )(parts, temporal_weight, row_of(temporal_bias))

    field = struct((frames_each, all_rows, width, channels))
    message = struct((edge + 3 * span, channels))
    stats_struct = struct((3 * span, channels))

    blended, down, up, stats = pl.pallas_call(
        functools.partial(borders_body, n_pair),
        out_shape=(field, message, message, stats_struct),
        in_specs=[VMEM] * 4,
        out_specs=(VMEM,) * 4,
        scratch_shapes=[pltpu.VMEM((2, slots, width, 3 * channels), BF16)],
        compiler_params=params,
        name="borders",
    )(total, above, below, temporal_weight)

    def exchange(down, up, stats):
        from_above = lax.ppermute(down, "pair", ring(1))
        from_below = lax.ppermute(up, "pair", ring(-1))
        others = [lax.ppermute(stats, "pair", ring(step)) for step in range(2, n_pair - 1)]
        return from_above, from_below, others

    def scratch():
        return [
            pltpu.VMEM((frames_each, all_rows + 2, width, 3 * channels), BF16),
            pltpu.VMEM((9 * channels, channels), BF16),
            pltpu.VMEM((frames_each, 1, channels), F32),
            pltpu.VMEM((frames_each, 1, channels), F32),
        ]

    from_above, from_below, others = exchange(down, up, stats)
    first_out, down, up, stats = pl.pallas_call(
        functools.partial(first_body, n_pair, len(others)),
        out_shape=(field, message, message, stats_struct),
        in_specs=[SMEM] + [VMEM] * (9 + len(others)),
        out_specs=(VMEM,) * 4,
        scratch_shapes=scratch(),
        compiler_params=params,
        name="first",
    )(
        index, blended, from_above, from_below, stats, *others, same, other,
        row_of(first_gain), row_of(first_shift), row_of(first_bias),
    )

    from_above, from_below, others = exchange(down, up, stats)
    half = struct((frames_each, rows, width, channels))
    kept, sent = pl.pallas_call(
        functools.partial(second_body, n_pair, len(others)),
        out_shape=(half, half),
        in_specs=[SMEM] + [VMEM] * (10 + len(others)),
        out_specs=(VMEM,) * 2,
        scratch_shapes=scratch() + [pltpu.VMEM(field.shape, BF16)],
        compiler_params=params,
        name="second",
    )(
        index, first_out, from_above, from_below, stats, *others, same, other,
        row_of(second_gain), row_of(second_shift), row_of(second_bias), blended,
    )
    received = lax.ppermute(sent, "core", [(0, 1), (1, 0)])
    early = jnp.where(core == 0, kept, received)
    late = jnp.where(core == 0, received, kept)
    return jnp.concatenate([early, late], axis=0)[:capacity]


def solution(mesh):
    n_frame, n_height = mesh.devices.shape
    split = Mesh(mesh.devices.reshape(n_frame, n_height // 2, 2), ("frame", "pair", "core"))
    height = ("pair", "core")
    placed = (
        P(None, height, "frame", None),
        P(),
        P(),
        P(),
        P(),
        P(),
        P(height, None),
        P(),
        P(),
        P(),
        P(height, None),
        P(),
    )
    return jax.shard_map(
        per_device,
        mesh=split,
        in_specs=placed,
        out_specs=P("frame", height, None, None),
        check_vma=False,
    )
```

```python
import functools

import jax
import jax.numpy as jnp
from jax import lax
from jax.experimental import pallas as pl
from jax.experimental.pallas import tpu as pltpu
from jax.sharding import Mesh, PartitionSpec as P

GROUPS = 32
EPS = 1e-06
VMEM = pl.BlockSpec(memory_space=pltpu.VMEM)
SMEM = pl.BlockSpec(memory_space=pltpu.SMEM)
HBM = pl.BlockSpec(memory_space=pl.ANY)
F32, BF16 = jnp.float32, jnp.bfloat16


def up_to(number, multiple):
    return -(-number // multiple) * multiple


def slots_of(frames, n_frame):
    return min(2 * ((frames + n_frame - 1) // n_frame), frames - n_frame + 1)


def silu(values):
    half = 0.5 * values
    return half + half * jnp.tanh(half)


def with_column_taps(values):
    axis, width = values.ndim - 2, values.shape[-2]
    column = lax.broadcasted_iota(jnp.int32, values.shape, axis)
    before = jnp.where(column == 0, 0.0, pltpu.roll(values, 1, axis))
    after = jnp.where(column == width - 1, 0.0, pltpu.roll(values, width - 1, axis))
    return jnp.concatenate([before.astype(BF16), values.astype(BF16), after.astype(BF16)], axis=-1)


def frame_offset(counts_ref, owner):
    offset = jnp.int32(0)
    for index in range(counts_ref.shape[0]):
        offset = offset + jnp.where(index < owner, counts_ref[index], 0)
    return offset


def pick_body(halves, frames_each, counts_ref, video_ref, out_ref):
    frames = video_ref.shape[0]
    slots = out_ref.shape[1]
    for owner in range(counts_ref.shape[0]):
        offset = frame_offset(counts_ref, owner)
        for half in range(halves):
            for slot in range(slots):
                frame = offset + (half * frames_each + slot - 2)
                values = video_ref[jnp.clip(frame, 0, frames - 1)]
                out_ref[owner * halves + half, slot] = jnp.where(
                    frame >= 0, values, jnp.zeros_like(values)
                )


def temporal_body(halves, rows, part_ref, weight_ref, bias_ref, total_ref, taps_ref):
    peers, slots, cells, channels = part_ref.shape
    columns = cells // rows
    frames_each, all_rows, width = total_ref.shape[:3]

    def place(slot, _):
        for half in range(halves):
            for row in range(rows):
                values = jnp.concatenate(
                    [
                        part_ref[peer * halves + half, slot].astype(F32)[
                            row * columns : (row + 1) * columns
                        ]
                        for peer in range(peers // halves)
                    ],
                    axis=0,
                )
                at = half * rows + row
                taps_ref[slot, at] = with_column_taps(silu(values))

                @pl.when(slot >= 2)
                def _():
                    total_ref[slot - 2, at] = values + bias_ref[...]

        return 0

    lax.fori_loop(0, slots, place, 0)
    depth = 3 * channels
    for row_tap in range(3):
        low, high = max(0, 1 - row_tap), min(all_rows, all_rows + 1 - row_tap)
        for time_tap in range(3):
            patches = taps_ref[
                time_tap : time_tap + frames_each, low + row_tap - 1 : high + row_tap - 1
            ]
            start = (time_tap * 3 + row_tap) * depth
            product = jnp.dot(
                patches.reshape(frames_each * (high - low) * width, depth),
                weight_ref[start : start + depth],
                preferred_element_type=F32,
            )
            total_ref[:, low:high] += product.reshape(frames_each, high - low, width, channels)


def write_stats(field_ref, stats_ref):
    frames_each, rows, width, channels = field_ref.shape
    span = stats_ref.shape[0] // 3
    sums, squares = [], []
    for frame in range(frames_each):
        values = field_ref[frame].astype(F32).reshape(rows * width, channels)
        part_sum = jnp.sum(values, axis=0, keepdims=True)
        centered = values - part_sum * (1.0 / (rows * width))
        sums.append(part_sum)
        squares.append(jnp.sum(centered * centered, axis=0, keepdims=True))
    pad = [jnp.zeros((span - 2 * frames_each, channels), F32)] if span > 2 * frames_each else []
    rest = jnp.concatenate(sums + squares + pad, axis=0)
    for piece in range(3):
        rounded = rest.astype(BF16)
        stats_ref[piece * span : (piece + 1) * span] = rounded
        rest = rest - rounded.astype(F32)


def write_messages(field_ref, down_ref, up_ref, stats_ref):
    frames_each, rows, width, channels = field_ref.shape
    write_stats(field_ref, stats_ref)
    edge = frames_each * width
    down_ref[:edge] = field_ref[:, rows - 1].reshape(edge, channels)
    up_ref[:edge] = field_ref[:, 0].reshape(edge, channels)
    down_ref[edge:] = stats_ref[...]
    up_ref[edge:] = stats_ref[...]


def borders_body(
    n_pair,
    total_ref,
    above_ref,
    below_ref,
    weight_ref,
    blended_ref,
    down_ref,
    up_ref,
    stats_ref,
    taps_ref,
):
    frames_each, rows, width, channels = total_ref.shape
    slots = above_ref.shape[0]
    depth = 3 * channels

    def place(slot, _):
        taps_ref[0, slot] = with_column_taps(silu(above_ref[slot].astype(F32)))
        taps_ref[1, slot] = with_column_taps(silu(below_ref[slot].astype(F32)))
        return 0

    lax.fori_loop(0, slots, place, 0)
    for side, row, row_tap in ((0, 0, 0), (1, rows - 1, 2)):
        summed = total_ref[:, row].reshape(frames_each * width, channels)
        for time_tap in range(3):
            patches = taps_ref[side, time_tap : time_tap + frames_each]
            start = (time_tap * 3 + row_tap) * depth
            summed = summed + jnp.dot(
                patches.reshape(frames_each * width, depth),
                weight_ref[start : start + depth],
                preferred_element_type=F32,
            )
        blended_ref[:, row] = summed.reshape(frames_each, width, channels).astype(BF16)
    blended_ref[:, 1 : rows - 1] = total_ref[:, 1 : rows - 1].astype(BF16)
    write_messages(blended_ref, down_ref, up_ref, stats_ref)


def group_total(values, width_group):
    lane = lax.broadcasted_iota(jnp.int32, values.shape, 1)
    size, step = values.shape[1], 1
    while step < width_group:
        upper = (lane // step) % 2 == 1
        values = values + jnp.where(
            upper, pltpu.roll(values, step, 1), pltpu.roll(values, size - step, 1)
        )
        step *= 2
    return values


def scale_and_offset(frames_each, cells, stats, gain_ref, shift_ref):
    channels = stats[0].shape[1]
    width_group = channels // GROUPS
    span = stats[0].shape[0] // 3
    parts = []
    for packed in stats:
        pieces = [packed[i * span : (i + 1) * span].astype(F32) for i in range(3)]
        parts.append(pieces[0] + (pieces[1] + pieces[2]))
    sums = [part[:frames_each] for part in parts]
    squares = [part[frames_each : 2 * frames_each] for part in parts]
    sample = float(cells * len(parts) * width_group)
    mean = group_total(functools.reduce(jnp.add, sums), width_group) * (1.0 / sample)
    spread = functools.reduce(jnp.add, squares)
    for part_sum in sums:
        apart = part_sum * (1.0 / cells) - mean
        spread = spread + float(cells) * apart * apart
    variance = group_total(spread, width_group) * (1.0 / sample)
    scale = lax.rsqrt(variance + EPS) * gain_ref[...]
    return scale, shift_ref[...] - mean * scale


def normed_taps(
    n_pair, index_ref, field_ref, above_ref, below_ref, stats, gain_ref, shift_ref, taps_ref,
    scale_ref, offset_ref,
):
    frames_each, rows, width, channels = field_ref.shape
    scale, offset = scale_and_offset(frames_each, rows * width, stats, gain_ref, shift_ref)
    for frame in range(frames_each):
        scale_ref[frame] = scale[frame : frame + 1]
        offset_ref[frame] = offset[frame : frame + 1]
    pair = index_ref[0]
    top = jnp.where(pair > 0, 1.0, 0.0)
    bottom = jnp.where(pair < n_pair - 1, 1.0, 0.0)

    def place(frame, _):
        scale_row, offset_row = scale_ref[frame], offset_ref[frame]
        for row in range(rows):
            values = field_ref[frame, row].astype(F32) * scale_row + offset_row
            taps_ref[frame, row + 1] = with_column_taps(silu(values))
        edge = pl.ds(pl.multiple_of(frame * width, width), width)
        values = silu(above_ref[edge].astype(F32) * scale_row + offset_row) * top
        taps_ref[frame, 0] = with_column_taps(values)
        values = silu(below_ref[edge].astype(F32) * scale_row + offset_row) * bottom
        taps_ref[frame, rows + 1] = with_column_taps(values)
        return 0

    lax.fori_loop(0, frames_each, place, 0)


def gather_weight(n_pair, which, index_ref, same_ref, other_ref, weight_ref):
    depth = weight_ref.shape[0] // (2 * n_pair)
    if same_ref.shape[0] != n_pair:
        weight_ref[...] = same_ref[which]
        return
    pair, core = index_ref[0], index_ref[1]
    for step in range(n_pair):
        source = lax.rem(pair - step + n_pair, n_pair)
        for parts_ref, of_core in ((same_ref, core), (other_ref, 1 - core)):
            shard = source * 2 + of_core
            rows = pl.ds(pl.multiple_of(shard * depth, depth), depth)
            weight_ref[rows] = parts_ref[step, which * depth : (which + 1) * depth]


def convolved(rows, row, taps_ref, weight_ref):
    frames_each, _, width, depth = taps_ref.shape
    summed = None
    for row_tap in range(3):
        patches = taps_ref[:, row + row_tap : row + row_tap + rows]
        product = jnp.dot(
            patches.reshape(frames_each * rows * width, depth),
            weight_ref[row_tap * depth : (row_tap + 1) * depth],
            preferred_element_type=F32,
        )
        summed = product if summed is None else summed + product
    return summed


def first_body(
    n_pair,
    n_others,
    index_ref,
    blended_ref,
    from_above_ref,
    from_below_ref,
    own_ref,
    *refs,
):
    others, refs = refs[:n_others], refs[n_others:]
    (
        same_ref, other_ref, gain_ref, shift_ref, bias_ref,
        out_ref, down_ref, up_ref, stats_ref,
        taps_ref, weight_ref, scale_ref, offset_ref,
    ) = refs
    frames_each, rows, width, channels = blended_ref.shape
    edge = frames_each * width
    stats = [own_ref[...], from_above_ref[edge:]]
    if n_pair > 2:
        stats.append(from_below_ref[edge:])
    stats = stats + [ref[...] for ref in others]
    normed_taps(
        n_pair, index_ref, blended_ref, from_above_ref, from_below_ref, stats,
        gain_ref, shift_ref, taps_ref, scale_ref, offset_ref,
    )
    gather_weight(n_pair, 0, index_ref, same_ref, other_ref, weight_ref)
    summed = convolved(rows, 0, taps_ref, weight_ref) + bias_ref[...]
    out_ref[...] = summed.astype(BF16).reshape(frames_each, rows, width, channels)
    write_messages(out_ref, down_ref, up_ref, stats_ref)


def second_body(
    n_pair,
    n_others,
    index_ref,
    field_ref,
    from_above_ref,
    from_below_ref,
    own_ref,
    *refs,
):
    others, refs = refs[:n_others], refs[n_others:]
    (
        same_ref, other_ref, gain_ref, shift_ref, bias_ref, blended_ref,
        kept_ref, sent_ref,
        taps_ref, weight_ref, scale_ref, offset_ref, whole_ref,
    ) = refs
    frames_each, rows, width, channels = field_ref.shape
    edge = frames_each * width
    stats = [own_ref[...], from_above_ref[edge:]]
    if n_pair > 2:
        stats.append(from_below_ref[edge:])
    stats = stats + [ref[...] for ref in others]
    normed_taps(
        n_pair, index_ref, field_ref, from_above_ref, from_below_ref, stats,
        gain_ref, shift_ref, taps_ref, scale_ref, offset_ref,
    )
    gather_weight(n_pair, 1, index_ref, same_ref, other_ref, weight_ref)
    core, count = index_ref[1], index_ref[2]
    summed = convolved(rows, 0, taps_ref, weight_ref) + bias_ref[...]
    summed = summed.reshape(frames_each, rows, width, channels) + blended_ref[...].astype(F32)
    half = rows // 2
    for frame in range(frames_each):
        live = core * frames_each + frame < count
        whole_ref[frame] = jnp.where(live, summed[frame], 0.0).astype(BF16)
    kept_ref[...] = whole_ref[:, pl.ds(core * half, half)]
    sent_ref[...] = whole_ref[:, pl.ds((1 - core) * half, half)]


def pick_frames_body(counts_ref, video_ref, out_ref):
    frames = video_ref.shape[0]
    n_owner = counts_ref.shape[0]
    frames_sent = out_ref.shape[1]
    n_pair = out_ref.shape[0] // (2 * n_owner)
    each = frames_sent - 1
    for owner in range(n_owner):
        offset = frame_offset(counts_ref, owner)
        for pair in range(n_pair):
            for core in range(2):
                for place in range(frames_sent):
                    first = 2 * each * pair
                    slot = first + (2 * each - 1 - place if core else place - 2)
                    frame = offset + slot
                    values = video_ref[jnp.clip(frame, 0, frames - 1)]
                    if slot < 0:
                        values = jnp.where(frame >= 0, values, jnp.zeros_like(values))
                    out_ref[(owner * n_pair + pair) * 2 + core, place] = values


def group_scale(values, gain_ref, shift_ref):
    cells, channels = values.shape
    width_group = channels // GROUPS
    sample = 1.0 / (cells * width_group)
    mean = group_total(jnp.sum(values, axis=0, keepdims=True), width_group) * sample
    centered = values - mean
    squares = jnp.sum(centered * centered, axis=0, keepdims=True)
    variance = group_total(squares, width_group) * sample
    scale = lax.rsqrt(variance + EPS) * gain_ref[...]
    return scale, shift_ref[...] - mean * scale


def frames_body(
    counts_ref, part_ref, swapped_ref, temporal_ref, same_ref, other_ref,
    temporal_bias_ref, first_gain_ref, first_shift_ref, first_bias_ref,
    second_gain_ref, second_shift_ref, second_bias_ref,
    out_ref,
    raw_ref, taps_ref, normed_ref, total_ref, blended_ref, weights_ref, sems,
):
    n_height, each, rows, width, channels = out_ref.shape
    n_pair = n_height // 2
    n_frame = part_ref.shape[0] // n_height
    columns = width // n_frame
    all_rows = n_height * rows
    depth = 3 * channels
    cells = all_rows * width
    pair, core = lax.axis_index("pair"), lax.axis_index("core")
    span = same_ref.shape[2]
    copies = []
    for which in range(2):
        for step in range(n_pair):
            source = lax.rem(pair - step + n_pair, n_pair)
            for side, (parts_ref, of_core) in enumerate(((same_ref, core), (other_ref, 1 - core))):
                copies.append(
                    pltpu.make_async_copy(
                        parts_ref.at[step, which],
                        weights_ref.at[which, source * 2 + of_core],
                        sems.at[which, step, side],
                    )
                )
    for copy in copies:
        copy.start()

    border = jnp.zeros((width, depth), BF16)
    for place in range(each + 2):
        taps_ref[place, 0] = border
        taps_ref[place, all_rows + 1] = border
    for place in range(each):
        normed_ref[place, 0] = border
        normed_ref[place, all_rows + 1] = border

    def lay(place, load):
        for height in range(n_height):
            pieces = [load(peer * n_height + height).astype(F32) for peer in range(n_frame)]
            for row in range(rows):
                values = jnp.concatenate(
                    [piece[row * columns : (row + 1) * columns] for piece in pieces], axis=0
                )
                raw_ref[place, height * rows + row] = values.astype(BF16)
                taps_ref[place, height * rows + row + 1] = with_column_taps(silu(values))

    def lay_part(place, _):
        lay(place, lambda source: part_ref[source, place])
        return 0

    lax.fori_loop(0, each + 1, lay_part, 0)
    lay(each + 1, lambda source: swapped_ref[source])

    def convolve(source_ref, weight_of, start):
        summed = None
        for row_tap in range(3):
            patches = source_ref[start, row_tap : row_tap + all_rows]
            product = jnp.dot(
                patches.reshape(each * cells, depth),
                weight_of(row_tap),
                preferred_element_type=F32,
            )
            summed = product if summed is None else summed + product
        return summed.reshape(each, cells, channels)

    for time_tap in range(3):
        start = time_tap + core * (2 - 2 * time_tap)
        product = convolve(
            taps_ref,
            lambda row_tap: temporal_ref[
                (time_tap * 3 + row_tap) * depth : (time_tap * 3 + row_tap + 1) * depth
            ],
            pl.ds(start, each),
        )
        if time_tap == 0:
            total_ref[...] = product
        else:
            total_ref[...] += product

    def norm(place, values, gain_ref, shift_ref):
        scale, offset = group_scale(values, gain_ref, shift_ref)
        for row in range(all_rows):
            line = values[row * width : (row + 1) * width] * scale + offset
            normed_ref[place, row + 1] = with_column_taps(silu(line))

    def norm_first(place, _):
        raw = raw_ref[place + 2 - 2 * core].astype(F32).reshape(cells, channels)
        blended = (raw + total_ref[place] + temporal_bias_ref[...]).astype(BF16)
        blended_ref[place] = blended
        norm(place, blended.astype(F32), first_gain_ref, first_shift_ref)
        return 0

    lax.fori_loop(0, each, norm_first, 0)
    for copy in copies[: len(copies) // 2]:
        copy.wait()

    def weight_of(which):
        weight = weights_ref[which].reshape(2 * n_pair * span, channels)
        return lambda row_tap: weight[row_tap * depth : (row_tap + 1) * depth]

    total_ref[...] = convolve(normed_ref, weight_of(0), slice(None))

    def norm_second(place, _):
        values = (total_ref[place] + first_bias_ref[...]).astype(BF16).astype(F32)
        norm(place, values, second_gain_ref, second_shift_ref)
        return 0

    lax.fori_loop(0, each, norm_second, 0)
    for copy in copies[len(copies) // 2 :]:
        copy.wait()
    total_ref[...] = convolve(normed_ref, weight_of(1), slice(None))
    count = counts_ref[lax.axis_index("frame")]

    def finish(place, _):
        at = place + core * (each - 1 - 2 * place)
        live = pair * 2 * each + core * each + at < count
        decoded = blended_ref[place].astype(F32) + (total_ref[place] + second_bias_ref[...])
        decoded = jnp.where(live, decoded, 0.0).astype(BF16)
        decoded = decoded.reshape(n_height, rows, width, channels)
        for height in range(n_height):
            out_ref[height, at] = decoded[height]
        return 0

    lax.fori_loop(0, each, finish, 0)


def ring(size, step):
    return [(i, (i + step) % size) for i in range(size)]


def whole_frames(
    video, frame_counts, temporal_weight, temporal_bias, first_gain, first_shift, first_weight,
    first_bias, second_gain, second_shift, second_weight, second_bias,
):
    frames, rows, columns, channels = video.shape
    n_frame, n_pair = lax.axis_size("frame"), lax.axis_size("pair")
    n_height = 2 * n_pair
    width = columns * n_frame
    all_rows = rows * n_height
    capacity = slots_of(frames, n_frame)
    each = -(-capacity // n_height)
    params = pltpu.CompilerParams(vmem_limit_bytes=40 * 1024 * 1024)
    swap = [(0, 1), (1, 0)]

    picked = pl.pallas_call(
        pick_frames_body,
        out_shape=jax.ShapeDtypeStruct(
            (n_frame * n_height, each + 1, rows * columns, channels), BF16
        ),
        in_specs=[SMEM, VMEM],
        out_specs=VMEM,
        compiler_params=params,
        name="pick",
    )(frame_counts, video.reshape(frames, rows * columns, channels))
    parts = lax.all_to_all(picked, ("frame", "pair", "core"), split_axis=0, concat_axis=0)
    swapped = lax.ppermute(parts[:, each], "core", swap)

    own = jnp.stack([first_weight, second_weight])
    same = jnp.stack(
        [own] + [lax.ppermute(own, "pair", ring(n_pair, step)) for step in range(1, n_pair)]
    )
    other = lax.ppermute(same, "core", swap)

    def row_of(vector):
        return vector.reshape(1, channels)

    taps = (width, 3 * channels)
    decoded = pl.pallas_call(
        frames_body,
        out_shape=jax.ShapeDtypeStruct((n_height, each, rows, width, channels), BF16),
        in_specs=[SMEM] + [VMEM] * 3 + [HBM] * 2 + [VMEM] * 7,
        out_specs=VMEM,
        scratch_shapes=[
            pltpu.VMEM((each + 2, all_rows, width, channels), BF16),
            pltpu.VMEM((each + 2, all_rows + 2) + taps, BF16),
            pltpu.VMEM((each, all_rows + 2) + taps, BF16),
            pltpu.VMEM((each, all_rows * width, channels), F32),
            pltpu.VMEM((each, all_rows * width, channels), BF16),
            pltpu.VMEM((2, n_height) + first_weight.shape, BF16),
            pltpu.SemaphoreType.DMA((2, n_pair, 2)),
        ],
        compiler_params=params,
        name="frames",
    )(
        frame_counts, parts, swapped, temporal_weight, same, other,
        row_of(temporal_bias), row_of(first_gain), row_of(first_shift), row_of(first_bias),
        row_of(second_gain), row_of(second_shift), row_of(second_bias),
    )
    owned = lax.all_to_all(decoded, ("pair", "core"), split_axis=0, concat_axis=0)
    return owned.reshape((n_height * each,) + owned.shape[2:])[:capacity]


def split_rows(
    video,
    frame_counts,
    temporal_weight,
    temporal_bias,
    first_gain,
    first_shift,
    first_weight,
    first_bias,
    second_gain,
    second_shift,
    second_weight,
    second_bias,
):
    frames, rows, columns, channels = video.shape
    n_frame, n_pair = lax.axis_size("frame"), lax.axis_size("pair")
    width = columns * n_frame
    capacity = slots_of(frames, n_frame)
    frames_each = up_to(capacity, 2) // 2
    slots = frames_each + 2
    all_rows = 2 * rows
    edge = frames_each * width
    span = up_to(2 * frames_each, 16)
    params = pltpu.CompilerParams(vmem_limit_bytes=20 * 1024 * 1024)

    def ring(step):
        return [(i, (i + step) % n_pair) for i in range(n_pair)]

    def line(step):
        return [(i, i + step) for i in range(n_pair) if 0 <= i + step < n_pair]

    def struct(shape, dtype=BF16):
        return jax.ShapeDtypeStruct(shape, dtype)

    def row_of(vector):
        return vector.reshape(1, channels)

    pair, core = lax.axis_index("pair"), lax.axis_index("core")
    owner = lax.axis_index("frame")
    my_count = lax.dynamic_index_in_dim(frame_counts, owner, keepdims=False)
    index = jnp.stack([pair, core, my_count]).astype(jnp.int32)

    picked = pl.pallas_call(
        functools.partial(pick_body, 2, frames_each),
        out_shape=struct((n_frame * 2, slots, rows * columns, channels)),
        in_specs=[SMEM, VMEM],
        out_specs=VMEM,
        compiler_params=params,
        name="pick",
    )(frame_counts, video.reshape(frames, rows * columns, channels))
    parts = lax.all_to_all(picked, ("frame", "core"), split_axis=0, concat_axis=0)

    if first_weight.shape[0] % 16 == 0 and n_pair > 2:
        own_weights = jnp.concatenate([first_weight, second_weight], axis=0)
        same = jnp.stack(
            [own_weights]
            + [lax.ppermute(own_weights, "pair", ring(step)) for step in range(1, n_pair)]
        )
        other = lax.ppermute(same, "core", [(0, 1), (1, 0)])
    else:
        both = (first_weight, second_weight)
        same = jnp.stack([lax.all_gather(w, ("pair", "core"), tiled=True) for w in both])
        other = jnp.zeros((16, channels), BF16)

    by_place = parts.reshape(n_frame, 2, slots, rows, columns, channels)

    def edge_row(array):
        return array.transpose(1, 0, 2, 3).reshape(slots, width, channels)

    above = lax.ppermute(edge_row(by_place[:, 1, :, rows - 1]), "pair", line(1))
    below = lax.ppermute(edge_row(by_place[:, 0, :, 0]), "pair", line(-1))

    total = pl.pallas_call(
        functools.partial(temporal_body, 2, rows),
        out_shape=struct((frames_each, all_rows, width, channels), F32),
        in_specs=[VMEM] * 3,
        out_specs=VMEM,
        scratch_shapes=[pltpu.VMEM((slots, all_rows, width, 3 * channels), BF16)],
        compiler_params=params,
        name="temporal",
    )(parts, temporal_weight, row_of(temporal_bias))

    field = struct((frames_each, all_rows, width, channels))
    message = struct((edge + 3 * span, channels))
    stats_struct = struct((3 * span, channels))

    blended, down, up, stats = pl.pallas_call(
        functools.partial(borders_body, n_pair),
        out_shape=(field, message, message, stats_struct),
        in_specs=[VMEM] * 4,
        out_specs=(VMEM,) * 4,
        scratch_shapes=[pltpu.VMEM((2, slots, width, 3 * channels), BF16)],
        compiler_params=params,
        name="borders",
    )(total, above, below, temporal_weight)

    def exchange(down, up, stats):
        from_above = lax.ppermute(down, "pair", ring(1))
        from_below = lax.ppermute(up, "pair", ring(-1))
        others = [lax.ppermute(stats, "pair", ring(step)) for step in range(2, n_pair - 1)]
        return from_above, from_below, others

    def scratch():
        return [
            pltpu.VMEM((frames_each, all_rows + 2, width, 3 * channels), BF16),
            pltpu.VMEM((9 * channels, channels), BF16),
            pltpu.VMEM((frames_each, 1, channels), F32),
            pltpu.VMEM((frames_each, 1, channels), F32),
        ]

    from_above, from_below, others = exchange(down, up, stats)
    first_out, down, up, stats = pl.pallas_call(
        functools.partial(first_body, n_pair, len(others)),
        out_shape=(field, message, message, stats_struct),
        in_specs=[SMEM] + [VMEM] * (9 + len(others)),
        out_specs=(VMEM,) * 4,
        scratch_shapes=scratch(),
        compiler_params=params,
        name="first",
    )(
        index, blended, from_above, from_below, stats, *others, same, other,
        row_of(first_gain), row_of(first_shift), row_of(first_bias),
    )

    from_above, from_below, others = exchange(down, up, stats)
    half = struct((frames_each, rows, width, channels))
    kept, sent = pl.pallas_call(
        functools.partial(second_body, n_pair, len(others)),
        out_shape=(half, half),
        in_specs=[SMEM] + [VMEM] * (10 + len(others)),
        out_specs=(VMEM,) * 2,
        scratch_shapes=scratch() + [pltpu.VMEM(field.shape, BF16)],
        compiler_params=params,
        name="second",
    )(
        index, first_out, from_above, from_below, stats, *others, same, other,
        row_of(second_gain), row_of(second_shift), row_of(second_bias), blended,
    )
    received = lax.ppermute(sent, "core", [(0, 1), (1, 0)])
    early = jnp.where(core == 0, kept, received)
    late = jnp.where(core == 0, received, kept)
    return jnp.concatenate([early, late], axis=0)[:capacity]


def per_device(video, *rest):
    n_height = lax.axis_size("pair") * lax.axis_size("core")
    if slots_of(video.shape[0], lax.axis_size("frame")) >= n_height:
        return whole_frames(video, *rest)
    return split_rows(video, *rest)


def solution(mesh):
    n_frame, n_height = mesh.devices.shape
    split = Mesh(mesh.devices.reshape(n_frame, n_height // 2, 2), ("frame", "pair", "core"))
    height = ("pair", "core")
    placed = (
        P(None, height, "frame", None),
        P(),
        P(),
        P(),
        P(),
        P(),
        P(height, None),
        P(),
        P(),
        P(),
        P(height, None),
        P(),
    )
    return jax.shard_map(
        per_device,
        mesh=split,
        in_specs=placed,
        out_specs=P("frame", height, None, None),
        check_vma=False,
    )
```

```python
import functools

import jax
import jax.numpy as jnp
from jax import lax
from jax.experimental import pallas as pl
from jax.experimental.pallas import tpu as pltpu
from jax.sharding import Mesh, PartitionSpec as P

GROUPS = 32
EPS = 1e-06
VMEM = pl.BlockSpec(memory_space=pltpu.VMEM)
SMEM = pl.BlockSpec(memory_space=pltpu.SMEM)
HBM = pl.BlockSpec(memory_space=pl.ANY)
F32, BF16 = jnp.float32, jnp.bfloat16


def up_to(number, multiple):
    return -(-number // multiple) * multiple


def slots_of(frames, n_frame):
    return min(2 * ((frames + n_frame - 1) // n_frame), frames - n_frame + 1)


def silu(values):
    half = 0.5 * values
    return half + half * jnp.tanh(half)


def with_column_taps(values):
    axis, width = values.ndim - 2, values.shape[-2]
    column = lax.broadcasted_iota(jnp.int32, values.shape, axis)
    before = jnp.where(column == 0, 0.0, pltpu.roll(values, 1, axis))
    after = jnp.where(column == width - 1, 0.0, pltpu.roll(values, width - 1, axis))
    return jnp.concatenate([before.astype(BF16), values.astype(BF16), after.astype(BF16)], axis=-1)


def frame_offset(counts_ref, owner):
    offset = jnp.int32(0)
    for index in range(counts_ref.shape[0]):
        offset = offset + jnp.where(index < owner, counts_ref[index], 0)
    return offset


def pick_body(halves, frames_each, counts_ref, video_ref, out_ref):
    frames = video_ref.shape[0]
    slots = out_ref.shape[1]
    for owner in range(counts_ref.shape[0]):
        offset = frame_offset(counts_ref, owner)
        for half in range(halves):
            for slot in range(slots):
                frame = offset + (half * frames_each + slot - 2)
                values = video_ref[jnp.clip(frame, 0, frames - 1)]
                out_ref[owner * halves + half, slot] = jnp.where(
                    frame >= 0, values, jnp.zeros_like(values)
                )


def temporal_body(halves, rows, part_ref, weight_ref, bias_ref, total_ref, taps_ref):
    peers, slots, cells, channels = part_ref.shape
    columns = cells // rows
    frames_each, all_rows, width = total_ref.shape[:3]

    def place(slot, _):
        for half in range(halves):
            for row in range(rows):
                values = jnp.concatenate(
                    [
                        part_ref[peer * halves + half, slot].astype(F32)[
                            row * columns : (row + 1) * columns
                        ]
                        for peer in range(peers // halves)
                    ],
                    axis=0,
                )
                at = half * rows + row
                taps_ref[slot, at] = with_column_taps(silu(values))

                @pl.when(slot >= 2)
                def _():
                    total_ref[slot - 2, at] = values + bias_ref[...]

        return 0

    lax.fori_loop(0, slots, place, 0)
    depth = 3 * channels
    for row_tap in range(3):
        low, high = max(0, 1 - row_tap), min(all_rows, all_rows + 1 - row_tap)
        for time_tap in range(3):
            patches = taps_ref[
                time_tap : time_tap + frames_each, low + row_tap - 1 : high + row_tap - 1
            ]
            start = (time_tap * 3 + row_tap) * depth
            product = jnp.dot(
                patches.reshape(frames_each * (high - low) * width, depth),
                weight_ref[start : start + depth],
                preferred_element_type=F32,
            )
            total_ref[:, low:high] += product.reshape(frames_each, high - low, width, channels)


def write_stats(field_ref, stats_ref):
    frames_each, rows, width, channels = field_ref.shape
    span = stats_ref.shape[0] // 3
    sums, squares = [], []
    for frame in range(frames_each):
        values = field_ref[frame].astype(F32).reshape(rows * width, channels)
        part_sum = jnp.sum(values, axis=0, keepdims=True)
        centered = values - part_sum * (1.0 / (rows * width))
        sums.append(part_sum)
        squares.append(jnp.sum(centered * centered, axis=0, keepdims=True))
    pad = [jnp.zeros((span - 2 * frames_each, channels), F32)] if span > 2 * frames_each else []
    rest = jnp.concatenate(sums + squares + pad, axis=0)
    for piece in range(3):
        rounded = rest.astype(BF16)
        stats_ref[piece * span : (piece + 1) * span] = rounded
        rest = rest - rounded.astype(F32)


def write_messages(field_ref, down_ref, up_ref, stats_ref):
    frames_each, rows, width, channels = field_ref.shape
    write_stats(field_ref, stats_ref)
    edge = frames_each * width
    down_ref[:edge] = field_ref[:, rows - 1].reshape(edge, channels)
    up_ref[:edge] = field_ref[:, 0].reshape(edge, channels)
    down_ref[edge:] = stats_ref[...]
    up_ref[edge:] = stats_ref[...]


def borders_body(
    n_pair,
    total_ref,
    above_ref,
    below_ref,
    weight_ref,
    blended_ref,
    down_ref,
    up_ref,
    stats_ref,
    taps_ref,
):
    frames_each, rows, width, channels = total_ref.shape
    slots = above_ref.shape[0]
    depth = 3 * channels

    def place(slot, _):
        taps_ref[0, slot] = with_column_taps(silu(above_ref[slot].astype(F32)))
        taps_ref[1, slot] = with_column_taps(silu(below_ref[slot].astype(F32)))
        return 0

    lax.fori_loop(0, slots, place, 0)
    for side, row, row_tap in ((0, 0, 0), (1, rows - 1, 2)):
        summed = total_ref[:, row].reshape(frames_each * width, channels)
        for time_tap in range(3):
            patches = taps_ref[side, time_tap : time_tap + frames_each]
            start = (time_tap * 3 + row_tap) * depth
            summed = summed + jnp.dot(
                patches.reshape(frames_each * width, depth),
                weight_ref[start : start + depth],
                preferred_element_type=F32,
            )
        blended_ref[:, row] = summed.reshape(frames_each, width, channels).astype(BF16)
    blended_ref[:, 1 : rows - 1] = total_ref[:, 1 : rows - 1].astype(BF16)
    write_messages(blended_ref, down_ref, up_ref, stats_ref)


def group_total(values, width_group):
    lane = lax.broadcasted_iota(jnp.int32, values.shape, 1)
    size, step = values.shape[1], 1
    while step < width_group:
        upper = (lane // step) % 2 == 1
        values = values + jnp.where(
            upper, pltpu.roll(values, step, 1), pltpu.roll(values, size - step, 1)
        )
        step *= 2
    return values


def scale_and_offset(frames_each, cells, stats, gain_ref, shift_ref):
    channels = stats[0].shape[1]
    width_group = channels // GROUPS
    span = stats[0].shape[0] // 3
    parts = []
    for packed in stats:
        pieces = [packed[i * span : (i + 1) * span].astype(F32) for i in range(3)]
        parts.append(pieces[0] + (pieces[1] + pieces[2]))
    sums = [part[:frames_each] for part in parts]
    squares = [part[frames_each : 2 * frames_each] for part in parts]
    sample = float(cells * len(parts) * width_group)
    mean = group_total(functools.reduce(jnp.add, sums), width_group) * (1.0 / sample)
    spread = functools.reduce(jnp.add, squares)
    for part_sum in sums:
        apart = part_sum * (1.0 / cells) - mean
        spread = spread + float(cells) * apart * apart
    variance = group_total(spread, width_group) * (1.0 / sample)
    scale = lax.rsqrt(variance + EPS) * gain_ref[...]
    return scale, shift_ref[...] - mean * scale


def normed_taps(
    n_pair, index_ref, field_ref, above_ref, below_ref, stats, gain_ref, shift_ref, taps_ref,
    scale_ref, offset_ref,
):
    frames_each, rows, width, channels = field_ref.shape
    scale, offset = scale_and_offset(frames_each, rows * width, stats, gain_ref, shift_ref)
    for frame in range(frames_each):
        scale_ref[frame] = scale[frame : frame + 1]
        offset_ref[frame] = offset[frame : frame + 1]
    pair = index_ref[0]
    top = jnp.where(pair > 0, 1.0, 0.0)
    bottom = jnp.where(pair < n_pair - 1, 1.0, 0.0)

    def place(frame, _):
        scale_row, offset_row = scale_ref[frame], offset_ref[frame]
        for row in range(rows):
            values = field_ref[frame, row].astype(F32) * scale_row + offset_row
            taps_ref[frame, row + 1] = with_column_taps(silu(values))
        edge = pl.ds(pl.multiple_of(frame * width, width), width)
        values = silu(above_ref[edge].astype(F32) * scale_row + offset_row) * top
        taps_ref[frame, 0] = with_column_taps(values)
        values = silu(below_ref[edge].astype(F32) * scale_row + offset_row) * bottom
        taps_ref[frame, rows + 1] = with_column_taps(values)
        return 0

    lax.fori_loop(0, frames_each, place, 0)


def gather_weight(n_pair, which, index_ref, same_ref, other_ref, weight_ref):
    depth = weight_ref.shape[0] // (2 * n_pair)
    if same_ref.shape[0] != n_pair:
        weight_ref[...] = same_ref[which]
        return
    pair, core = index_ref[0], index_ref[1]
    for step in range(n_pair):
        source = lax.rem(pair - step + n_pair, n_pair)
        for parts_ref, of_core in ((same_ref, core), (other_ref, 1 - core)):
            shard = source * 2 + of_core
            rows = pl.ds(pl.multiple_of(shard * depth, depth), depth)
            weight_ref[rows] = parts_ref[step, which * depth : (which + 1) * depth]


def convolved(rows, row, taps_ref, weight_ref):
    frames_each, _, width, depth = taps_ref.shape
    summed = None
    for row_tap in range(3):
        patches = taps_ref[:, row + row_tap : row + row_tap + rows]
        product = jnp.dot(
            patches.reshape(frames_each * rows * width, depth),
            weight_ref[row_tap * depth : (row_tap + 1) * depth],
            preferred_element_type=F32,
        )
        summed = product if summed is None else summed + product
    return summed


def first_body(
    n_pair,
    n_others,
    index_ref,
    blended_ref,
    from_above_ref,
    from_below_ref,
    own_ref,
    *refs,
):
    others, refs = refs[:n_others], refs[n_others:]
    (
        same_ref, other_ref, gain_ref, shift_ref, bias_ref,
        out_ref, down_ref, up_ref, stats_ref,
        taps_ref, weight_ref, scale_ref, offset_ref,
    ) = refs
    frames_each, rows, width, channels = blended_ref.shape
    edge = frames_each * width
    stats = [own_ref[...], from_above_ref[edge:]]
    if n_pair > 2:
        stats.append(from_below_ref[edge:])
    stats = stats + [ref[...] for ref in others]
    normed_taps(
        n_pair, index_ref, blended_ref, from_above_ref, from_below_ref, stats,
        gain_ref, shift_ref, taps_ref, scale_ref, offset_ref,
    )
    gather_weight(n_pair, 0, index_ref, same_ref, other_ref, weight_ref)
    summed = convolved(rows, 0, taps_ref, weight_ref) + bias_ref[...]
    out_ref[...] = summed.astype(BF16).reshape(frames_each, rows, width, channels)
    write_messages(out_ref, down_ref, up_ref, stats_ref)


def second_body(
    n_pair,
    n_others,
    index_ref,
    field_ref,
    from_above_ref,
    from_below_ref,
    own_ref,
    *refs,
):
    others, refs = refs[:n_others], refs[n_others:]
    (
        same_ref, other_ref, gain_ref, shift_ref, bias_ref, blended_ref,
        kept_ref, sent_ref,
        taps_ref, weight_ref, scale_ref, offset_ref, whole_ref,
    ) = refs
    frames_each, rows, width, channels = field_ref.shape
    edge = frames_each * width
    stats = [own_ref[...], from_above_ref[edge:]]
    if n_pair > 2:
        stats.append(from_below_ref[edge:])
    stats = stats + [ref[...] for ref in others]
    normed_taps(
        n_pair, index_ref, field_ref, from_above_ref, from_below_ref, stats,
        gain_ref, shift_ref, taps_ref, scale_ref, offset_ref,
    )
    gather_weight(n_pair, 1, index_ref, same_ref, other_ref, weight_ref)
    core, count = index_ref[1], index_ref[2]
    summed = convolved(rows, 0, taps_ref, weight_ref) + bias_ref[...]
    summed = summed.reshape(frames_each, rows, width, channels) + blended_ref[...].astype(F32)
    half = rows // 2
    for frame in range(frames_each):
        live = core * frames_each + frame < count
        whole_ref[frame] = jnp.where(live, summed[frame], 0.0).astype(BF16)
    kept_ref[...] = whole_ref[:, pl.ds(core * half, half)]
    sent_ref[...] = whole_ref[:, pl.ds((1 - core) * half, half)]


def pick_frames_body(counts_ref, video_ref, out_ref):
    frames = video_ref.shape[0]
    n_owner = counts_ref.shape[0]
    frames_sent = out_ref.shape[1]
    n_pair = out_ref.shape[0] // (2 * n_owner)
    each = frames_sent - 1
    for owner in range(n_owner):
        offset = frame_offset(counts_ref, owner)
        for pair in range(n_pair):
            for core in range(2):
                for place in range(frames_sent):
                    first = 2 * each * pair
                    slot = first + (2 * each - 1 - place if core else place - 2)
                    frame = offset + slot
                    values = video_ref[jnp.clip(frame, 0, frames - 1)]
                    if slot < 0:
                        values = jnp.where(frame >= 0, values, jnp.zeros_like(values))
                    out_ref[(owner * n_pair + pair) * 2 + core, place] = values


def group_spread(values, width_group):
    lane = lax.broadcasted_iota(jnp.int32, values.shape, 1) % width_group
    size, total = values.shape[1], values
    for step in range(1, width_group):
        total = total + jnp.where(
            lane >= step,
            pltpu.roll(values, step, 1),
            pltpu.roll(values, size - width_group + step, 1),
        )
    return total


def frames_body(
    counts_ref, part_ref, swapped_ref, temporal_ref, same_ref, other_ref,
    temporal_bias_ref, first_gain_ref, first_shift_ref, first_bias_ref,
    second_gain_ref, second_shift_ref, second_bias_ref,
    out_ref,
    *refs,
):
    n_height, each, rows, width, channels = out_ref.shape
    places = each + 2
    taps_refs, refs = refs[:places], refs[places:]
    normed_refs, refs = refs[:each], refs[each:]
    total_refs, refs = refs[:each], refs[each:]
    blended_refs, refs = refs[:each], refs[each:]
    field_refs, refs = refs[:each], refs[each:]
    landed_ref, raw_ref, time_ref, weights_ref, land_sems, time_sems, sems = refs
    n_pair = n_height // 2
    n_frame = part_ref.shape[0] // n_height
    columns = width // n_frame
    all_rows = n_height * rows
    depth = 3 * channels
    cells = all_rows * width
    width_group = channels // GROUPS
    pair, core = lax.axis_index("pair"), lax.axis_index("core")
    span = same_ref.shape[2]

    landings = [
        pltpu.make_async_copy(
            part_ref.at[:, place] if place <= each else swapped_ref,
            landed_ref.at[place],
            land_sems.at[place],
        )
        for place in range(places)
    ]
    time_copies = [
        pltpu.make_async_copy(
            temporal_ref.at[pl.ds(tap * 3 * depth, 3 * depth)],
            time_ref.at[tap],
            time_sems.at[tap],
        )
        for tap in range(3)
    ]
    copies = []
    for which in range(2):
        of_weight = []
        for step in range(n_pair):
            source = lax.rem(pair - step + n_pair, n_pair)
            for side, (parts_ref, of_core) in enumerate(((same_ref, core), (other_ref, 1 - core))):
                start = pl.multiple_of((source * 2 + of_core) * span, span)
                of_weight.append(
                    pltpu.make_async_copy(
                        parts_ref.at[step, which],
                        weights_ref.at[which, pl.ds(start, span)],
                        sems.at[which, step, side],
                    )
                )
        copies.append(of_weight)
    for copy in landings[:3] + time_copies + landings[3:] + copies[0] + copies[1]:
        copy.start()

    border = jnp.zeros((width, depth), BF16)
    for ref in taps_refs + normed_refs:
        ref[0] = border
        ref[all_rows + 1] = border

    def lay(place):
        landings[place].wait()
        for height in range(n_height):
            pieces = [
                landed_ref[place, peer * n_height + height].astype(F32) for peer in range(n_frame)
            ]
            for row in range(rows):
                values = jnp.concatenate(
                    [piece[row * columns : (row + 1) * columns] for piece in pieces], axis=0
                )
                raw_ref[place, height * rows + row] = values.astype(BF16)
                taps_refs[place][height * rows + row + 1] = with_column_taps(silu(values))

    def convolved(source_ref, weight_ref):
        summed = None
        for row_tap in range(3):
            product = jnp.dot(
                source_ref[row_tap : row_tap + all_rows].reshape(cells, depth),
                weight_ref[row_tap * depth : (row_tap + 1) * depth],
                preferred_element_type=F32,
            )
            summed = product if summed is None else summed + product
        return summed

    def temporal(place):
        for step in range(3):
            tap = step + core * (2 - 2 * step)
            product = convolved(taps_refs[place + step], time_ref.at[tap])
            if step == 0:
                total_refs[place][...] = product
            else:
                total_refs[place][...] += product

    def field_and_scale(field_ref, row_of, gain_ref, shift_ref):
        pivot = None
        sums = squares = jnp.zeros((8, channels), F32)
        for row in range(all_rows):
            rounded = row_of(row).astype(BF16)
            field_ref[row] = rounded
            values = rounded.astype(F32)
            if pivot is None:
                pivot = values[:1]
            apart = (values - pivot).reshape(width // 8, 8, channels)
            sums = sums + jnp.sum(apart, axis=0)
            squares = squares + jnp.sum(apart * apart, axis=0)
        sums = jnp.sum(sums, axis=0, keepdims=True)
        squares = jnp.sum(squares, axis=0, keepdims=True)
        own = sums * (1.0 / cells)
        sample = 1.0 / width_group
        mean = group_spread(own + pivot, width_group) * sample
        off = own + pivot - mean
        spread = squares * (1.0 / cells) - own * own + off * off
        variance = jnp.maximum(group_spread(spread, width_group) * sample, 0.0)
        scale = lax.rsqrt(variance + EPS) * gain_ref[...]
        return 0.5 * scale, 0.5 * (shift_ref[...] - mean * scale)

    def norm(place, field_ref, row_of, gain_ref, shift_ref):
        scale, offset = field_and_scale(field_ref, row_of, gain_ref, shift_ref)
        for row in range(all_rows):
            half = field_ref[row].astype(F32) * scale + offset
            normed_refs[place][row + 1] = with_column_taps(half + half * jnp.tanh(half))

    def first_norm(place):
        raw_at = place + 2 - 2 * core

        def row_of(row):
            product = total_refs[place][row * width : (row + 1) * width]
            return raw_ref[raw_at, row].astype(F32) + product + temporal_bias_ref[...]

        norm(place, blended_refs[place], row_of, first_gain_ref, first_shift_ref)

    count = counts_ref[lax.axis_index("frame")]

    def first_conv(place):
        total_refs[place][...] = convolved(normed_refs[place], weights_ref.at[0])

    def second_norm(place):
        def row_of(row):
            return total_refs[place][row * width : (row + 1) * width] + first_bias_ref[...]

        norm(place, field_refs[place], row_of, second_gain_ref, second_shift_ref)

    def second_conv(place):
        total_refs[place][...] = convolved(normed_refs[place], weights_ref.at[1])

    def finish(place):
        at = place + core * (each - 1 - 2 * place)
        live = pair * 2 * each + core * each + at < count
        for row in range(all_rows):
            product = total_refs[place][row * width : (row + 1) * width] + second_bias_ref[...]
            decoded = blended_refs[place][row].astype(F32) + product
            out_ref[row // rows, at, row % rows] = jnp.where(live, decoded, 0.0).astype(BF16)

    def ready(which):
        for copy in which:
            copy.wait()

    for place in range(3):
        lay(place)
    ready(time_copies)
    temporal(0)
    for place in range(3, places):
        lay(place)
    for place in range(1, each):
        temporal(place)
        first_norm(place - 1)
    ready(copies[0])
    ready(copies[1])
    first_norm(each - 1)
    for place in range(each):
        first_conv(place)
        if place > 0:
            second_norm(place - 1)
    second_norm(each - 1)
    for place in range(each):
        second_conv(place)
        if place > 0:
            finish(place - 1)
    finish(each - 1)


def ring(size, step):
    return [(i, (i + step) % size) for i in range(size)]


def whole_frames(
    video, frame_counts, temporal_weight, temporal_bias, first_gain, first_shift, first_weight,
    first_bias, second_gain, second_shift, second_weight, second_bias,
):
    frames, rows, columns, channels = video.shape
    n_frame, n_pair = lax.axis_size("frame"), lax.axis_size("pair")
    n_height = 2 * n_pair
    width = columns * n_frame
    all_rows = rows * n_height
    capacity = slots_of(frames, n_frame)
    each = -(-capacity // n_height)
    params = pltpu.CompilerParams(vmem_limit_bytes=40 * 1024 * 1024)
    swap = [(0, 1), (1, 0)]

    picked = pl.pallas_call(
        pick_frames_body,
        out_shape=jax.ShapeDtypeStruct(
            (n_frame * n_height, each + 1, rows * columns, channels), BF16
        ),
        in_specs=[SMEM, VMEM],
        out_specs=VMEM,
        compiler_params=params,
        name="pick",
    )(frame_counts, video.reshape(frames, rows * columns, channels))
    parts = lax.all_to_all(picked, ("frame", "pair", "core"), split_axis=0, concat_axis=0)
    swapped = lax.ppermute(parts[:, each], "core", swap)

    own = jnp.stack([first_weight, second_weight])
    same = jnp.stack(
        [own] + [lax.ppermute(own, "pair", ring(n_pair, step)) for step in range(1, n_pair)]
    )
    other = lax.ppermute(same, "core", swap)

    def row_of(vector):
        return vector.reshape(1, channels)

    taps = (width, 3 * channels)
    decoded = pl.pallas_call(
        frames_body,
        out_shape=jax.ShapeDtypeStruct((n_height, each, rows, width, channels), BF16),
        in_specs=[SMEM] + [HBM] * 5 + [VMEM] * 7,
        out_specs=VMEM,
        scratch_shapes=[pltpu.VMEM((all_rows + 2,) + taps, BF16)] * (2 * each + 2)
        + [pltpu.VMEM((all_rows * width, channels), F32)] * each
        + [pltpu.VMEM((all_rows, width, channels), BF16)] * (2 * each)
        + [
            pltpu.VMEM((each + 2, n_frame * n_height, rows * columns, channels), BF16),
            pltpu.VMEM((each + 2, all_rows, width, channels), BF16),
            pltpu.VMEM((3, 9 * channels, channels), BF16),
            pltpu.VMEM((2, 9 * channels, channels), BF16),
            pltpu.SemaphoreType.DMA((each + 2,)),
            pltpu.SemaphoreType.DMA((3,)),
            pltpu.SemaphoreType.DMA((2, n_pair, 2)),
        ],
        compiler_params=params,
        name="frames",
    )(
        frame_counts, parts, swapped, temporal_weight, same, other,
        row_of(temporal_bias), row_of(first_gain), row_of(first_shift), row_of(first_bias),
        row_of(second_gain), row_of(second_shift), row_of(second_bias),
    )
    owned = lax.all_to_all(decoded, ("pair", "core"), split_axis=0, concat_axis=0)
    return owned.reshape((n_height * each,) + owned.shape[2:])[:capacity]


def split_rows(
    video,
    frame_counts,
    temporal_weight,
    temporal_bias,
    first_gain,
    first_shift,
    first_weight,
    first_bias,
    second_gain,
    second_shift,
    second_weight,
    second_bias,
):
    frames, rows, columns, channels = video.shape
    n_frame, n_pair = lax.axis_size("frame"), lax.axis_size("pair")
    width = columns * n_frame
    capacity = slots_of(frames, n_frame)
    frames_each = up_to(capacity, 2) // 2
    slots = frames_each + 2
    all_rows = 2 * rows
    edge = frames_each * width
    span = up_to(2 * frames_each, 16)
    params = pltpu.CompilerParams(vmem_limit_bytes=20 * 1024 * 1024)

    def ring(step):
        return [(i, (i + step) % n_pair) for i in range(n_pair)]

    def line(step):
        return [(i, i + step) for i in range(n_pair) if 0 <= i + step < n_pair]

    def struct(shape, dtype=BF16):
        return jax.ShapeDtypeStruct(shape, dtype)

    def row_of(vector):
        return vector.reshape(1, channels)

    pair, core = lax.axis_index("pair"), lax.axis_index("core")
    owner = lax.axis_index("frame")
    my_count = lax.dynamic_index_in_dim(frame_counts, owner, keepdims=False)
    index = jnp.stack([pair, core, my_count]).astype(jnp.int32)

    picked = pl.pallas_call(
        functools.partial(pick_body, 2, frames_each),
        out_shape=struct((n_frame * 2, slots, rows * columns, channels)),
        in_specs=[SMEM, VMEM],
        out_specs=VMEM,
        compiler_params=params,
        name="pick",
    )(frame_counts, video.reshape(frames, rows * columns, channels))
    parts = lax.all_to_all(picked, ("frame", "core"), split_axis=0, concat_axis=0)

    if first_weight.shape[0] % 16 == 0 and n_pair > 2:
        own_weights = jnp.concatenate([first_weight, second_weight], axis=0)
        same = jnp.stack(
            [own_weights]
            + [lax.ppermute(own_weights, "pair", ring(step)) for step in range(1, n_pair)]
        )
        other = lax.ppermute(same, "core", [(0, 1), (1, 0)])
    else:
        both = (first_weight, second_weight)
        same = jnp.stack([lax.all_gather(w, ("pair", "core"), tiled=True) for w in both])
        other = jnp.zeros((16, channels), BF16)

    by_place = parts.reshape(n_frame, 2, slots, rows, columns, channels)

    def edge_row(array):
        return array.transpose(1, 0, 2, 3).reshape(slots, width, channels)

    above = lax.ppermute(edge_row(by_place[:, 1, :, rows - 1]), "pair", line(1))
    below = lax.ppermute(edge_row(by_place[:, 0, :, 0]), "pair", line(-1))

    total = pl.pallas_call(
        functools.partial(temporal_body, 2, rows),
        out_shape=struct((frames_each, all_rows, width, channels), F32),
        in_specs=[VMEM] * 3,
        out_specs=VMEM,
        scratch_shapes=[pltpu.VMEM((slots, all_rows, width, 3 * channels), BF16)],
        compiler_params=params,
        name="temporal",
    )(parts, temporal_weight, row_of(temporal_bias))

    field = struct((frames_each, all_rows, width, channels))
    message = struct((edge + 3 * span, channels))
    stats_struct = struct((3 * span, channels))

    blended, down, up, stats = pl.pallas_call(
        functools.partial(borders_body, n_pair),
        out_shape=(field, message, message, stats_struct),
        in_specs=[VMEM] * 4,
        out_specs=(VMEM,) * 4,
        scratch_shapes=[pltpu.VMEM((2, slots, width, 3 * channels), BF16)],
        compiler_params=params,
        name="borders",
    )(total, above, below, temporal_weight)

    def exchange(down, up, stats):
        from_above = lax.ppermute(down, "pair", ring(1))
        from_below = lax.ppermute(up, "pair", ring(-1))
        others = [lax.ppermute(stats, "pair", ring(step)) for step in range(2, n_pair - 1)]
        return from_above, from_below, others

    def scratch():
        return [
            pltpu.VMEM((frames_each, all_rows + 2, width, 3 * channels), BF16),
            pltpu.VMEM((9 * channels, channels), BF16),
            pltpu.VMEM((frames_each, 1, channels), F32),
            pltpu.VMEM((frames_each, 1, channels), F32),
        ]

    from_above, from_below, others = exchange(down, up, stats)
    first_out, down, up, stats = pl.pallas_call(
        functools.partial(first_body, n_pair, len(others)),
        out_shape=(field, message, message, stats_struct),
        in_specs=[SMEM] + [VMEM] * (9 + len(others)),
        out_specs=(VMEM,) * 4,
        scratch_shapes=scratch(),
        compiler_params=params,
        name="first",
    )(
        index, blended, from_above, from_below, stats, *others, same, other,
        row_of(first_gain), row_of(first_shift), row_of(first_bias),
    )

    from_above, from_below, others = exchange(down, up, stats)
    half = struct((frames_each, rows, width, channels))
    kept, sent = pl.pallas_call(
        functools.partial(second_body, n_pair, len(others)),
        out_shape=(half, half),
        in_specs=[SMEM] + [VMEM] * (10 + len(others)),
        out_specs=(VMEM,) * 2,
        scratch_shapes=scratch() + [pltpu.VMEM(field.shape, BF16)],
        compiler_params=params,
        name="second",
    )(
        index, first_out, from_above, from_below, stats, *others, same, other,
        row_of(second_gain), row_of(second_shift), row_of(second_bias), blended,
    )
    received = lax.ppermute(sent, "core", [(0, 1), (1, 0)])
    early = jnp.where(core == 0, kept, received)
    late = jnp.where(core == 0, received, kept)
    return jnp.concatenate([early, late], axis=0)[:capacity]


def per_device(video, *rest):
    n_height = lax.axis_size("pair") * lax.axis_size("core")
    if slots_of(video.shape[0], lax.axis_size("frame")) >= n_height:
        return whole_frames(video, *rest)
    return split_rows(video, *rest)


def solution(mesh):
    n_frame, n_height = mesh.devices.shape
    split = Mesh(mesh.devices.reshape(n_frame, n_height // 2, 2), ("frame", "pair", "core"))
    height = ("pair", "core")
    placed = (
        P(None, height, "frame", None),
        P(),
        P(),
        P(),
        P(),
        P(),
        P(height, None),
        P(),
        P(),
        P(),
        P(height, None),
        P(),
    )
    return jax.shard_map(
        per_device,
        mesh=split,
        in_specs=placed,
        out_specs=P("frame", height, None, None),
        check_vma=False,
    )
```

```python
import functools

import jax
import jax.numpy as jnp
from jax import lax
from jax.experimental import pallas as pl
from jax.experimental.pallas import tpu as pltpu
from jax.sharding import Mesh, PartitionSpec as P

GROUPS = 32
EPS = 1e-06
VMEM = pl.BlockSpec(memory_space=pltpu.VMEM)
SMEM = pl.BlockSpec(memory_space=pltpu.SMEM)
HBM = pl.BlockSpec(memory_space=pl.ANY)
F32, BF16 = jnp.float32, jnp.bfloat16


def up_to(number, multiple):
    return -(-number // multiple) * multiple


def slots_of(frames, n_frame):
    return min(2 * ((frames + n_frame - 1) // n_frame), frames - n_frame + 1)


def silu(values):
    half = 0.5 * values
    return half + half * jnp.tanh(half)


def with_column_taps(values):
    axis, width = values.ndim - 2, values.shape[-2]
    column = lax.broadcasted_iota(jnp.int32, values.shape, axis)
    before = jnp.where(column == 0, 0.0, pltpu.roll(values, 1, axis))
    after = jnp.where(column == width - 1, 0.0, pltpu.roll(values, width - 1, axis))
    return jnp.concatenate([before.astype(BF16), values.astype(BF16), after.astype(BF16)], axis=-1)


def frame_offset(counts_ref, owner):
    offset = jnp.int32(0)
    for index in range(counts_ref.shape[0]):
        offset = offset + jnp.where(index < owner, counts_ref[index], 0)
    return offset


def pick_body(halves, frames_each, counts_ref, video_ref, out_ref):
    frames = video_ref.shape[0]
    slots = out_ref.shape[1]
    for owner in range(counts_ref.shape[0]):
        offset = frame_offset(counts_ref, owner)
        for half in range(halves):
            for slot in range(slots):
                frame = offset + (half * frames_each + slot - 2)
                values = video_ref[jnp.clip(frame, 0, frames - 1)]
                out_ref[owner * halves + half, slot] = jnp.where(
                    frame >= 0, values, jnp.zeros_like(values)
                )


def temporal_body(halves, rows, part_ref, weight_ref, bias_ref, total_ref, taps_ref):
    peers, slots, cells, channels = part_ref.shape
    columns = cells // rows
    frames_each, all_rows, width = total_ref.shape[:3]

    def place(slot, _):
        for half in range(halves):
            for row in range(rows):
                values = jnp.concatenate(
                    [
                        part_ref[peer * halves + half, slot].astype(F32)[
                            row * columns : (row + 1) * columns
                        ]
                        for peer in range(peers // halves)
                    ],
                    axis=0,
                )
                at = half * rows + row
                taps_ref[slot, at] = with_column_taps(silu(values))

                @pl.when(slot >= 2)
                def _():
                    total_ref[slot - 2, at] = values + bias_ref[...]

        return 0

    lax.fori_loop(0, slots, place, 0)
    depth = 3 * channels
    for row_tap in range(3):
        low, high = max(0, 1 - row_tap), min(all_rows, all_rows + 1 - row_tap)
        for time_tap in range(3):
            patches = taps_ref[
                time_tap : time_tap + frames_each, low + row_tap - 1 : high + row_tap - 1
            ]
            start = (time_tap * 3 + row_tap) * depth
            product = jnp.dot(
                patches.reshape(frames_each * (high - low) * width, depth),
                weight_ref[start : start + depth],
                preferred_element_type=F32,
            )
            total_ref[:, low:high] += product.reshape(frames_each, high - low, width, channels)


def write_stats(field_ref, stats_ref):
    frames_each, rows, width, channels = field_ref.shape
    span = stats_ref.shape[0] // 3
    sums, squares = [], []
    for frame in range(frames_each):
        values = field_ref[frame].astype(F32).reshape(rows * width, channels)
        part_sum = jnp.sum(values, axis=0, keepdims=True)
        centered = values - part_sum * (1.0 / (rows * width))
        sums.append(part_sum)
        squares.append(jnp.sum(centered * centered, axis=0, keepdims=True))
    pad = [jnp.zeros((span - 2 * frames_each, channels), F32)] if span > 2 * frames_each else []
    rest = jnp.concatenate(sums + squares + pad, axis=0)
    for piece in range(3):
        rounded = rest.astype(BF16)
        stats_ref[piece * span : (piece + 1) * span] = rounded
        rest = rest - rounded.astype(F32)


def write_messages(field_ref, down_ref, up_ref, stats_ref):
    frames_each, rows, width, channels = field_ref.shape
    write_stats(field_ref, stats_ref)
    edge = frames_each * width
    down_ref[:edge] = field_ref[:, rows - 1].reshape(edge, channels)
    up_ref[:edge] = field_ref[:, 0].reshape(edge, channels)
    down_ref[edge:] = stats_ref[...]
    up_ref[edge:] = stats_ref[...]


def borders_body(
    n_pair,
    total_ref,
    above_ref,
    below_ref,
    weight_ref,
    blended_ref,
    down_ref,
    up_ref,
    stats_ref,
    taps_ref,
):
    frames_each, rows, width, channels = total_ref.shape
    slots = above_ref.shape[0]
    depth = 3 * channels

    def place(slot, _):
        taps_ref[0, slot] = with_column_taps(silu(above_ref[slot].astype(F32)))
        taps_ref[1, slot] = with_column_taps(silu(below_ref[slot].astype(F32)))
        return 0

    lax.fori_loop(0, slots, place, 0)
    for side, row, row_tap in ((0, 0, 0), (1, rows - 1, 2)):
        summed = total_ref[:, row].reshape(frames_each * width, channels)
        for time_tap in range(3):
            patches = taps_ref[side, time_tap : time_tap + frames_each]
            start = (time_tap * 3 + row_tap) * depth
            summed = summed + jnp.dot(
                patches.reshape(frames_each * width, depth),
                weight_ref[start : start + depth],
                preferred_element_type=F32,
            )
        blended_ref[:, row] = summed.reshape(frames_each, width, channels).astype(BF16)
    blended_ref[:, 1 : rows - 1] = total_ref[:, 1 : rows - 1].astype(BF16)
    write_messages(blended_ref, down_ref, up_ref, stats_ref)


def group_total(values, width_group):
    lane = lax.broadcasted_iota(jnp.int32, values.shape, 1)
    size, step = values.shape[1], 1
    while step < width_group:
        upper = (lane // step) % 2 == 1
        values = values + jnp.where(
            upper, pltpu.roll(values, step, 1), pltpu.roll(values, size - step, 1)
        )
        step *= 2
    return values


def scale_and_offset(frames_each, cells, stats, gain_ref, shift_ref):
    channels = stats[0].shape[1]
    width_group = channels // GROUPS
    span = stats[0].shape[0] // 3
    parts = []
    for packed in stats:
        pieces = [packed[i * span : (i + 1) * span].astype(F32) for i in range(3)]
        parts.append(pieces[0] + (pieces[1] + pieces[2]))
    sums = [part[:frames_each] for part in parts]
    squares = [part[frames_each : 2 * frames_each] for part in parts]
    sample = float(cells * len(parts) * width_group)
    mean = group_total(functools.reduce(jnp.add, sums), width_group) * (1.0 / sample)
    spread = functools.reduce(jnp.add, squares)
    for part_sum in sums:
        apart = part_sum * (1.0 / cells) - mean
        spread = spread + float(cells) * apart * apart
    variance = group_total(spread, width_group) * (1.0 / sample)
    scale = lax.rsqrt(variance + EPS) * gain_ref[...]
    return scale, shift_ref[...] - mean * scale


def normed_taps(
    n_pair, index_ref, field_ref, above_ref, below_ref, stats, gain_ref, shift_ref, taps_ref,
    scale_ref, offset_ref,
):
    frames_each, rows, width, channels = field_ref.shape
    scale, offset = scale_and_offset(frames_each, rows * width, stats, gain_ref, shift_ref)
    for frame in range(frames_each):
        scale_ref[frame] = scale[frame : frame + 1]
        offset_ref[frame] = offset[frame : frame + 1]
    pair = index_ref[0]
    top = jnp.where(pair > 0, 1.0, 0.0)
    bottom = jnp.where(pair < n_pair - 1, 1.0, 0.0)

    def place(frame, _):
        scale_row, offset_row = scale_ref[frame], offset_ref[frame]
        for row in range(rows):
            values = field_ref[frame, row].astype(F32) * scale_row + offset_row
            taps_ref[frame, row + 1] = with_column_taps(silu(values))
        edge = pl.ds(pl.multiple_of(frame * width, width), width)
        values = silu(above_ref[edge].astype(F32) * scale_row + offset_row) * top
        taps_ref[frame, 0] = with_column_taps(values)
        values = silu(below_ref[edge].astype(F32) * scale_row + offset_row) * bottom
        taps_ref[frame, rows + 1] = with_column_taps(values)
        return 0

    lax.fori_loop(0, frames_each, place, 0)


def gather_weight(n_pair, which, index_ref, same_ref, other_ref, weight_ref):
    depth = weight_ref.shape[0] // (2 * n_pair)
    if same_ref.shape[0] != n_pair:
        weight_ref[...] = same_ref[which]
        return
    pair, core = index_ref[0], index_ref[1]
    for step in range(n_pair):
        source = lax.rem(pair - step + n_pair, n_pair)
        for parts_ref, of_core in ((same_ref, core), (other_ref, 1 - core)):
            shard = source * 2 + of_core
            rows = pl.ds(pl.multiple_of(shard * depth, depth), depth)
            weight_ref[rows] = parts_ref[step, which * depth : (which + 1) * depth]


def convolved(rows, row, taps_ref, weight_ref):
    frames_each, _, width, depth = taps_ref.shape
    summed = None
    for row_tap in range(3):
        patches = taps_ref[:, row + row_tap : row + row_tap + rows]
        product = jnp.dot(
            patches.reshape(frames_each * rows * width, depth),
            weight_ref[row_tap * depth : (row_tap + 1) * depth],
            preferred_element_type=F32,
        )
        summed = product if summed is None else summed + product
    return summed


def first_body(
    n_pair,
    n_others,
    index_ref,
    blended_ref,
    from_above_ref,
    from_below_ref,
    own_ref,
    *refs,
):
    others, refs = refs[:n_others], refs[n_others:]
    (
        same_ref, other_ref, gain_ref, shift_ref, bias_ref,
        out_ref, down_ref, up_ref, stats_ref,
        taps_ref, weight_ref, scale_ref, offset_ref,
    ) = refs
    frames_each, rows, width, channels = blended_ref.shape
    edge = frames_each * width
    stats = [own_ref[...], from_above_ref[edge:]]
    if n_pair > 2:
        stats.append(from_below_ref[edge:])
    stats = stats + [ref[...] for ref in others]
    normed_taps(
        n_pair, index_ref, blended_ref, from_above_ref, from_below_ref, stats,
        gain_ref, shift_ref, taps_ref, scale_ref, offset_ref,
    )
    gather_weight(n_pair, 0, index_ref, same_ref, other_ref, weight_ref)
    summed = convolved(rows, 0, taps_ref, weight_ref) + bias_ref[...]
    out_ref[...] = summed.astype(BF16).reshape(frames_each, rows, width, channels)
    write_messages(out_ref, down_ref, up_ref, stats_ref)


def second_body(
    n_pair,
    n_others,
    index_ref,
    field_ref,
    from_above_ref,
    from_below_ref,
    own_ref,
    *refs,
):
    others, refs = refs[:n_others], refs[n_others:]
    (
        same_ref, other_ref, gain_ref, shift_ref, bias_ref, blended_ref,
        kept_ref, sent_ref,
        taps_ref, weight_ref, scale_ref, offset_ref, whole_ref,
    ) = refs
    frames_each, rows, width, channels = field_ref.shape
    edge = frames_each * width
    stats = [own_ref[...], from_above_ref[edge:]]
    if n_pair > 2:
        stats.append(from_below_ref[edge:])
    stats = stats + [ref[...] for ref in others]
    normed_taps(
        n_pair, index_ref, field_ref, from_above_ref, from_below_ref, stats,
        gain_ref, shift_ref, taps_ref, scale_ref, offset_ref,
    )
    gather_weight(n_pair, 1, index_ref, same_ref, other_ref, weight_ref)
    core, count = index_ref[1], index_ref[2]
    summed = convolved(rows, 0, taps_ref, weight_ref) + bias_ref[...]
    summed = summed.reshape(frames_each, rows, width, channels) + blended_ref[...].astype(F32)
    half = rows // 2
    for frame in range(frames_each):
        live = core * frames_each + frame < count
        whole_ref[frame] = jnp.where(live, summed[frame], 0.0).astype(BF16)
    kept_ref[...] = whole_ref[:, pl.ds(core * half, half)]
    sent_ref[...] = whole_ref[:, pl.ds((1 - core) * half, half)]


def pick_frames_body(counts_ref, video_ref, out_ref, held_ref, placed_ref, held_sem, sems):
    load = pltpu.make_async_copy(video_ref, held_ref, held_sem)
    load.start()
    frames, (parts, sent) = video_ref.shape[0], out_ref.shape[:2]
    n_owner = counts_ref.shape[0]
    span, each = parts // n_owner, sent - 1
    load.wait()
    copies = []
    for owner in range(n_owner):
        offset = frame_offset(counts_ref, owner)
        for part in range(span):
            pair, core = part // 2, part % 2
            for place in range(sent):
                slot = 2 * each * pair + (2 * each - 1 - place if core else place - 2)
                frame = offset + slot
                values = held_ref[jnp.clip(frame, 0, frames - 1)]
                if slot < 0:
                    values = jnp.where(frame >= 0, values, jnp.zeros_like(values))
                placed_ref[owner * span + part, place] = values
        rows = pl.ds(owner * span, span)
        copies.append(
            pltpu.make_async_copy(placed_ref.at[rows], out_ref.at[rows], sems.at[owner])
        )
        copies[-1].start()
    for copy in copies:
        copy.wait()


def group_spread(values, width_group):
    lane = lax.broadcasted_iota(jnp.int32, values.shape, 1) % width_group
    size, total = values.shape[1], values
    for step in range(1, width_group):
        total = total + jnp.where(
            lane >= step,
            pltpu.roll(values, step, 1),
            pltpu.roll(values, size - width_group + step, 1),
        )
    return total


def interleave(main, side, pace):
    for _ in main:
        for _ in range(pace):
            next(side, None)
    for _ in side:
        pass


def frames_body(
    counts_ref, part_ref, swapped_ref, temporal_ref, same_ref, other_ref, *refs
):
    vectors, (out_ref, *refs) = refs[:7], refs[7:]
    n_height, each, rows, width, channels = out_ref.shape
    places = each + 2
    taps_refs, refs = refs[:places], refs[places:]
    normed_refs, refs = refs[:each], refs[each:]
    total_refs, refs = refs[:each], refs[each:]
    blended_refs, refs = refs[:each], refs[each:]
    field_refs, refs = refs[:each], refs[each:]
    landed_refs, refs = refs[:places], refs[places:]
    raw_ref, time_ref, weights_ref, done_ref, vectors_ref, held_ref, *refs = refs
    land_sems, time_sems, sems, out_sems, vector_sems, held_sem = refs
    n_pair = n_height // 2
    n_frame = part_ref.shape[0] // n_height
    columns = width // n_frame
    all_rows = n_height * rows
    depth = 3 * channels
    cells = all_rows * width
    width_group = channels // GROUPS
    owner, pair, core = lax.axis_index("frame"), lax.axis_index("pair"), lax.axis_index("core")
    span = same_ref.shape[2]
    landings = [
        pltpu.make_async_copy(
            part_ref.at[:, place] if place <= each else swapped_ref,
            landed_refs[place],
            land_sems.at[place],
        )
        for place in range(places)
    ]
    time_copies = []
    for step in range(3):
        tap = step + core * (2 - 2 * step)
        begin = pl.multiple_of(tap * 3 * depth, 3 * depth)
        time_copies.append(
            pltpu.make_async_copy(
                temporal_ref.at[pl.ds(begin, 3 * depth)], time_ref.at[step], time_sems.at[step]
            )
        )
    vector_copies = [
        pltpu.make_async_copy(ref, vectors_ref.at[line], vector_sems.at[line])
        for line, ref in enumerate(vectors)
    ]
    vector_copies.append(pltpu.make_async_copy(counts_ref, held_ref, held_sem))
    copies = []
    for which in range(2):
        of_weight = []
        for step in range(n_pair):
            source = lax.rem(pair - step + n_pair, n_pair)
            for side, (parts_ref, of_core) in enumerate(((same_ref, core), (other_ref, 1 - core))):
                begin = pl.multiple_of((source * 2 + of_core) * span, span)
                of_weight.append(
                    pltpu.make_async_copy(
                        parts_ref.at[step, which],
                        weights_ref.at[which, pl.ds(begin, span)],
                        sems.at[which, step, side],
                    )
                )
        copies.append(of_weight)
    for copy in landings[:3] + time_copies + landings[3:] + vector_copies + copies[0] + copies[1]:
        copy.start()

    border = jnp.zeros((width, depth), BF16)
    for ref in taps_refs + normed_refs:
        ref[0] = border
        ref[all_rows + 1] = border

    def lay(place):
        landings[place].wait()
        for height in range(n_height):
            pieces = [
                landed_refs[place][peer * n_height + height].astype(F32)
                for peer in range(n_frame)
            ]
            for row in range(rows):
                values = jnp.concatenate(
                    [piece[row * columns : (row + 1) * columns] for piece in pieces], axis=0
                )
                raw_ref[place, height * rows + row] = values.astype(BF16)
                taps_refs[place][height * rows + row + 1] = with_column_taps(silu(values))
            yield

    parts_of_field = 2
    part_rows = all_rows // parts_of_field
    part_cells = part_rows * width

    def products(source_ref, weight_ref, part):
        summed = None
        for row_tap in range(3):
            low = part * part_rows + row_tap
            product = jnp.dot(
                source_ref[low : low + part_rows].reshape(part_cells, depth),
                weight_ref[row_tap * depth : (row_tap + 1) * depth],
                preferred_element_type=F32,
            )
            summed = product if summed is None else summed + product
            yield summed

    def temporal(place):
        for step in range(3):
            if place == 0:
                time_copies[step].wait()
            for part in range(parts_of_field):
                for summed in products(taps_refs[place + step], time_ref.at[step], part):
                    yield
                cut = slice(part * part_cells, (part + 1) * part_cells)
                if step == 0:
                    total_refs[place][cut] = summed
                else:
                    total_refs[place][cut] += summed

    def convolve(place, which):
        for part in range(parts_of_field):
            for summed in products(normed_refs[place], weights_ref.at[which], part):
                yield
            total_refs[place][part * part_cells : (part + 1) * part_cells] = summed

    def norm(place, field_ref, row_of, gain, shift):
        pivot = None
        sums = squares = jnp.zeros((8, channels), F32)
        for row in range(all_rows):
            rounded = row_of(row).astype(BF16)
            field_ref[row] = rounded
            values = rounded.astype(F32)
            if pivot is None:
                pivot = values[:1]
            apart = (values - pivot).reshape(width // 8, 8, channels)
            sums = sums + jnp.sum(apart, axis=0)
            squares = squares + jnp.sum(apart * apart, axis=0)
            if row % 4 == 3:
                yield
        own = jnp.sum(sums, axis=0, keepdims=True) * (1.0 / cells)
        squares = jnp.sum(squares, axis=0, keepdims=True) * (1.0 / cells)
        sample = 1.0 / width_group
        mean = group_spread(own + pivot, width_group) * sample
        off = own + pivot - mean
        spread = squares - own * own + off * off
        variance = jnp.maximum(group_spread(spread, width_group) * sample, 0.0)
        scale = lax.rsqrt(variance + EPS) * gain
        offset = 0.5 * (shift - mean * scale)
        scale = 0.5 * scale
        yield
        for row in range(all_rows):
            half = field_ref[row].astype(F32) * scale + offset
            normed_refs[place][row + 1] = with_column_taps(half + half * jnp.tanh(half))
            if row % 2 == 1:
                yield

    def first_norm(place):
        raw_at = place + 2 - 2 * core

        def row_of(row):
            product = total_refs[place][row * width : (row + 1) * width]
            return raw_ref[raw_at, row].astype(F32) + product + temporal_bias

        return norm(place, blended_refs[place], row_of, first_gain, first_shift)

    def second_norm(place):
        def row_of(row):
            return total_refs[place][row * width : (row + 1) * width] + first_bias

        return norm(place, field_refs[place], row_of, second_gain, second_shift)

    def finish(place):
        count = held_ref[owner]
        at = place + core * (each - 1 - 2 * place)
        live = pair * 2 * each + core * each + at < count
        for row in range(all_rows):
            product = total_refs[place][row * width : (row + 1) * width] + second_bias
            decoded = blended_refs[place][row].astype(F32) + product
            done_ref[place, row // rows, row % rows] = jnp.where(live, decoded, 0.0).astype(BF16)
            if row % 4 == 3:
                yield
        store = pltpu.make_async_copy(
            done_ref.at[place], out_ref.at[:, at], out_sems.at[place]
        )
        store.start()
        stores.append(store)

    stores = []

    def ready(which):
        for copy in which:
            copy.wait()

    def both(one, other):
        yield from one
        yield from other

    nothing = iter(())
    for place in range(3):
        interleave(lay(place), nothing, 0)
    laying = nothing
    for place in range(3, places):
        laying = both(laying, lay(place))
    interleave(temporal(0), laying, 1)
    ready(vector_copies)
    (
        temporal_bias, first_gain, first_shift, first_bias, second_gain, second_shift, second_bias
    ) = [vectors_ref[line] for line in range(7)]
    for place in range(1, each):
        interleave(temporal(place), first_norm(place - 1), 1)
    ready(copies[0])
    pending = first_norm(each - 1)
    for place in range(each):
        interleave(convolve(place, 0), pending, 3)
        pending = second_norm(place)
    ready(copies[1])
    for place in range(each):
        interleave(convolve(place, 1), pending, 3)
        pending = finish(place)
    interleave(pending, nothing, 0)
    ready(stores)


def ring(size, step):
    return [(i, (i + step) % size) for i in range(size)]


def whole_frames(
    video, frame_counts, temporal_weight, temporal_bias, first_gain, first_shift, first_weight,
    first_bias, second_gain, second_shift, second_weight, second_bias,
):
    frames, rows, columns, channels = video.shape
    n_frame, n_pair = lax.axis_size("frame"), lax.axis_size("pair")
    n_height = 2 * n_pair
    width = columns * n_frame
    all_rows = rows * n_height
    capacity = slots_of(frames, n_frame)
    each = -(-capacity // n_height)
    params = pltpu.CompilerParams(vmem_limit_bytes=60 * 1024 * 1024)
    swap = [(0, 1), (1, 0)]

    picked = pl.pallas_call(
        pick_frames_body,
        out_shape=jax.ShapeDtypeStruct(
            (n_frame * n_height, each + 1, rows * columns, channels), BF16
        ),
        in_specs=[SMEM, HBM],
        out_specs=HBM,
        scratch_shapes=[
            pltpu.VMEM((frames, rows * columns, channels), BF16),
            pltpu.VMEM((n_frame * n_height, each + 1, rows * columns, channels), BF16),
            pltpu.SemaphoreType.DMA(()),
            pltpu.SemaphoreType.DMA((n_frame,)),
        ],
        compiler_params=params,
        name="pick",
    )(frame_counts, video.reshape(frames, rows * columns, channels))
    parts = lax.all_to_all(picked, ("frame", "pair", "core"), split_axis=0, concat_axis=0)
    swapped = lax.ppermute(parts[:, each], "core", swap)

    own = jnp.stack([first_weight, second_weight])
    same = jnp.stack(
        [own] + [lax.ppermute(own, "pair", ring(n_pair, step)) for step in range(1, n_pair)]
    )
    other = lax.ppermute(same, "core", swap)

    vectors = (
        temporal_bias, first_gain, first_shift, first_bias, second_gain, second_shift, second_bias
    )
    field = (all_rows, width, channels)
    taps = (all_rows + 2, width, 3 * channels)
    decoded = pl.pallas_call(
        frames_body,
        out_shape=jax.ShapeDtypeStruct((n_height, each, rows, width, channels), BF16),
        in_specs=[HBM] * 13,
        out_specs=HBM,
        scratch_shapes=[pltpu.VMEM(taps, BF16)] * (2 * each + 2)
        + [pltpu.VMEM((all_rows * width, channels), F32)] * each
        + [pltpu.VMEM(field, BF16)] * (2 * each)
        + [pltpu.VMEM((n_frame * n_height, rows * columns, channels), BF16)] * (each + 2)
        + [
            pltpu.VMEM((each + 2,) + field, BF16),
            pltpu.VMEM((3, 9 * channels, channels), BF16),
            pltpu.VMEM((2, 9 * channels, channels), BF16),
            pltpu.VMEM((each, n_height, rows, width, channels), BF16),
            pltpu.VMEM((7, 1, channels), F32),
            pltpu.SMEM(frame_counts.shape, jnp.int32),
            pltpu.SemaphoreType.DMA((each + 2,)),
            pltpu.SemaphoreType.DMA((3,)),
            pltpu.SemaphoreType.DMA((2, n_pair, 2)),
            pltpu.SemaphoreType.DMA((each,)),
            pltpu.SemaphoreType.DMA((7,)),
            pltpu.SemaphoreType.DMA(()),
        ],
        compiler_params=params,
        name="frames",
    )(
        frame_counts, parts, swapped, temporal_weight, same, other,
        *[vector.reshape(1, channels) for vector in vectors],
    )
    owned = lax.all_to_all(decoded, ("pair", "core"), split_axis=0, concat_axis=0)
    return owned.reshape((n_height * each,) + owned.shape[2:])[:capacity]


def split_rows(
    video,
    frame_counts,
    temporal_weight,
    temporal_bias,
    first_gain,
    first_shift,
    first_weight,
    first_bias,
    second_gain,
    second_shift,
    second_weight,
    second_bias,
):
    frames, rows, columns, channels = video.shape
    n_frame, n_pair = lax.axis_size("frame"), lax.axis_size("pair")
    width = columns * n_frame
    capacity = slots_of(frames, n_frame)
    frames_each = up_to(capacity, 2) // 2
    slots = frames_each + 2
    all_rows = 2 * rows
    edge = frames_each * width
    span = up_to(2 * frames_each, 16)
    params = pltpu.CompilerParams(vmem_limit_bytes=20 * 1024 * 1024)

    def ring(step):
        return [(i, (i + step) % n_pair) for i in range(n_pair)]

    def line(step):
        return [(i, i + step) for i in range(n_pair) if 0 <= i + step < n_pair]

    def struct(shape, dtype=BF16):
        return jax.ShapeDtypeStruct(shape, dtype)

    def row_of(vector):
        return vector.reshape(1, channels)

    pair, core = lax.axis_index("pair"), lax.axis_index("core")
    owner = lax.axis_index("frame")
    my_count = lax.dynamic_index_in_dim(frame_counts, owner, keepdims=False)
    index = jnp.stack([pair, core, my_count]).astype(jnp.int32)

    picked = pl.pallas_call(
        functools.partial(pick_body, 2, frames_each),
        out_shape=struct((n_frame * 2, slots, rows * columns, channels)),
        in_specs=[SMEM, VMEM],
        out_specs=VMEM,
        compiler_params=params,
        name="pick",
    )(frame_counts, video.reshape(frames, rows * columns, channels))
    parts = lax.all_to_all(picked, ("frame", "core"), split_axis=0, concat_axis=0)

    if first_weight.shape[0] % 16 == 0 and n_pair > 2:
        own_weights = jnp.concatenate([first_weight, second_weight], axis=0)
        same = jnp.stack(
            [own_weights]
            + [lax.ppermute(own_weights, "pair", ring(step)) for step in range(1, n_pair)]
        )
        other = lax.ppermute(same, "core", [(0, 1), (1, 0)])
    else:
        both = (first_weight, second_weight)
        same = jnp.stack([lax.all_gather(w, ("pair", "core"), tiled=True) for w in both])
        other = jnp.zeros((16, channels), BF16)

    by_place = parts.reshape(n_frame, 2, slots, rows, columns, channels)

    def edge_row(array):
        return array.transpose(1, 0, 2, 3).reshape(slots, width, channels)

    above = lax.ppermute(edge_row(by_place[:, 1, :, rows - 1]), "pair", line(1))
    below = lax.ppermute(edge_row(by_place[:, 0, :, 0]), "pair", line(-1))

    total = pl.pallas_call(
        functools.partial(temporal_body, 2, rows),
        out_shape=struct((frames_each, all_rows, width, channels), F32),
        in_specs=[VMEM] * 3,
        out_specs=VMEM,
        scratch_shapes=[pltpu.VMEM((slots, all_rows, width, 3 * channels), BF16)],
        compiler_params=params,
        name="temporal",
    )(parts, temporal_weight, row_of(temporal_bias))

    field = struct((frames_each, all_rows, width, channels))
    message = struct((edge + 3 * span, channels))
    stats_struct = struct((3 * span, channels))

    blended, down, up, stats = pl.pallas_call(
        functools.partial(borders_body, n_pair),
        out_shape=(field, message, message, stats_struct),
        in_specs=[VMEM] * 4,
        out_specs=(VMEM,) * 4,
        scratch_shapes=[pltpu.VMEM((2, slots, width, 3 * channels), BF16)],
        compiler_params=params,
        name="borders",
    )(total, above, below, temporal_weight)

    def exchange(down, up, stats):
        from_above = lax.ppermute(down, "pair", ring(1))
        from_below = lax.ppermute(up, "pair", ring(-1))
        others = [lax.ppermute(stats, "pair", ring(step)) for step in range(2, n_pair - 1)]
        return from_above, from_below, others

    def scratch():
        return [
            pltpu.VMEM((frames_each, all_rows + 2, width, 3 * channels), BF16),
            pltpu.VMEM((9 * channels, channels), BF16),
            pltpu.VMEM((frames_each, 1, channels), F32),
            pltpu.VMEM((frames_each, 1, channels), F32),
        ]

    from_above, from_below, others = exchange(down, up, stats)
    first_out, down, up, stats = pl.pallas_call(
        functools.partial(first_body, n_pair, len(others)),
        out_shape=(field, message, message, stats_struct),
        in_specs=[SMEM] + [VMEM] * (9 + len(others)),
        out_specs=(VMEM,) * 4,
        scratch_shapes=scratch(),
        compiler_params=params,
        name="first",
    )(
        index, blended, from_above, from_below, stats, *others, same, other,
        row_of(first_gain), row_of(first_shift), row_of(first_bias),
    )

    from_above, from_below, others = exchange(down, up, stats)
    half = struct((frames_each, rows, width, channels))
    kept, sent = pl.pallas_call(
        functools.partial(second_body, n_pair, len(others)),
        out_shape=(half, half),
        in_specs=[SMEM] + [VMEM] * (10 + len(others)),
        out_specs=(VMEM,) * 2,
        scratch_shapes=scratch() + [pltpu.VMEM(field.shape, BF16)],
        compiler_params=params,
        name="second",
    )(
        index, first_out, from_above, from_below, stats, *others, same, other,
        row_of(second_gain), row_of(second_shift), row_of(second_bias), blended,
    )
    received = lax.ppermute(sent, "core", [(0, 1), (1, 0)])
    early = jnp.where(core == 0, kept, received)
    late = jnp.where(core == 0, received, kept)
    return jnp.concatenate([early, late], axis=0)[:capacity]


def per_device(video, *rest):
    n_height = lax.axis_size("pair") * lax.axis_size("core")
    if slots_of(video.shape[0], lax.axis_size("frame")) >= n_height:
        return whole_frames(video, *rest)
    return split_rows(video, *rest)


def solution(mesh):
    n_frame, n_height = mesh.devices.shape
    split = Mesh(mesh.devices.reshape(n_frame, n_height // 2, 2), ("frame", "pair", "core"))
    height = ("pair", "core")
    placed = (
        P(None, height, "frame", None),
        P(),
        P(),
        P(),
        P(),
        P(),
        P(height, None),
        P(),
        P(),
        P(),
        P(height, None),
        P(),
    )
    return jax.shard_map(
        per_device,
        mesh=split,
        in_specs=placed,
        out_specs=P("frame", height, None, None),
        check_vma=False,
    )
```

```python
import functools

import jax
import jax.numpy as jnp
from jax import lax
from jax.experimental import pallas as pl
from jax.experimental.pallas import tpu as pltpu
from jax.sharding import Mesh, PartitionSpec as P

GROUPS = 32
EPS = 1e-06
VMEM = pl.BlockSpec(memory_space=pltpu.VMEM)
SMEM = pl.BlockSpec(memory_space=pltpu.SMEM)
HBM = pl.BlockSpec(memory_space=pl.ANY)
F32, BF16 = jnp.float32, jnp.bfloat16


def up_to(number, multiple):
    return -(-number // multiple) * multiple


def slots_of(frames, n_frame):
    return min(2 * ((frames + n_frame - 1) // n_frame), frames - n_frame + 1)


def silu(values):
    half = 0.5 * values
    return half + half * jnp.tanh(half)


def with_column_taps(values):
    axis, width = values.ndim - 2, values.shape[-2]
    column = lax.broadcasted_iota(jnp.int32, values.shape, axis)
    before = jnp.where(column == 0, 0.0, pltpu.roll(values, 1, axis))
    after = jnp.where(column == width - 1, 0.0, pltpu.roll(values, width - 1, axis))
    return jnp.concatenate([before.astype(BF16), values.astype(BF16), after.astype(BF16)], axis=-1)


def frame_offset(counts_ref, owner):
    offset = jnp.int32(0)
    for index in range(counts_ref.shape[0]):
        offset = offset + jnp.where(index < owner, counts_ref[index], 0)
    return offset


def pick_body(halves, frames_each, counts_ref, video_ref, out_ref):
    frames = video_ref.shape[0]
    slots = out_ref.shape[1]
    for owner in range(counts_ref.shape[0]):
        offset = frame_offset(counts_ref, owner)
        for half in range(halves):
            for slot in range(slots):
                frame = offset + (half * frames_each + slot - 2)
                values = video_ref[jnp.clip(frame, 0, frames - 1)]
                out_ref[owner * halves + half, slot] = jnp.where(
                    frame >= 0, values, jnp.zeros_like(values)
                )


def temporal_body(halves, rows, part_ref, weight_ref, bias_ref, total_ref, taps_ref):
    peers, slots, cells, channels = part_ref.shape
    columns = cells // rows
    frames_each, all_rows, width = total_ref.shape[:3]

    def place(slot, _):
        for half in range(halves):
            for row in range(rows):
                values = jnp.concatenate(
                    [
                        part_ref[peer * halves + half, slot].astype(F32)[
                            row * columns : (row + 1) * columns
                        ]
                        for peer in range(peers // halves)
                    ],
                    axis=0,
                )
                at = half * rows + row
                taps_ref[slot, at] = with_column_taps(silu(values))

                @pl.when(slot >= 2)
                def _():
                    total_ref[slot - 2, at] = values + bias_ref[...]

        return 0

    lax.fori_loop(0, slots, place, 0)
    depth = 3 * channels
    for row_tap in range(3):
        low, high = max(0, 1 - row_tap), min(all_rows, all_rows + 1 - row_tap)
        for time_tap in range(3):
            patches = taps_ref[
                time_tap : time_tap + frames_each, low + row_tap - 1 : high + row_tap - 1
            ]
            start = (time_tap * 3 + row_tap) * depth
            product = jnp.dot(
                patches.reshape(frames_each * (high - low) * width, depth),
                weight_ref[start : start + depth],
                preferred_element_type=F32,
            )
            total_ref[:, low:high] += product.reshape(frames_each, high - low, width, channels)


def write_stats(field_ref, stats_ref):
    frames_each, rows, width, channels = field_ref.shape
    span = stats_ref.shape[0] // 3
    sums, squares = [], []
    for frame in range(frames_each):
        values = field_ref[frame].astype(F32).reshape(rows * width, channels)
        part_sum = jnp.sum(values, axis=0, keepdims=True)
        centered = values - part_sum * (1.0 / (rows * width))
        sums.append(part_sum)
        squares.append(jnp.sum(centered * centered, axis=0, keepdims=True))
    pad = [jnp.zeros((span - 2 * frames_each, channels), F32)] if span > 2 * frames_each else []
    rest = jnp.concatenate(sums + squares + pad, axis=0)
    for piece in range(3):
        rounded = rest.astype(BF16)
        stats_ref[piece * span : (piece + 1) * span] = rounded
        rest = rest - rounded.astype(F32)


def write_messages(field_ref, down_ref, up_ref, stats_ref):
    frames_each, rows, width, channels = field_ref.shape
    write_stats(field_ref, stats_ref)
    edge = frames_each * width
    down_ref[:edge] = field_ref[:, rows - 1].reshape(edge, channels)
    up_ref[:edge] = field_ref[:, 0].reshape(edge, channels)
    down_ref[edge:] = stats_ref[...]
    up_ref[edge:] = stats_ref[...]


def borders_body(
    n_pair,
    total_ref,
    above_ref,
    below_ref,
    weight_ref,
    blended_ref,
    down_ref,
    up_ref,
    stats_ref,
    taps_ref,
):
    frames_each, rows, width, channels = total_ref.shape
    slots = above_ref.shape[0]
    depth = 3 * channels

    def place(slot, _):
        taps_ref[0, slot] = with_column_taps(silu(above_ref[slot].astype(F32)))
        taps_ref[1, slot] = with_column_taps(silu(below_ref[slot].astype(F32)))
        return 0

    lax.fori_loop(0, slots, place, 0)
    for side, row, row_tap in ((0, 0, 0), (1, rows - 1, 2)):
        summed = total_ref[:, row].reshape(frames_each * width, channels)
        for time_tap in range(3):
            patches = taps_ref[side, time_tap : time_tap + frames_each]
            start = (time_tap * 3 + row_tap) * depth
            summed = summed + jnp.dot(
                patches.reshape(frames_each * width, depth),
                weight_ref[start : start + depth],
                preferred_element_type=F32,
            )
        blended_ref[:, row] = summed.reshape(frames_each, width, channels).astype(BF16)
    blended_ref[:, 1 : rows - 1] = total_ref[:, 1 : rows - 1].astype(BF16)
    write_messages(blended_ref, down_ref, up_ref, stats_ref)


def group_total(values, width_group):
    lane = lax.broadcasted_iota(jnp.int32, values.shape, 1)
    size, step = values.shape[1], 1
    while step < width_group:
        upper = (lane // step) % 2 == 1
        values = values + jnp.where(
            upper, pltpu.roll(values, step, 1), pltpu.roll(values, size - step, 1)
        )
        step *= 2
    return values


def scale_and_offset(frames_each, cells, stats, gain_ref, shift_ref):
    channels = stats[0].shape[1]
    width_group = channels // GROUPS
    span = stats[0].shape[0] // 3
    parts = []
    for packed in stats:
        pieces = [packed[i * span : (i + 1) * span].astype(F32) for i in range(3)]
        parts.append(pieces[0] + (pieces[1] + pieces[2]))
    sums = [part[:frames_each] for part in parts]
    squares = [part[frames_each : 2 * frames_each] for part in parts]
    sample = float(cells * len(parts) * width_group)
    mean = group_total(functools.reduce(jnp.add, sums), width_group) * (1.0 / sample)
    spread = functools.reduce(jnp.add, squares)
    for part_sum in sums:
        apart = part_sum * (1.0 / cells) - mean
        spread = spread + float(cells) * apart * apart
    variance = group_total(spread, width_group) * (1.0 / sample)
    scale = lax.rsqrt(variance + EPS) * gain_ref[...]
    return scale, shift_ref[...] - mean * scale


def normed_taps(
    n_pair, index_ref, field_ref, above_ref, below_ref, stats, gain_ref, shift_ref, taps_ref,
    scale_ref, offset_ref,
):
    frames_each, rows, width, channels = field_ref.shape
    scale, offset = scale_and_offset(frames_each, rows * width, stats, gain_ref, shift_ref)
    for frame in range(frames_each):
        scale_ref[frame] = scale[frame : frame + 1]
        offset_ref[frame] = offset[frame : frame + 1]
    pair = index_ref[0]
    top = jnp.where(pair > 0, 1.0, 0.0)
    bottom = jnp.where(pair < n_pair - 1, 1.0, 0.0)

    def place(frame, _):
        scale_row, offset_row = scale_ref[frame], offset_ref[frame]
        for row in range(rows):
            values = field_ref[frame, row].astype(F32) * scale_row + offset_row
            taps_ref[frame, row + 1] = with_column_taps(silu(values))
        edge = pl.ds(pl.multiple_of(frame * width, width), width)
        values = silu(above_ref[edge].astype(F32) * scale_row + offset_row) * top
        taps_ref[frame, 0] = with_column_taps(values)
        values = silu(below_ref[edge].astype(F32) * scale_row + offset_row) * bottom
        taps_ref[frame, rows + 1] = with_column_taps(values)
        return 0

    lax.fori_loop(0, frames_each, place, 0)


def gather_weight(n_pair, which, index_ref, same_ref, other_ref, weight_ref):
    depth = weight_ref.shape[0] // (2 * n_pair)
    if same_ref.shape[0] != n_pair:
        weight_ref[...] = same_ref[which]
        return
    pair, core = index_ref[0], index_ref[1]
    for step in range(n_pair):
        source = lax.rem(pair - step + n_pair, n_pair)
        for parts_ref, of_core in ((same_ref, core), (other_ref, 1 - core)):
            shard = source * 2 + of_core
            rows = pl.ds(pl.multiple_of(shard * depth, depth), depth)
            weight_ref[rows] = parts_ref[step, which * depth : (which + 1) * depth]


def convolved(rows, row, taps_ref, weight_ref):
    frames_each, _, width, depth = taps_ref.shape
    summed = None
    for row_tap in range(3):
        patches = taps_ref[:, row + row_tap : row + row_tap + rows]
        product = jnp.dot(
            patches.reshape(frames_each * rows * width, depth),
            weight_ref[row_tap * depth : (row_tap + 1) * depth],
            preferred_element_type=F32,
        )
        summed = product if summed is None else summed + product
    return summed


def first_body(
    n_pair,
    n_others,
    index_ref,
    blended_ref,
    from_above_ref,
    from_below_ref,
    own_ref,
    *refs,
):
    others, refs = refs[:n_others], refs[n_others:]
    (
        same_ref, other_ref, gain_ref, shift_ref, bias_ref,
        out_ref, down_ref, up_ref, stats_ref,
        taps_ref, weight_ref, scale_ref, offset_ref,
    ) = refs
    frames_each, rows, width, channels = blended_ref.shape
    edge = frames_each * width
    stats = [own_ref[...], from_above_ref[edge:]]
    if n_pair > 2:
        stats.append(from_below_ref[edge:])
    stats = stats + [ref[...] for ref in others]
    normed_taps(
        n_pair, index_ref, blended_ref, from_above_ref, from_below_ref, stats,
        gain_ref, shift_ref, taps_ref, scale_ref, offset_ref,
    )
    gather_weight(n_pair, 0, index_ref, same_ref, other_ref, weight_ref)
    summed = convolved(rows, 0, taps_ref, weight_ref) + bias_ref[...]
    out_ref[...] = summed.astype(BF16).reshape(frames_each, rows, width, channels)
    write_messages(out_ref, down_ref, up_ref, stats_ref)


def second_body(
    n_pair,
    n_others,
    index_ref,
    field_ref,
    from_above_ref,
    from_below_ref,
    own_ref,
    *refs,
):
    others, refs = refs[:n_others], refs[n_others:]
    (
        same_ref, other_ref, gain_ref, shift_ref, bias_ref, blended_ref,
        kept_ref, sent_ref,
        taps_ref, weight_ref, scale_ref, offset_ref, whole_ref,
    ) = refs
    frames_each, rows, width, channels = field_ref.shape
    edge = frames_each * width
    stats = [own_ref[...], from_above_ref[edge:]]
    if n_pair > 2:
        stats.append(from_below_ref[edge:])
    stats = stats + [ref[...] for ref in others]
    normed_taps(
        n_pair, index_ref, field_ref, from_above_ref, from_below_ref, stats,
        gain_ref, shift_ref, taps_ref, scale_ref, offset_ref,
    )
    gather_weight(n_pair, 1, index_ref, same_ref, other_ref, weight_ref)
    core, count = index_ref[1], index_ref[2]
    summed = convolved(rows, 0, taps_ref, weight_ref) + bias_ref[...]
    summed = summed.reshape(frames_each, rows, width, channels) + blended_ref[...].astype(F32)
    half = rows // 2
    for frame in range(frames_each):
        live = core * frames_each + frame < count
        whole_ref[frame] = jnp.where(live, summed[frame], 0.0).astype(BF16)
    kept_ref[...] = whole_ref[:, pl.ds(core * half, half)]
    sent_ref[...] = whole_ref[:, pl.ds((1 - core) * half, half)]


def extremes(counts_ref):
    most = least = jnp.int32(0)
    high = low = counts_ref[0]
    for owner in range(1, counts_ref.shape[0]):
        count = counts_ref[owner]
        most, high = jnp.where(count > high, owner, most), jnp.maximum(count, high)
        least, low = jnp.where(count < low, owner, least), jnp.minimum(count, low)
    return most, least


def pick_frames_body(
    capacity, counts_ref, video_ref, out_ref, held_ref, placed_ref, held_sem, sems
):
    load = pltpu.make_async_copy(video_ref, held_ref, held_sem)
    load.start()
    frames, (parts, sent) = video_ref.shape[0], out_ref.shape[:2]
    n_owner = counts_ref.shape[0]
    span, each = parts // n_owner, sent - 1
    most, least = extremes(counts_ref)
    last = frame_offset(counts_ref, most) + (capacity - 2 * each)
    load.wait()
    copies = []
    for owner in range(n_owner):
        offset = frame_offset(counts_ref, owner)
        for part in range(span):
            pair, core = part // 2, part % 2
            base = offset + 2 * each * pair
            if pair == span // 2 - 1:
                base = jnp.where(least == owner, last, base)
            for place in range(sent):
                frame = base + (2 * each - 1 - place if core else place - 2)
                values = held_ref[jnp.clip(frame, 0, frames - 1)]
                if not core and place < 2:
                    values = jnp.where(frame >= 0, values, jnp.zeros_like(values))
                placed_ref[owner * span + part, place] = values
        rows = pl.ds(owner * span, span)
        copies.append(
            pltpu.make_async_copy(placed_ref.at[rows], out_ref.at[rows], sems.at[owner])
        )
        copies[-1].start()
    for copy in copies:
        copy.wait()


def group_spread(values, width_group):
    lane = lax.broadcasted_iota(jnp.int32, values.shape, 1) % width_group
    size, total = values.shape[1], values
    for step in range(1, width_group):
        total = total + jnp.where(
            lane >= step,
            pltpu.roll(values, step, 1),
            pltpu.roll(values, size - width_group + step, 1),
        )
    return total


def interleave(main, side, pace):
    for _ in main:
        for _ in range(pace):
            next(side, None)
    for _ in side:
        pass


def frames_body(
    part_ref, swapped_ref, temporal_ref, same_ref, other_ref, *refs
):
    vectors, (out_ref, *refs) = refs[:7], refs[7:]
    n_height, each, rows, width, channels = out_ref.shape
    places = each + 2
    taps_refs, refs = refs[:places], refs[places:]
    normed_refs, refs = refs[:each], refs[each:]
    total_refs, refs = refs[:each], refs[each:]
    blended_refs, refs = refs[:each], refs[each:]
    field_refs, refs = refs[:each], refs[each:]
    landed_refs, refs = refs[:places], refs[places:]
    raw_ref, time_ref, weights_ref, done_ref, vectors_ref, *refs = refs
    land_sems, time_sems, sems, out_sems, vector_sems = refs
    n_pair = n_height // 2
    n_frame = part_ref.shape[0] // n_height
    columns = width // n_frame
    all_rows = n_height * rows
    depth = 3 * channels
    cells = all_rows * width
    width_group = channels // GROUPS
    pair, core = lax.axis_index("pair"), lax.axis_index("core")
    span = same_ref.shape[2]
    landings = [
        pltpu.make_async_copy(
            part_ref.at[:, place] if place <= each else swapped_ref,
            landed_refs[place],
            land_sems.at[place],
        )
        for place in range(places)
    ]
    time_copies = []
    for step in range(3):
        tap = step + core * (2 - 2 * step)
        begin = pl.multiple_of(tap * 3 * depth, 3 * depth)
        time_copies.append(
            pltpu.make_async_copy(
                temporal_ref.at[pl.ds(begin, 3 * depth)], time_ref.at[step], time_sems.at[step]
            )
        )
    vector_copies = [
        pltpu.make_async_copy(ref, vectors_ref.at[line], vector_sems.at[line])
        for line, ref in enumerate(vectors)
    ]
    copies = []
    for which in range(2):
        of_weight = []
        for step in range(n_pair):
            source = lax.rem(pair - step + n_pair, n_pair)
            for side, (parts_ref, of_core) in enumerate(((same_ref, core), (other_ref, 1 - core))):
                begin = pl.multiple_of((source * 2 + of_core) * span, span)
                of_weight.append(
                    pltpu.make_async_copy(
                        parts_ref.at[step, which],
                        weights_ref.at[which, pl.ds(begin, span)],
                        sems.at[which, step, side],
                    )
                )
        copies.append(of_weight)
    for copy in landings[:3] + time_copies + landings[3:] + vector_copies + copies[0] + copies[1]:
        copy.start()

    border = jnp.zeros((width, depth), BF16)
    for ref in taps_refs + normed_refs:
        ref[0] = border
        ref[all_rows + 1] = border

    def lay(place):
        landings[place].wait()
        for height in range(n_height):
            pieces = [
                landed_refs[place][peer * n_height + height].astype(F32)
                for peer in range(n_frame)
            ]
            for row in range(rows):
                values = jnp.concatenate(
                    [piece[row * columns : (row + 1) * columns] for piece in pieces], axis=0
                )
                raw_ref[place, height * rows + row] = values.astype(BF16)
                taps_refs[place][height * rows + row + 1] = with_column_taps(silu(values))
            yield

    parts_of_field = 2
    part_rows = all_rows // parts_of_field
    part_cells = part_rows * width

    def products(source_ref, weight_ref, part):
        summed = None
        for row_tap in range(3):
            low = part * part_rows + row_tap
            product = jnp.dot(
                source_ref[low : low + part_rows].reshape(part_cells, depth),
                weight_ref[row_tap * depth : (row_tap + 1) * depth],
                preferred_element_type=F32,
            )
            summed = product if summed is None else summed + product
            yield summed

    def temporal(place):
        for step in range(3):
            if place == 0:
                time_copies[step].wait()
            for part in range(parts_of_field):
                for summed in products(taps_refs[place + step], time_ref.at[step], part):
                    yield
                cut = slice(part * part_cells, (part + 1) * part_cells)
                if step == 0:
                    total_refs[place][cut] = summed
                else:
                    total_refs[place][cut] += summed

    def convolve(place, which):
        for part in range(parts_of_field):
            for summed in products(normed_refs[place], weights_ref.at[which], part):
                yield
            total_refs[place][part * part_cells : (part + 1) * part_cells] = summed

    def norm(place, field_ref, row_of, gain, shift):
        pivot = None
        sums = squares = jnp.zeros((8, channels), F32)
        for row in range(all_rows):
            rounded = row_of(row).astype(BF16)
            field_ref[row] = rounded
            values = rounded.astype(F32)
            if pivot is None:
                pivot = values[:1]
            apart = (values - pivot).reshape(width // 8, 8, channels)
            sums = sums + jnp.sum(apart, axis=0)
            squares = squares + jnp.sum(apart * apart, axis=0)
            if row % 4 == 3:
                yield
        own = jnp.sum(sums, axis=0, keepdims=True) * (1.0 / cells)
        squares = jnp.sum(squares, axis=0, keepdims=True) * (1.0 / cells)
        sample = 1.0 / width_group
        mean = group_spread(own + pivot, width_group) * sample
        off = own + pivot - mean
        spread = squares - own * own + off * off
        variance = jnp.maximum(group_spread(spread, width_group) * sample, 0.0)
        scale = lax.rsqrt(variance + EPS) * gain
        offset = 0.5 * (shift - mean * scale)
        scale = 0.5 * scale
        yield
        for row in range(all_rows):
            half = field_ref[row].astype(F32) * scale + offset
            normed_refs[place][row + 1] = with_column_taps(half + half * jnp.tanh(half))
            if row % 2 == 1:
                yield

    def first_norm(place):
        raw_at = place + 2 - 2 * core

        def row_of(row):
            product = total_refs[place][row * width : (row + 1) * width]
            return raw_ref[raw_at, row].astype(F32) + product + temporal_bias

        return norm(place, blended_refs[place], row_of, first_gain, first_shift)

    def second_norm(place):
        def row_of(row):
            return total_refs[place][row * width : (row + 1) * width] + first_bias

        return norm(place, field_refs[place], row_of, second_gain, second_shift)

    def finish(place):
        at = place + core * (each - 1 - 2 * place)
        for row in range(all_rows):
            product = total_refs[place][row * width : (row + 1) * width] + second_bias
            decoded = blended_refs[place][row].astype(F32) + product
            done_ref[place, row // rows, row % rows] = decoded.astype(BF16)
            if row % 4 == 3:
                yield
        store = pltpu.make_async_copy(
            done_ref.at[place], out_ref.at[:, at], out_sems.at[place]
        )
        store.start()
        stores.append(store)

    stores = []

    def ready(which):
        for copy in which:
            copy.wait()

    def both(one, other):
        yield from one
        yield from other

    nothing = iter(())
    for place in range(3):
        interleave(lay(place), nothing, 0)
    laying = nothing
    for place in range(3, places):
        laying = both(laying, lay(place))
    interleave(temporal(0), laying, 1)
    ready(vector_copies)
    (
        temporal_bias, first_gain, first_shift, first_bias, second_gain, second_shift, second_bias
    ) = [vectors_ref[line] for line in range(7)]
    for place in range(1, each):
        interleave(temporal(place), first_norm(place - 1), 1)
    ready(copies[0])
    pending = first_norm(each - 1)
    for place in range(each):
        interleave(convolve(place, 0), pending, 3)
        pending = second_norm(place)
    ready(copies[1])
    for place in range(each):
        interleave(convolve(place, 1), pending, 3)
        pending = finish(place)
    interleave(pending, nothing, 0)
    ready(stores)


def ring(size, step):
    return [(i, (i + step) % size) for i in range(size)]


def whole_frames(
    video, frame_counts, temporal_weight, temporal_bias, first_gain, first_shift, first_weight,
    first_bias, second_gain, second_shift, second_weight, second_bias,
):
    frames, rows, columns, channels = video.shape
    n_frame, n_pair = lax.axis_size("frame"), lax.axis_size("pair")
    n_height = 2 * n_pair
    width = columns * n_frame
    all_rows = rows * n_height
    capacity = slots_of(frames, n_frame)
    each = capacity // n_height
    extra = capacity - each * n_height
    params = pltpu.CompilerParams(vmem_limit_bytes=60 * 1024 * 1024)
    swap = [(0, 1), (1, 0)]

    picked = pl.pallas_call(
        functools.partial(pick_frames_body, capacity),
        out_shape=jax.ShapeDtypeStruct(
            (n_frame * n_height, each + 1, rows * columns, channels), BF16
        ),
        in_specs=[SMEM, HBM],
        out_specs=HBM,
        scratch_shapes=[
            pltpu.VMEM((frames, rows * columns, channels), BF16),
            pltpu.VMEM((n_frame * n_height, each + 1, rows * columns, channels), BF16),
            pltpu.SemaphoreType.DMA(()),
            pltpu.SemaphoreType.DMA((n_frame,)),
        ],
        compiler_params=params,
        name="pick",
    )(frame_counts, video.reshape(frames, rows * columns, channels))
    parts = lax.all_to_all(picked, ("frame", "pair", "core"), split_axis=0, concat_axis=0)
    swapped = lax.ppermute(parts[:, each], "core", swap)

    own = jnp.stack([first_weight, second_weight])
    same = jnp.stack(
        [own] + [lax.ppermute(own, "pair", ring(n_pair, step)) for step in range(1, n_pair)]
    )
    other = lax.ppermute(same, "core", swap)

    vectors = (
        temporal_bias, first_gain, first_shift, first_bias, second_gain, second_shift, second_bias
    )
    field = (all_rows, width, channels)
    taps = (all_rows + 2, width, 3 * channels)
    decoded = pl.pallas_call(
        frames_body,
        out_shape=jax.ShapeDtypeStruct((n_height, each, rows, width, channels), BF16),
        in_specs=[HBM] * 12,
        out_specs=HBM,
        scratch_shapes=[pltpu.VMEM(taps, BF16)] * (2 * each + 2)
        + [pltpu.VMEM((all_rows * width, channels), F32)] * each
        + [pltpu.VMEM(field, BF16)] * (2 * each)
        + [pltpu.VMEM((n_frame * n_height, rows * columns, channels), BF16)] * (each + 2)
        + [
            pltpu.VMEM((each + 2,) + field, BF16),
            pltpu.VMEM((3, 9 * channels, channels), BF16),
            pltpu.VMEM((2, 9 * channels, channels), BF16),
            pltpu.VMEM((each, n_height, rows, width, channels), BF16),
            pltpu.VMEM((7, 1, channels), F32),
            pltpu.SemaphoreType.DMA((each + 2,)),
            pltpu.SemaphoreType.DMA((3,)),
            pltpu.SemaphoreType.DMA((2, n_pair, 2)),
            pltpu.SemaphoreType.DMA((each,)),
            pltpu.SemaphoreType.DMA((7,)),
        ],
        compiler_params=pltpu.CompilerParams(vmem_limit_bytes=52 * 1024 * 1024),
        name="frames",
    )(
        parts, swapped, temporal_weight, same, other,
        *[vector.reshape(1, channels) for vector in vectors],
    )
    owned = lax.all_to_all(decoded, ("pair", "core"), split_axis=0, concat_axis=0)
    owned = owned.reshape((n_height * each,) + owned.shape[2:])
    if extra:
        most, least = jnp.argmax(frame_counts), jnp.argmin(frame_counts)

        def homeward(route):
            source, target = route % n_frame, route // n_frame
            if source == target:
                return jnp.zeros_like
            return lambda rows: lax.ppermute(rows, "frame", [(source, target)])

        owned = jnp.concatenate(
            [
                owned,
                lax.switch(
                    most * n_frame + least,
                    [homeward(route) for route in range(n_frame * n_frame)],
                    owned[-extra:],
                ),
            ]
        )
    mine = lax.dynamic_index_in_dim(frame_counts, lax.axis_index("frame"), keepdims=False)
    live = jnp.arange(capacity) < mine
    return jnp.where(live[:, None, None, None], owned, jnp.zeros_like(owned))


def split_rows(
    video,
    frame_counts,
    temporal_weight,
    temporal_bias,
    first_gain,
    first_shift,
    first_weight,
    first_bias,
    second_gain,
    second_shift,
    second_weight,
    second_bias,
):
    frames, rows, columns, channels = video.shape
    n_frame, n_pair = lax.axis_size("frame"), lax.axis_size("pair")
    width = columns * n_frame
    capacity = slots_of(frames, n_frame)
    frames_each = up_to(capacity, 2) // 2
    slots = frames_each + 2
    all_rows = 2 * rows
    edge = frames_each * width
    span = up_to(2 * frames_each, 16)
    params = pltpu.CompilerParams(vmem_limit_bytes=20 * 1024 * 1024)

    def ring(step):
        return [(i, (i + step) % n_pair) for i in range(n_pair)]

    def line(step):
        return [(i, i + step) for i in range(n_pair) if 0 <= i + step < n_pair]

    def struct(shape, dtype=BF16):
        return jax.ShapeDtypeStruct(shape, dtype)

    def row_of(vector):
        return vector.reshape(1, channels)

    pair, core = lax.axis_index("pair"), lax.axis_index("core")
    owner = lax.axis_index("frame")
    my_count = lax.dynamic_index_in_dim(frame_counts, owner, keepdims=False)
    index = jnp.stack([pair, core, my_count]).astype(jnp.int32)

    picked = pl.pallas_call(
        functools.partial(pick_body, 2, frames_each),
        out_shape=struct((n_frame * 2, slots, rows * columns, channels)),
        in_specs=[SMEM, VMEM],
        out_specs=VMEM,
        compiler_params=params,
        name="pick",
    )(frame_counts, video.reshape(frames, rows * columns, channels))
    parts = lax.all_to_all(picked, ("frame", "core"), split_axis=0, concat_axis=0)

    if first_weight.shape[0] % 16 == 0 and n_pair > 2:
        own_weights = jnp.concatenate([first_weight, second_weight], axis=0)
        same = jnp.stack(
            [own_weights]
            + [lax.ppermute(own_weights, "pair", ring(step)) for step in range(1, n_pair)]
        )
        other = lax.ppermute(same, "core", [(0, 1), (1, 0)])
    else:
        both = (first_weight, second_weight)
        same = jnp.stack([lax.all_gather(w, ("pair", "core"), tiled=True) for w in both])
        other = jnp.zeros((16, channels), BF16)

    by_place = parts.reshape(n_frame, 2, slots, rows, columns, channels)

    def edge_row(array):
        return array.transpose(1, 0, 2, 3).reshape(slots, width, channels)

    above = lax.ppermute(edge_row(by_place[:, 1, :, rows - 1]), "pair", line(1))
    below = lax.ppermute(edge_row(by_place[:, 0, :, 0]), "pair", line(-1))

    total = pl.pallas_call(
        functools.partial(temporal_body, 2, rows),
        out_shape=struct((frames_each, all_rows, width, channels), F32),
        in_specs=[VMEM] * 3,
        out_specs=VMEM,
        scratch_shapes=[pltpu.VMEM((slots, all_rows, width, 3 * channels), BF16)],
        compiler_params=params,
        name="temporal",
    )(parts, temporal_weight, row_of(temporal_bias))

    field = struct((frames_each, all_rows, width, channels))
    message = struct((edge + 3 * span, channels))
    stats_struct = struct((3 * span, channels))

    blended, down, up, stats = pl.pallas_call(
        functools.partial(borders_body, n_pair),
        out_shape=(field, message, message, stats_struct),
        in_specs=[VMEM] * 4,
        out_specs=(VMEM,) * 4,
        scratch_shapes=[pltpu.VMEM((2, slots, width, 3 * channels), BF16)],
        compiler_params=params,
        name="borders",
    )(total, above, below, temporal_weight)

    def exchange(down, up, stats):
        from_above = lax.ppermute(down, "pair", ring(1))
        from_below = lax.ppermute(up, "pair", ring(-1))
        others = [lax.ppermute(stats, "pair", ring(step)) for step in range(2, n_pair - 1)]
        return from_above, from_below, others

    def scratch():
        return [
            pltpu.VMEM((frames_each, all_rows + 2, width, 3 * channels), BF16),
            pltpu.VMEM((9 * channels, channels), BF16),
            pltpu.VMEM((frames_each, 1, channels), F32),
            pltpu.VMEM((frames_each, 1, channels), F32),
        ]

    from_above, from_below, others = exchange(down, up, stats)
    first_out, down, up, stats = pl.pallas_call(
        functools.partial(first_body, n_pair, len(others)),
        out_shape=(field, message, message, stats_struct),
        in_specs=[SMEM] + [VMEM] * (9 + len(others)),
        out_specs=(VMEM,) * 4,
        scratch_shapes=scratch(),
        compiler_params=params,
        name="first",
    )(
        index, blended, from_above, from_below, stats, *others, same, other,
        row_of(first_gain), row_of(first_shift), row_of(first_bias),
    )

    from_above, from_below, others = exchange(down, up, stats)
    half = struct((frames_each, rows, width, channels))
    kept, sent = pl.pallas_call(
        functools.partial(second_body, n_pair, len(others)),
        out_shape=(half, half),
        in_specs=[SMEM] + [VMEM] * (10 + len(others)),
        out_specs=(VMEM,) * 2,
        scratch_shapes=scratch() + [pltpu.VMEM(field.shape, BF16)],
        compiler_params=params,
        name="second",
    )(
        index, first_out, from_above, from_below, stats, *others, same, other,
        row_of(second_gain), row_of(second_shift), row_of(second_bias), blended,
    )
    received = lax.ppermute(sent, "core", [(0, 1), (1, 0)])
    early = jnp.where(core == 0, kept, received)
    late = jnp.where(core == 0, received, kept)
    return jnp.concatenate([early, late], axis=0)[:capacity]


def per_device(video, *rest):
    frames, n_frame = video.shape[0], lax.axis_size("frame")
    n_height = lax.axis_size("pair") * lax.axis_size("core")
    capacity = slots_of(frames, n_frame)
    each, extra = divmod(capacity, n_height)
    room = each * (n_height - 2)
    fits = each > 0 and extra <= 2 * each and n_frame > 1
    if fits and 2 * (each * n_height + 1) > frames and frames - capacity < n_frame * room:
        return whole_frames(video, *rest)
    return split_rows(video, *rest)


def solution(mesh):
    n_frame, n_height = mesh.devices.shape
    split = Mesh(mesh.devices.reshape(n_frame, n_height // 2, 2), ("frame", "pair", "core"))
    height = ("pair", "core")
    placed = (
        P(None, height, "frame", None),
        P(),
        P(),
        P(),
        P(),
        P(),
        P(height, None),
        P(),
        P(),
        P(),
        P(height, None),
        P(),
    )
    return jax.shard_map(
        per_device,
        mesh=split,
        in_specs=placed,
        out_specs=P("frame", height, None, None),
        check_vma=False,
    )
```

```python
import functools
import itertools

import jax
import jax.numpy as jnp
from jax import lax
from jax.experimental import pallas as pl
from jax.experimental.pallas import tpu as pltpu
from jax.sharding import Mesh, PartitionSpec as P

GROUPS = 32
EPS = 1e-06
VMEM = pl.BlockSpec(memory_space=pltpu.VMEM)
SMEM = pl.BlockSpec(memory_space=pltpu.SMEM)
HBM = pl.BlockSpec(memory_space=pl.ANY)
F32, BF16 = jnp.float32, jnp.bfloat16


def up_to(number, multiple):
    return -(-number // multiple) * multiple


def slots_of(frames, n_frame):
    return min(2 * ((frames + n_frame - 1) // n_frame), frames - n_frame + 1)


def silu(values):
    half = 0.5 * values
    return half + half * jnp.tanh(half)


def with_column_taps(values):
    axis, width = values.ndim - 2, values.shape[-2]
    column = lax.broadcasted_iota(jnp.int32, values.shape, axis)
    before = jnp.where(column == 0, 0.0, pltpu.roll(values, 1, axis))
    after = jnp.where(column == width - 1, 0.0, pltpu.roll(values, width - 1, axis))
    return jnp.concatenate([before.astype(BF16), values.astype(BF16), after.astype(BF16)], axis=-1)


def frame_offset(counts_ref, owner):
    offset = jnp.int32(0)
    for index in range(counts_ref.shape[0]):
        offset = offset + jnp.where(index < owner, counts_ref[index], 0)
    return offset


def pick_body(halves, frames_each, counts_ref, video_ref, out_ref):
    frames = video_ref.shape[0]
    slots = out_ref.shape[1]
    for owner in range(counts_ref.shape[0]):
        offset = frame_offset(counts_ref, owner)
        for half in range(halves):
            for slot in range(slots):
                frame = offset + (half * frames_each + slot - 2)
                values = video_ref[jnp.clip(frame, 0, frames - 1)]
                out_ref[owner * halves + half, slot] = jnp.where(
                    frame >= 0, values, jnp.zeros_like(values)
                )


def temporal_body(halves, rows, part_ref, weight_ref, bias_ref, total_ref, taps_ref):
    peers, slots, cells, channels = part_ref.shape
    columns = cells // rows
    frames_each, all_rows, width = total_ref.shape[:3]

    def place(slot, _):
        for half in range(halves):
            for row in range(rows):
                values = jnp.concatenate(
                    [
                        part_ref[peer * halves + half, slot].astype(F32)[
                            row * columns : (row + 1) * columns
                        ]
                        for peer in range(peers // halves)
                    ],
                    axis=0,
                )
                at = half * rows + row
                taps_ref[slot, at] = with_column_taps(silu(values))

                @pl.when(slot >= 2)
                def _():
                    total_ref[slot - 2, at] = values + bias_ref[...]

        return 0

    lax.fori_loop(0, slots, place, 0)
    depth = 3 * channels
    for row_tap in range(3):
        low, high = max(0, 1 - row_tap), min(all_rows, all_rows + 1 - row_tap)
        for time_tap in range(3):
            patches = taps_ref[
                time_tap : time_tap + frames_each, low + row_tap - 1 : high + row_tap - 1
            ]
            start = (time_tap * 3 + row_tap) * depth
            product = jnp.dot(
                patches.reshape(frames_each * (high - low) * width, depth),
                weight_ref[start : start + depth],
                preferred_element_type=F32,
            )
            total_ref[:, low:high] += product.reshape(frames_each, high - low, width, channels)


def write_stats(field_ref, stats_ref):
    frames_each, rows, width, channels = field_ref.shape
    span = stats_ref.shape[0] // 3
    sums, squares = [], []
    for frame in range(frames_each):
        values = field_ref[frame].astype(F32).reshape(rows * width, channels)
        part_sum = jnp.sum(values, axis=0, keepdims=True)
        centered = values - part_sum * (1.0 / (rows * width))
        sums.append(part_sum)
        squares.append(jnp.sum(centered * centered, axis=0, keepdims=True))
    pad = [jnp.zeros((span - 2 * frames_each, channels), F32)] if span > 2 * frames_each else []
    rest = jnp.concatenate(sums + squares + pad, axis=0)
    for piece in range(3):
        rounded = rest.astype(BF16)
        stats_ref[piece * span : (piece + 1) * span] = rounded
        rest = rest - rounded.astype(F32)


def write_messages(field_ref, down_ref, up_ref, stats_ref):
    frames_each, rows, width, channels = field_ref.shape
    write_stats(field_ref, stats_ref)
    edge = frames_each * width
    down_ref[:edge] = field_ref[:, rows - 1].reshape(edge, channels)
    up_ref[:edge] = field_ref[:, 0].reshape(edge, channels)
    down_ref[edge:] = stats_ref[...]
    up_ref[edge:] = stats_ref[...]


def borders_body(
    n_pair,
    total_ref,
    above_ref,
    below_ref,
    weight_ref,
    blended_ref,
    down_ref,
    up_ref,
    stats_ref,
    taps_ref,
):
    frames_each, rows, width, channels = total_ref.shape
    slots = above_ref.shape[0]
    depth = 3 * channels

    def place(slot, _):
        taps_ref[0, slot] = with_column_taps(silu(above_ref[slot].astype(F32)))
        taps_ref[1, slot] = with_column_taps(silu(below_ref[slot].astype(F32)))
        return 0

    lax.fori_loop(0, slots, place, 0)
    for side, row, row_tap in ((0, 0, 0), (1, rows - 1, 2)):
        summed = total_ref[:, row].reshape(frames_each * width, channels)
        for time_tap in range(3):
            patches = taps_ref[side, time_tap : time_tap + frames_each]
            start = (time_tap * 3 + row_tap) * depth
            summed = summed + jnp.dot(
                patches.reshape(frames_each * width, depth),
                weight_ref[start : start + depth],
                preferred_element_type=F32,
            )
        blended_ref[:, row] = summed.reshape(frames_each, width, channels).astype(BF16)
    blended_ref[:, 1 : rows - 1] = total_ref[:, 1 : rows - 1].astype(BF16)
    write_messages(blended_ref, down_ref, up_ref, stats_ref)


def group_total(values, width_group):
    lane = lax.broadcasted_iota(jnp.int32, values.shape, 1)
    size, step = values.shape[1], 1
    while step < width_group:
        upper = (lane // step) % 2 == 1
        values = values + jnp.where(
            upper, pltpu.roll(values, step, 1), pltpu.roll(values, size - step, 1)
        )
        step *= 2
    return values


def scale_and_offset(frames_each, cells, stats, gain_ref, shift_ref):
    channels = stats[0].shape[1]
    width_group = channels // GROUPS
    span = stats[0].shape[0] // 3
    parts = []
    for packed in stats:
        pieces = [packed[i * span : (i + 1) * span].astype(F32) for i in range(3)]
        parts.append(pieces[0] + (pieces[1] + pieces[2]))
    sums = [part[:frames_each] for part in parts]
    squares = [part[frames_each : 2 * frames_each] for part in parts]
    sample = float(cells * len(parts) * width_group)
    mean = group_total(functools.reduce(jnp.add, sums), width_group) * (1.0 / sample)
    spread = functools.reduce(jnp.add, squares)
    for part_sum in sums:
        apart = part_sum * (1.0 / cells) - mean
        spread = spread + float(cells) * apart * apart
    variance = group_total(spread, width_group) * (1.0 / sample)
    scale = lax.rsqrt(variance + EPS) * gain_ref[...]
    return scale, shift_ref[...] - mean * scale


def normed_taps(
    n_pair, index_ref, field_ref, above_ref, below_ref, stats, gain_ref, shift_ref, taps_ref,
    scale_ref, offset_ref,
):
    frames_each, rows, width, channels = field_ref.shape
    scale, offset = scale_and_offset(frames_each, rows * width, stats, gain_ref, shift_ref)
    for frame in range(frames_each):
        scale_ref[frame] = scale[frame : frame + 1]
        offset_ref[frame] = offset[frame : frame + 1]
    pair = index_ref[0]
    top = jnp.where(pair > 0, 1.0, 0.0)
    bottom = jnp.where(pair < n_pair - 1, 1.0, 0.0)

    def place(frame, _):
        scale_row, offset_row = scale_ref[frame], offset_ref[frame]
        for row in range(rows):
            values = field_ref[frame, row].astype(F32) * scale_row + offset_row
            taps_ref[frame, row + 1] = with_column_taps(silu(values))
        edge = pl.ds(pl.multiple_of(frame * width, width), width)
        values = silu(above_ref[edge].astype(F32) * scale_row + offset_row) * top
        taps_ref[frame, 0] = with_column_taps(values)
        values = silu(below_ref[edge].astype(F32) * scale_row + offset_row) * bottom
        taps_ref[frame, rows + 1] = with_column_taps(values)
        return 0

    lax.fori_loop(0, frames_each, place, 0)


def gather_weight(n_pair, which, index_ref, same_ref, other_ref, weight_ref):
    depth = weight_ref.shape[0] // (2 * n_pair)
    if same_ref.shape[0] != n_pair:
        weight_ref[...] = same_ref[which]
        return
    pair, core = index_ref[0], index_ref[1]
    for step in range(n_pair):
        source = lax.rem(pair - step + n_pair, n_pair)
        for parts_ref, of_core in ((same_ref, core), (other_ref, 1 - core)):
            shard = source * 2 + of_core
            rows = pl.ds(pl.multiple_of(shard * depth, depth), depth)
            weight_ref[rows] = parts_ref[step, which * depth : (which + 1) * depth]


def convolved(rows, row, taps_ref, weight_ref):
    frames_each, _, width, depth = taps_ref.shape
    summed = None
    for row_tap in range(3):
        patches = taps_ref[:, row + row_tap : row + row_tap + rows]
        product = jnp.dot(
            patches.reshape(frames_each * rows * width, depth),
            weight_ref[row_tap * depth : (row_tap + 1) * depth],
            preferred_element_type=F32,
        )
        summed = product if summed is None else summed + product
    return summed


def first_body(
    n_pair,
    n_others,
    index_ref,
    blended_ref,
    from_above_ref,
    from_below_ref,
    own_ref,
    *refs,
):
    others, refs = refs[:n_others], refs[n_others:]
    (
        same_ref, other_ref, gain_ref, shift_ref, bias_ref,
        out_ref, down_ref, up_ref, stats_ref,
        taps_ref, weight_ref, scale_ref, offset_ref,
    ) = refs
    frames_each, rows, width, channels = blended_ref.shape
    edge = frames_each * width
    stats = [own_ref[...], from_above_ref[edge:]]
    if n_pair > 2:
        stats.append(from_below_ref[edge:])
    stats = stats + [ref[...] for ref in others]
    normed_taps(
        n_pair, index_ref, blended_ref, from_above_ref, from_below_ref, stats,
        gain_ref, shift_ref, taps_ref, scale_ref, offset_ref,
    )
    gather_weight(n_pair, 0, index_ref, same_ref, other_ref, weight_ref)
    summed = convolved(rows, 0, taps_ref, weight_ref) + bias_ref[...]
    out_ref[...] = summed.astype(BF16).reshape(frames_each, rows, width, channels)
    write_messages(out_ref, down_ref, up_ref, stats_ref)


def second_body(
    n_pair,
    n_others,
    index_ref,
    field_ref,
    from_above_ref,
    from_below_ref,
    own_ref,
    *refs,
):
    others, refs = refs[:n_others], refs[n_others:]
    (
        same_ref, other_ref, gain_ref, shift_ref, bias_ref, blended_ref,
        kept_ref, sent_ref,
        taps_ref, weight_ref, scale_ref, offset_ref, whole_ref,
    ) = refs
    frames_each, rows, width, channels = field_ref.shape
    edge = frames_each * width
    stats = [own_ref[...], from_above_ref[edge:]]
    if n_pair > 2:
        stats.append(from_below_ref[edge:])
    stats = stats + [ref[...] for ref in others]
    normed_taps(
        n_pair, index_ref, field_ref, from_above_ref, from_below_ref, stats,
        gain_ref, shift_ref, taps_ref, scale_ref, offset_ref,
    )
    gather_weight(n_pair, 1, index_ref, same_ref, other_ref, weight_ref)
    core, count = index_ref[1], index_ref[2]
    summed = convolved(rows, 0, taps_ref, weight_ref) + bias_ref[...]
    summed = summed.reshape(frames_each, rows, width, channels) + blended_ref[...].astype(F32)
    half = rows // 2
    for frame in range(frames_each):
        live = core * frames_each + frame < count
        whole_ref[frame] = jnp.where(live, summed[frame], 0.0).astype(BF16)
    kept_ref[...] = whole_ref[:, pl.ds(core * half, half)]
    sent_ref[...] = whole_ref[:, pl.ds((1 - core) * half, half)]


def extremes(counts_ref):
    most = least = jnp.int32(0)
    high = low = counts_ref[0]
    for owner in range(1, counts_ref.shape[0]):
        count = counts_ref[owner]
        most, high = jnp.where(count > high, owner, most), jnp.maximum(count, high)
        least, low = jnp.where(count < low, owner, least), jnp.minimum(count, low)
    return most, least


def pick_frames_body(
    capacity, counts_ref, video_ref, out_ref, held_ref, placed_ref, held_sem, sems
):
    load = pltpu.make_async_copy(video_ref, held_ref, held_sem)
    load.start()
    frames, (parts, sent) = video_ref.shape[0], out_ref.shape[:2]
    n_owner = counts_ref.shape[0]
    span, each = parts // n_owner, sent - 1
    most, least = extremes(counts_ref)
    last = frame_offset(counts_ref, most) + (capacity - 2 * each)
    load.wait()
    copies = []
    for owner in range(n_owner):
        offset = frame_offset(counts_ref, owner)
        for part in range(span):
            pair, core = part // 2, part % 2
            base = offset + 2 * each * pair
            if pair == span // 2 - 1:
                base = jnp.where(least == owner, last, base)
            for place in range(sent):
                frame = base + (2 * each - 1 - place if core else place - 2)
                values = held_ref[jnp.clip(frame, 0, frames - 1)]
                if not core and place < 2:
                    values = jnp.where(frame >= 0, values, jnp.zeros_like(values))
                placed_ref[owner * span + part, place] = values
        rows = pl.ds(owner * span, span)
        copies.append(
            pltpu.make_async_copy(placed_ref.at[rows], out_ref.at[rows], sems.at[owner])
        )
        copies[-1].start()
    for copy in copies:
        copy.wait()


def group_spread(values, width_group):
    lane = lax.broadcasted_iota(jnp.int32, values.shape, 1) % width_group
    size, total = values.shape[1], values
    for step in range(1, width_group):
        total = total + jnp.where(
            lane >= step,
            pltpu.roll(values, step, 1),
            pltpu.roll(values, size - width_group + step, 1),
        )
    return total


def interleave(main, side, pace):
    for _ in main:
        for _ in range(pace):
            next(side, None)
    for _ in side:
        pass


def dot_pieces(source_ref, weight_ref, total_ref, add, parts=2):
    rows, width, depth = source_ref.shape
    part_rows = (rows - 2) // parts
    cells = part_rows * width
    for part in range(parts):
        summed = None
        for row_tap in range(3):
            low = part * part_rows + row_tap
            product = jnp.dot(
                source_ref[low : low + part_rows].reshape(cells, depth),
                weight_ref[row_tap * depth : (row_tap + 1) * depth],
                preferred_element_type=F32,
            )
            summed = product if summed is None else summed + product
            yield
        if add:
            total_ref[part * cells : (part + 1) * cells] += summed
        else:
            total_ref[part * cells : (part + 1) * cells] = summed


def norm_pieces(field_ref, normed_ref, row_of, gain, shift):
    all_rows, width, channels = field_ref.shape
    cells, width_group = all_rows * width, channels // GROUPS
    pivot = None
    sums = squares = jnp.zeros((8, channels), F32)
    for row in range(all_rows):
        if row_of is None:
            values = field_ref[row].astype(F32)
        else:
            rounded = row_of(row).astype(BF16)
            field_ref[row] = rounded
            values = rounded.astype(F32)
        if pivot is None:
            pivot = values[:1]
        apart = (values - pivot).reshape(width // 8, 8, channels)
        sums = sums + jnp.sum(apart, axis=0)
        squares = squares + jnp.sum(apart * apart, axis=0)
        if row % 4 == 3:
            yield
    own = jnp.sum(sums, axis=0, keepdims=True) * (1.0 / cells)
    squares = jnp.sum(squares, axis=0, keepdims=True) * (1.0 / cells)
    sample = 1.0 / width_group
    mean = group_spread(own + pivot, width_group) * sample
    off = own + pivot - mean
    spread = squares - own * own + off * off
    variance = jnp.maximum(group_spread(spread, width_group) * sample, 0.0)
    scale = lax.rsqrt(variance + EPS) * gain
    offset = 0.5 * (shift - mean * scale)
    scale = 0.5 * scale
    yield
    for row in range(all_rows):
        half = field_ref[row].astype(F32) * scale + offset
        normed_ref[row + 1] = with_column_taps(half + half * jnp.tanh(half))
        if row % 2 == 1:
            yield


def clear_borders(refs):
    for ref in refs:
        border = jnp.zeros(ref.shape[1:], BF16)
        ref[0] = border
        ref[ref.shape[0] - 1] = border


def start_all(copies):
    for copy in copies:
        copy.start()


def wait_all(copies):
    for copy in copies:
        copy.wait()


def frames_body(n_height, part_ref, swapped_ref, temporal_ref, bias_ref, gain_ref, shift_ref, *refs):
    normed_out_ref, blended_out_ref, order_ref, *refs = refs
    order_ref[...] = jnp.zeros_like(order_ref)
    each, all_rows, width, channels = blended_out_ref.shape
    places = each + 2
    taps_refs, refs = refs[:places], refs[places:]
    total_refs, refs = refs[:each], refs[each:]
    raw_ref, time_ref, time_sems = refs
    n_frame = part_ref.shape[0] // n_height
    columns, rows = width // n_frame, all_rows // n_height
    depth = 3 * channels
    core = lax.axis_index("core")

    time_copies = []
    for step in range(3):
        tap = step + core * (2 - 2 * step)
        begin = pl.multiple_of(tap * 3 * depth, 3 * depth)
        time_copies.append(
            pltpu.make_async_copy(
                temporal_ref.at[pl.ds(begin, 3 * depth)], time_ref.at[step], time_sems.at[step]
            )
        )
    start_all(time_copies)
    normed_refs = [normed_out_ref.at[place] for place in range(each - 1)]
    clear_borders(list(taps_refs) + normed_refs)

    def piece_of(place, source):
        return part_ref[source, place] if place <= each else swapped_ref[source]

    def lay(place):
        for height in range(n_height):
            pieces = [
                piece_of(place, peer * n_height + height).astype(F32) for peer in range(n_frame)
            ]
            for row in range(rows):
                values = jnp.concatenate(
                    [piece[row * columns : (row + 1) * columns] for piece in pieces], axis=0
                )
                raw_ref[place, height * rows + row] = values.astype(BF16)
                taps_refs[place][height * rows + row + 1] = with_column_taps(silu(values))
            yield

    def temporal(place, step):
        if place == 0:
            time_copies[step].wait()
        return dot_pieces(taps_refs[place + step], time_ref.at[step], total_refs[place], step > 0)

    def blended_row(place):
        raw_at = place + 2 - 2 * core

        def row_of(row):
            product = total_refs[place][row * width : (row + 1) * width]
            return raw_ref[raw_at, row].astype(F32) + product + bias_ref[...]

        return row_of

    nothing = iter(())
    for place in range(3):
        interleave(lay(place), nothing, 0)
    rest = itertools.chain.from_iterable(lay(place) for place in range(3, places))
    pieces = itertools.chain.from_iterable(temporal(0, step) for step in range(3))
    interleave(pieces, rest, 1)
    for place in range(1, each):
        norm = norm_pieces(
            blended_out_ref.at[place - 1], normed_refs[place - 1], blended_row(place - 1),
            gain_ref[...], shift_ref[...],
        )
        pieces = itertools.chain.from_iterable(temporal(place, step) for step in range(3))
        interleave(pieces, norm, 1)
    row_of = blended_row(each - 1)
    for row in range(all_rows):
        blended_out_ref[each - 1, row] = row_of(row).astype(BF16)


def spatial_body(n_pair, normed_ref, blended_ref, order_ref, *refs):
    same_refs, refs = refs[:n_pair], refs[n_pair:]
    other_refs, refs = refs[:n_pair], refs[n_pair:]
    gain_ref, shift_ref, first_bias_ref, second_gain_ref, second_shift_ref, *refs = refs
    second_bias_ref, out_ref, *refs = refs
    n_height, each, rows, width, channels = out_ref.shape
    all_rows = n_height * rows
    normed_refs, refs = refs[:each], refs[each:]
    total_refs, refs = refs[:each], refs[each:]
    field_refs, refs = refs[:each], refs[each:]
    weights_ref, done_ref, out_sems = refs
    pair, core = lax.axis_index("pair"), lax.axis_index("core")
    span = same_refs[0].shape[1]

    def gather(which):
        for step in range(n_pair):
            for shard_ref, of_core in ((same_refs[step], core), (other_refs[step], 1 - core)):
                source = jnp.bitwise_xor(pair, step) * 2 + of_core
                begin = pl.multiple_of(source * span, span)
                weights_ref[which, pl.ds(begin, span)] = shard_ref[which]
                yield

    clear_borders(normed_refs)

    def first_source(place):
        return normed_ref.at[place] if place < each - 1 else normed_refs[place]

    def second_norm(place):
        def row_of(row):
            return total_refs[place][row * width : (row + 1) * width] + first_bias_ref[...]

        return norm_pieces(
            field_refs[place], normed_refs[place], row_of, second_gain_ref[...],
            second_shift_ref[...],
        )

    def finish(place):
        at = place + core * (each - 1 - 2 * place)
        for row in range(all_rows):
            product = total_refs[place][row * width : (row + 1) * width] + second_bias_ref[...]
            decoded = blended_ref[place, row].astype(F32) + product
            done_ref[place, row // rows, row % rows] = decoded.astype(BF16)
            if row % 4 == 3:
                yield
        stores.append(
            pltpu.make_async_copy(done_ref.at[place], out_ref.at[:, at], out_sems.at[place])
        )
        stores[-1].start()

    stores = []
    pending = norm_pieces(
        blended_ref.at[each - 1], normed_refs[each - 1], None, gain_ref[...], shift_ref[...]
    )
    interleave(gather(0), pending, 1)
    pending = gather(1)
    for place in range(each):
        interleave(
            dot_pieces(first_source(place), weights_ref.at[0], total_refs[place], False),
            pending, 3,
        )
        pending = second_norm(place)
    for place in range(each):
        interleave(
            dot_pieces(normed_refs[place], weights_ref.at[1], total_refs[place], False),
            pending, 3,
        )
        pending = finish(place)
    interleave(pending, iter(()), 0)
    wait_all(stores)


def partners(size, step):
    return [(i, i ^ step) for i in range(size)]


def whole_frames(
    video, frame_counts, temporal_weight, temporal_bias, first_gain, first_shift, first_weight,
    first_bias, second_gain, second_shift, second_weight, second_bias,
):
    frames, rows, columns, channels = video.shape
    n_frame, n_pair = lax.axis_size("frame"), lax.axis_size("pair")
    n_height = 2 * n_pair
    width = columns * n_frame
    all_rows = rows * n_height
    capacity = slots_of(frames, n_frame)
    each = capacity // n_height
    extra = capacity - each * n_height
    params = pltpu.CompilerParams(vmem_limit_bytes=60 * 1024 * 1024)
    swap = [(0, 1), (1, 0)]

    picked = pl.pallas_call(
        functools.partial(pick_frames_body, capacity),
        out_shape=jax.ShapeDtypeStruct(
            (n_frame * n_height, each + 1, rows * columns, channels), BF16
        ),
        in_specs=[SMEM, HBM],
        out_specs=HBM,
        scratch_shapes=[
            pltpu.VMEM((frames, rows * columns, channels), BF16),
            pltpu.VMEM((n_frame * n_height, each + 1, rows * columns, channels), BF16),
            pltpu.SemaphoreType.DMA(()),
            pltpu.SemaphoreType.DMA((n_frame,)),
        ],
        compiler_params=params,
        name="pick",
    )(frame_counts, video.reshape(frames, rows * columns, channels))
    parts = lax.all_to_all(picked, ("frame", "pair", "core"), split_axis=0, concat_axis=0)
    swapped = lax.ppermute(parts[:, each], "core", swap)

    own = jnp.stack([first_weight, second_weight])
    same = [own] + [
        lax.ppermute(own, "pair", partners(n_pair, step)) for step in range(1, n_pair)
    ]

    def row_of(vector):
        return vector.reshape(1, channels)

    field = (all_rows, width, channels)
    taps = (all_rows + 2, width, 3 * channels)
    total = pltpu.VMEM((all_rows * width, channels), F32)
    limit = pltpu.CompilerParams(vmem_limit_bytes=50 * 1024 * 1024)
    normed, blended, order = pl.pallas_call(
        functools.partial(frames_body, n_height),
        out_shape=(
            jax.ShapeDtypeStruct((max(each - 1, 1),) + taps, BF16),
            jax.ShapeDtypeStruct((each,) + field, BF16),
            jax.ShapeDtypeStruct((8, 128), F32),
        ),
        in_specs=[VMEM, VMEM, HBM] + [VMEM] * 3,
        out_specs=(VMEM,) * 3,
        scratch_shapes=[pltpu.VMEM(taps, BF16)] * (each + 2)
        + [total] * each
        + [
            pltpu.VMEM((each + 2,) + field, BF16),
            pltpu.VMEM((3, 9 * channels, channels), BF16),
            pltpu.SemaphoreType.DMA((3,)),
        ],
        compiler_params=limit,
        name="frames",
    )(
        parts, swapped, temporal_weight,
        row_of(temporal_bias), row_of(first_gain), row_of(first_shift),
    )
    same[1:], order = lax.optimization_barrier((same[1:], order))
    other = [lax.ppermute(shard, "core", swap) for shard in same]
    decoded = pl.pallas_call(
        functools.partial(spatial_body, n_pair),
        out_shape=jax.ShapeDtypeStruct((n_height, each, rows, width, channels), BF16),
        in_specs=[VMEM] * (9 + 2 * n_pair),
        out_specs=HBM,
        scratch_shapes=[pltpu.VMEM(taps, BF16)] * each
        + [total] * each
        + [pltpu.VMEM(field, BF16)] * each
        + [
            pltpu.VMEM((2, 9 * channels, channels), BF16),
            pltpu.VMEM((each, n_height, rows, width, channels), BF16),
            pltpu.SemaphoreType.DMA((each,)),
        ],
        compiler_params=pltpu.CompilerParams(vmem_limit_bytes=20 * 1024 * 1024),
        name="spatial",
    )(
        normed, blended, order, *same, *other,
        row_of(first_gain), row_of(first_shift), row_of(first_bias),
        row_of(second_gain), row_of(second_shift), row_of(second_bias),
    )
    owned = lax.all_to_all(decoded, ("pair", "core"), split_axis=0, concat_axis=0)
    owned = owned.reshape((n_height * each,) + owned.shape[2:])
    if extra:
        most, least = jnp.argmax(frame_counts), jnp.argmin(frame_counts)

        def homeward(route):
            source, target = route % n_frame, route // n_frame
            if source == target:
                return jnp.zeros_like
            return lambda rows: lax.ppermute(rows, "frame", [(source, target)])

        owned = jnp.concatenate(
            [
                owned,
                lax.switch(
                    most * n_frame + least,
                    [homeward(route) for route in range(n_frame * n_frame)],
                    owned[-extra:],
                ),
            ]
        )
    mine = lax.dynamic_index_in_dim(frame_counts, lax.axis_index("frame"), keepdims=False)
    live = jnp.arange(capacity) < mine
    return jnp.where(live[:, None, None, None], owned, jnp.zeros_like(owned))


def split_rows(
    video,
    frame_counts,
    temporal_weight,
    temporal_bias,
    first_gain,
    first_shift,
    first_weight,
    first_bias,
    second_gain,
    second_shift,
    second_weight,
    second_bias,
):
    frames, rows, columns, channels = video.shape
    n_frame, n_pair = lax.axis_size("frame"), lax.axis_size("pair")
    width = columns * n_frame
    capacity = slots_of(frames, n_frame)
    frames_each = up_to(capacity, 2) // 2
    slots = frames_each + 2
    all_rows = 2 * rows
    edge = frames_each * width
    span = up_to(2 * frames_each, 16)
    params = pltpu.CompilerParams(vmem_limit_bytes=20 * 1024 * 1024)

    def ring(step):
        return [(i, (i + step) % n_pair) for i in range(n_pair)]

    def line(step):
        return [(i, i + step) for i in range(n_pair) if 0 <= i + step < n_pair]

    def struct(shape, dtype=BF16):
        return jax.ShapeDtypeStruct(shape, dtype)

    def row_of(vector):
        return vector.reshape(1, channels)

    pair, core = lax.axis_index("pair"), lax.axis_index("core")
    owner = lax.axis_index("frame")
    my_count = lax.dynamic_index_in_dim(frame_counts, owner, keepdims=False)
    index = jnp.stack([pair, core, my_count]).astype(jnp.int32)

    picked = pl.pallas_call(
        functools.partial(pick_body, 2, frames_each),
        out_shape=struct((n_frame * 2, slots, rows * columns, channels)),
        in_specs=[SMEM, VMEM],
        out_specs=VMEM,
        compiler_params=params,
        name="pick",
    )(frame_counts, video.reshape(frames, rows * columns, channels))
    parts = lax.all_to_all(picked, ("frame", "core"), split_axis=0, concat_axis=0)

    if first_weight.shape[0] % 16 == 0 and n_pair > 2:
        own_weights = jnp.concatenate([first_weight, second_weight], axis=0)
        same = jnp.stack(
            [own_weights]
            + [lax.ppermute(own_weights, "pair", ring(step)) for step in range(1, n_pair)]
        )
        other = lax.ppermute(same, "core", [(0, 1), (1, 0)])
    else:
        both = (first_weight, second_weight)
        same = jnp.stack([lax.all_gather(w, ("pair", "core"), tiled=True) for w in both])
        other = jnp.zeros((16, channels), BF16)

    by_place = parts.reshape(n_frame, 2, slots, rows, columns, channels)

    def edge_row(array):
        return array.transpose(1, 0, 2, 3).reshape(slots, width, channels)

    above = lax.ppermute(edge_row(by_place[:, 1, :, rows - 1]), "pair", line(1))
    below = lax.ppermute(edge_row(by_place[:, 0, :, 0]), "pair", line(-1))

    total = pl.pallas_call(
        functools.partial(temporal_body, 2, rows),
        out_shape=struct((frames_each, all_rows, width, channels), F32),
        in_specs=[VMEM] * 3,
        out_specs=VMEM,
        scratch_shapes=[pltpu.VMEM((slots, all_rows, width, 3 * channels), BF16)],
        compiler_params=params,
        name="temporal",
    )(parts, temporal_weight, row_of(temporal_bias))

    field = struct((frames_each, all_rows, width, channels))
    message = struct((edge + 3 * span, channels))
    stats_struct = struct((3 * span, channels))

    blended, down, up, stats = pl.pallas_call(
        functools.partial(borders_body, n_pair),
        out_shape=(field, message, message, stats_struct),
        in_specs=[VMEM] * 4,
        out_specs=(VMEM,) * 4,
        scratch_shapes=[pltpu.VMEM((2, slots, width, 3 * channels), BF16)],
        compiler_params=params,
        name="borders",
    )(total, above, below, temporal_weight)

    def exchange(down, up, stats):
        from_above = lax.ppermute(down, "pair", ring(1))
        from_below = lax.ppermute(up, "pair", ring(-1))
        others = [lax.ppermute(stats, "pair", ring(step)) for step in range(2, n_pair - 1)]
        return from_above, from_below, others

    def scratch():
        return [
            pltpu.VMEM((frames_each, all_rows + 2, width, 3 * channels), BF16),
            pltpu.VMEM((9 * channels, channels), BF16),
            pltpu.VMEM((frames_each, 1, channels), F32),
            pltpu.VMEM((frames_each, 1, channels), F32),
        ]

    from_above, from_below, others = exchange(down, up, stats)
    first_out, down, up, stats = pl.pallas_call(
        functools.partial(first_body, n_pair, len(others)),
        out_shape=(field, message, message, stats_struct),
        in_specs=[SMEM] + [VMEM] * (9 + len(others)),
        out_specs=(VMEM,) * 4,
        scratch_shapes=scratch(),
        compiler_params=params,
        name="first",
    )(
        index, blended, from_above, from_below, stats, *others, same, other,
        row_of(first_gain), row_of(first_shift), row_of(first_bias),
    )

    from_above, from_below, others = exchange(down, up, stats)
    half = struct((frames_each, rows, width, channels))
    kept, sent = pl.pallas_call(
        functools.partial(second_body, n_pair, len(others)),
        out_shape=(half, half),
        in_specs=[SMEM] + [VMEM] * (10 + len(others)),
        out_specs=(VMEM,) * 2,
        scratch_shapes=scratch() + [pltpu.VMEM(field.shape, BF16)],
        compiler_params=params,
        name="second",
    )(
        index, first_out, from_above, from_below, stats, *others, same, other,
        row_of(second_gain), row_of(second_shift), row_of(second_bias), blended,
    )
    received = lax.ppermute(sent, "core", [(0, 1), (1, 0)])
    early = jnp.where(core == 0, kept, received)
    late = jnp.where(core == 0, received, kept)
    return jnp.concatenate([early, late], axis=0)[:capacity]


def per_device(video, *rest):
    frames, n_frame = video.shape[0], lax.axis_size("frame")
    n_height = lax.axis_size("pair") * lax.axis_size("core")
    capacity = slots_of(frames, n_frame)
    each, extra = divmod(capacity, n_height)
    room = each * (n_height - 2)
    n_pair = lax.axis_size("pair")
    fits = each > 0 and extra <= 2 * each and n_frame > 1 and n_pair > 1
    fits = fits and n_pair & (n_pair - 1) == 0
    if fits and 2 * (each * n_height + 1) > frames and frames - capacity < n_frame * room:
        return whole_frames(video, *rest)
    return split_rows(video, *rest)


def solution(mesh):
    n_frame, n_height = mesh.devices.shape
    split = Mesh(mesh.devices.reshape(n_frame, n_height // 2, 2), ("frame", "pair", "core"))
    height = ("pair", "core")
    placed = (
        P(None, height, "frame", None),
        P(),
        P(),
        P(),
        P(),
        P(),
        P(height, None),
        P(),
        P(),
        P(),
        P(height, None),
        P(),
    )
    return jax.shard_map(
        per_device,
        mesh=split,
        in_specs=placed,
        out_specs=P("frame", height, None, None),
        check_vma=False,
    )
```

```python
import functools
import itertools

import jax
import jax.numpy as jnp
from jax import lax
from jax.experimental import pallas as pl
from jax.experimental.pallas import tpu as pltpu
from jax.sharding import Mesh, PartitionSpec as P

GROUPS = 32
EPS = 1e-06
VMEM = pl.BlockSpec(memory_space=pltpu.VMEM)
SMEM = pl.BlockSpec(memory_space=pltpu.SMEM)
HBM = pl.BlockSpec(memory_space=pl.ANY)
F32, BF16 = jnp.float32, jnp.bfloat16


def up_to(number, multiple):
    return -(-number // multiple) * multiple


def slots_of(frames, n_frame):
    return min(2 * ((frames + n_frame - 1) // n_frame), frames - n_frame + 1)


def silu(values):
    half = 0.5 * values
    return half + half * jnp.tanh(half)


def with_column_taps(values):
    axis, width = values.ndim - 2, values.shape[-2]
    column = lax.broadcasted_iota(jnp.int32, values.shape, axis)
    before = jnp.where(column == 0, 0.0, pltpu.roll(values, 1, axis))
    after = jnp.where(column == width - 1, 0.0, pltpu.roll(values, width - 1, axis))
    return jnp.concatenate([before.astype(BF16), values.astype(BF16), after.astype(BF16)], axis=-1)


def frame_offset(counts_ref, owner):
    offset = jnp.int32(0)
    for index in range(counts_ref.shape[0]):
        offset = offset + jnp.where(index < owner, counts_ref[index], 0)
    return offset


def pick_body(halves, frames_each, counts_ref, video_ref, out_ref):
    frames = video_ref.shape[0]
    slots = out_ref.shape[1]
    for owner in range(counts_ref.shape[0]):
        offset = frame_offset(counts_ref, owner)
        for half in range(halves):
            for slot in range(slots):
                frame = offset + (half * frames_each + slot - 2)
                values = video_ref[jnp.clip(frame, 0, frames - 1)]
                out_ref[owner * halves + half, slot] = jnp.where(
                    frame >= 0, values, jnp.zeros_like(values)
                )


def temporal_body(halves, rows, part_ref, weight_ref, bias_ref, total_ref, taps_ref):
    peers, slots, cells, channels = part_ref.shape
    columns = cells // rows
    frames_each, all_rows, width = total_ref.shape[:3]

    def place(slot, _):
        for half in range(halves):
            for row in range(rows):
                values = jnp.concatenate(
                    [
                        part_ref[peer * halves + half, slot].astype(F32)[
                            row * columns : (row + 1) * columns
                        ]
                        for peer in range(peers // halves)
                    ],
                    axis=0,
                )
                at = half * rows + row
                taps_ref[slot, at] = with_column_taps(silu(values))

                @pl.when(slot >= 2)
                def _():
                    total_ref[slot - 2, at] = values + bias_ref[...]

        return 0

    lax.fori_loop(0, slots, place, 0)
    depth = 3 * channels
    for row_tap in range(3):
        low, high = max(0, 1 - row_tap), min(all_rows, all_rows + 1 - row_tap)
        for time_tap in range(3):
            patches = taps_ref[
                time_tap : time_tap + frames_each, low + row_tap - 1 : high + row_tap - 1
            ]
            start = (time_tap * 3 + row_tap) * depth
            product = jnp.dot(
                patches.reshape(frames_each * (high - low) * width, depth),
                weight_ref[start : start + depth],
                preferred_element_type=F32,
            )
            total_ref[:, low:high] += product.reshape(frames_each, high - low, width, channels)


def write_stats(field_ref, stats_ref):
    frames_each, rows, width, channels = field_ref.shape
    span = stats_ref.shape[0] // 3
    sums, squares = [], []
    for frame in range(frames_each):
        values = field_ref[frame].astype(F32).reshape(rows * width, channels)
        part_sum = jnp.sum(values, axis=0, keepdims=True)
        centered = values - part_sum * (1.0 / (rows * width))
        sums.append(part_sum)
        squares.append(jnp.sum(centered * centered, axis=0, keepdims=True))
    pad = [jnp.zeros((span - 2 * frames_each, channels), F32)] if span > 2 * frames_each else []
    rest = jnp.concatenate(sums + squares + pad, axis=0)
    for piece in range(3):
        rounded = rest.astype(BF16)
        stats_ref[piece * span : (piece + 1) * span] = rounded
        rest = rest - rounded.astype(F32)


def write_messages(field_ref, down_ref, up_ref, stats_ref):
    frames_each, rows, width, channels = field_ref.shape
    write_stats(field_ref, stats_ref)
    edge = frames_each * width
    down_ref[:edge] = field_ref[:, rows - 1].reshape(edge, channels)
    up_ref[:edge] = field_ref[:, 0].reshape(edge, channels)
    down_ref[edge:] = stats_ref[...]
    up_ref[edge:] = stats_ref[...]


def borders_body(
    n_pair,
    total_ref,
    above_ref,
    below_ref,
    weight_ref,
    blended_ref,
    down_ref,
    up_ref,
    stats_ref,
    taps_ref,
):
    frames_each, rows, width, channels = total_ref.shape
    slots = above_ref.shape[0]
    depth = 3 * channels

    def place(slot, _):
        taps_ref[0, slot] = with_column_taps(silu(above_ref[slot].astype(F32)))
        taps_ref[1, slot] = with_column_taps(silu(below_ref[slot].astype(F32)))
        return 0

    lax.fori_loop(0, slots, place, 0)
    for side, row, row_tap in ((0, 0, 0), (1, rows - 1, 2)):
        summed = total_ref[:, row].reshape(frames_each * width, channels)
        for time_tap in range(3):
            patches = taps_ref[side, time_tap : time_tap + frames_each]
            start = (time_tap * 3 + row_tap) * depth
            summed = summed + jnp.dot(
                patches.reshape(frames_each * width, depth),
                weight_ref[start : start + depth],
                preferred_element_type=F32,
            )
        blended_ref[:, row] = summed.reshape(frames_each, width, channels).astype(BF16)
    blended_ref[:, 1 : rows - 1] = total_ref[:, 1 : rows - 1].astype(BF16)
    write_messages(blended_ref, down_ref, up_ref, stats_ref)


def group_total(values, width_group):
    lane = lax.broadcasted_iota(jnp.int32, values.shape, 1)
    size, step = values.shape[1], 1
    while step < width_group:
        upper = (lane // step) % 2 == 1
        values = values + jnp.where(
            upper, pltpu.roll(values, step, 1), pltpu.roll(values, size - step, 1)
        )
        step *= 2
    return values


def scale_and_offset(frames_each, cells, stats, gain_ref, shift_ref):
    channels = stats[0].shape[1]
    width_group = channels // GROUPS
    span = stats[0].shape[0] // 3
    parts = []
    for packed in stats:
        pieces = [packed[i * span : (i + 1) * span].astype(F32) for i in range(3)]
        parts.append(pieces[0] + (pieces[1] + pieces[2]))
    sums = [part[:frames_each] for part in parts]
    squares = [part[frames_each : 2 * frames_each] for part in parts]
    sample = float(cells * len(parts) * width_group)
    mean = group_total(functools.reduce(jnp.add, sums), width_group) * (1.0 / sample)
    spread = functools.reduce(jnp.add, squares)
    for part_sum in sums:
        apart = part_sum * (1.0 / cells) - mean
        spread = spread + float(cells) * apart * apart
    variance = group_total(spread, width_group) * (1.0 / sample)
    scale = lax.rsqrt(variance + EPS) * gain_ref[...]
    return scale, shift_ref[...] - mean * scale


def normed_taps(
    n_pair, index_ref, field_ref, above_ref, below_ref, stats, gain_ref, shift_ref, taps_ref,
    scale_ref, offset_ref,
):
    frames_each, rows, width, channels = field_ref.shape
    scale, offset = scale_and_offset(frames_each, rows * width, stats, gain_ref, shift_ref)
    for frame in range(frames_each):
        scale_ref[frame] = scale[frame : frame + 1]
        offset_ref[frame] = offset[frame : frame + 1]
    pair = index_ref[0]
    top = jnp.where(pair > 0, 1.0, 0.0)
    bottom = jnp.where(pair < n_pair - 1, 1.0, 0.0)

    def place(frame, _):
        scale_row, offset_row = scale_ref[frame], offset_ref[frame]
        for row in range(rows):
            values = field_ref[frame, row].astype(F32) * scale_row + offset_row
            taps_ref[frame, row + 1] = with_column_taps(silu(values))
        edge = pl.ds(pl.multiple_of(frame * width, width), width)
        values = silu(above_ref[edge].astype(F32) * scale_row + offset_row) * top
        taps_ref[frame, 0] = with_column_taps(values)
        values = silu(below_ref[edge].astype(F32) * scale_row + offset_row) * bottom
        taps_ref[frame, rows + 1] = with_column_taps(values)
        return 0

    lax.fori_loop(0, frames_each, place, 0)


def gather_weight(n_pair, which, index_ref, same_ref, other_ref, weight_ref):
    depth = weight_ref.shape[0] // (2 * n_pair)
    if same_ref.shape[0] != n_pair:
        weight_ref[...] = same_ref[which]
        return
    pair, core = index_ref[0], index_ref[1]
    for step in range(n_pair):
        source = lax.rem(pair - step + n_pair, n_pair)
        for parts_ref, of_core in ((same_ref, core), (other_ref, 1 - core)):
            shard = source * 2 + of_core
            rows = pl.ds(pl.multiple_of(shard * depth, depth), depth)
            weight_ref[rows] = parts_ref[step, which * depth : (which + 1) * depth]


def convolved(rows, row, taps_ref, weight_ref):
    frames_each, _, width, depth = taps_ref.shape
    summed = None
    for row_tap in range(3):
        patches = taps_ref[:, row + row_tap : row + row_tap + rows]
        product = jnp.dot(
            patches.reshape(frames_each * rows * width, depth),
            weight_ref[row_tap * depth : (row_tap + 1) * depth],
            preferred_element_type=F32,
        )
        summed = product if summed is None else summed + product
    return summed


def first_body(
    n_pair,
    n_others,
    index_ref,
    blended_ref,
    from_above_ref,
    from_below_ref,
    own_ref,
    *refs,
):
    others, refs = refs[:n_others], refs[n_others:]
    (
        same_ref, other_ref, gain_ref, shift_ref, bias_ref,
        out_ref, down_ref, up_ref, stats_ref,
        taps_ref, weight_ref, scale_ref, offset_ref,
    ) = refs
    frames_each, rows, width, channels = blended_ref.shape
    edge = frames_each * width
    stats = [own_ref[...], from_above_ref[edge:]]
    if n_pair > 2:
        stats.append(from_below_ref[edge:])
    stats = stats + [ref[...] for ref in others]
    normed_taps(
        n_pair, index_ref, blended_ref, from_above_ref, from_below_ref, stats,
        gain_ref, shift_ref, taps_ref, scale_ref, offset_ref,
    )
    gather_weight(n_pair, 0, index_ref, same_ref, other_ref, weight_ref)
    summed = convolved(rows, 0, taps_ref, weight_ref) + bias_ref[...]
    out_ref[...] = summed.astype(BF16).reshape(frames_each, rows, width, channels)
    write_messages(out_ref, down_ref, up_ref, stats_ref)


def second_body(
    n_pair,
    n_others,
    index_ref,
    field_ref,
    from_above_ref,
    from_below_ref,
    own_ref,
    *refs,
):
    others, refs = refs[:n_others], refs[n_others:]
    (
        same_ref, other_ref, gain_ref, shift_ref, bias_ref, blended_ref,
        kept_ref, sent_ref,
        taps_ref, weight_ref, scale_ref, offset_ref, whole_ref,
    ) = refs
    frames_each, rows, width, channels = field_ref.shape
    edge = frames_each * width
    stats = [own_ref[...], from_above_ref[edge:]]
    if n_pair > 2:
        stats.append(from_below_ref[edge:])
    stats = stats + [ref[...] for ref in others]
    normed_taps(
        n_pair, index_ref, field_ref, from_above_ref, from_below_ref, stats,
        gain_ref, shift_ref, taps_ref, scale_ref, offset_ref,
    )
    gather_weight(n_pair, 1, index_ref, same_ref, other_ref, weight_ref)
    core, count = index_ref[1], index_ref[2]
    summed = convolved(rows, 0, taps_ref, weight_ref) + bias_ref[...]
    summed = summed.reshape(frames_each, rows, width, channels) + blended_ref[...].astype(F32)
    half = rows // 2
    for frame in range(frames_each):
        live = core * frames_each + frame < count
        whole_ref[frame] = jnp.where(live, summed[frame], 0.0).astype(BF16)
    kept_ref[...] = whole_ref[:, pl.ds(core * half, half)]
    sent_ref[...] = whole_ref[:, pl.ds((1 - core) * half, half)]


def most_and_helper(counts, n_owner, room):
    most, high = jnp.int32(0), counts[0]
    for owner in range(1, n_owner):
        count = counts[owner]
        most, high = jnp.where(count > high, owner, most), jnp.maximum(count, high)
    helper, near = jnp.int32(0), jnp.int32(2 * n_owner)
    for owner in range(n_owner):
        away = jnp.where((counts[owner] > room) | (most == owner), 2 * n_owner, jnp.abs(most - owner))
        helper, near = jnp.where(away < near, owner, helper), jnp.minimum(away, near)
    return most, helper


def pick_frames_body(
    capacity, given_ref, video_ref, out_ref, held_ref, placed_ref, counts_ref, load_sems, sems
):
    read = pltpu.make_async_copy(given_ref, counts_ref, load_sems.at[0])
    load = pltpu.make_async_copy(video_ref, held_ref, load_sems.at[1])
    read.start()
    load.start()
    read.wait()
    frames, (parts, sent) = video_ref.shape[0], out_ref.shape[:2]
    n_owner = counts_ref.shape[0]
    span, each = parts // n_owner, sent - 1
    most, least = most_and_helper(counts_ref, n_owner, each * (span - 2))
    last = frame_offset(counts_ref, most) + (capacity - 2 * each)
    load.wait()
    copies = []
    for owner in range(n_owner):
        offset = frame_offset(counts_ref, owner)
        for part in range(span):
            pair, core = part // 2, part % 2
            base = offset + 2 * each * pair
            if pair == span // 2 - 1:
                base = jnp.where(least == owner, last, base)
            for place in range(sent):
                frame = base + (2 * each - 1 - place if core else place - 2)
                values = held_ref[jnp.clip(frame, 0, frames - 1)]
                if not core and place < 2:
                    values = jnp.where(frame >= 0, values, jnp.zeros_like(values))
                placed_ref[owner * span + part, place] = values
        rows = pl.ds(owner * span, span)
        copies.append(
            pltpu.make_async_copy(placed_ref.at[rows], out_ref.at[rows], sems.at[owner])
        )
        copies[-1].start()
    for copy in copies:
        copy.wait()


def group_spread(values, width_group):
    lane = lax.broadcasted_iota(jnp.int32, values.shape, 1) % width_group
    size, total = values.shape[1], values
    for step in range(1, width_group):
        total = total + jnp.where(
            lane >= step,
            pltpu.roll(values, step, 1),
            pltpu.roll(values, size - width_group + step, 1),
        )
    return total


def interleave(main, side, pace):
    for _ in main:
        for _ in range(pace):
            next(side, None)
    for _ in side:
        pass


def dot_pieces(source_ref, weight_ref, total_ref, add, parts=2):
    rows, width, depth = source_ref.shape
    part_rows = (rows - 2) // parts
    cells = part_rows * width
    for part in range(parts):
        summed = None
        for row_tap in range(3):
            low = part * part_rows + row_tap
            product = jnp.dot(
                source_ref[low : low + part_rows].reshape(cells, depth),
                weight_ref[row_tap * depth : (row_tap + 1) * depth],
                preferred_element_type=F32,
            )
            summed = product if summed is None else summed + product
            yield
        if add:
            total_ref[part * cells : (part + 1) * cells] += summed
        else:
            total_ref[part * cells : (part + 1) * cells] = summed


def norm_pieces(field_ref, normed_ref, row_of, gain, shift):
    all_rows, width, channels = field_ref.shape
    cells, width_group = all_rows * width, channels // GROUPS
    pivot = None
    sums = squares = jnp.zeros((8, channels), F32)
    for row in range(all_rows):
        if row_of is None:
            values = field_ref[row].astype(F32)
        else:
            rounded = row_of(row).astype(BF16)
            field_ref[row] = rounded
            values = rounded.astype(F32)
        if pivot is None:
            pivot = values[:1]
        apart = (values - pivot).reshape(width // 8, 8, channels)
        sums = sums + jnp.sum(apart, axis=0)
        squares = squares + jnp.sum(apart * apart, axis=0)
        if row % 4 == 3:
            yield
    own = jnp.sum(sums, axis=0, keepdims=True) * (1.0 / cells)
    squares = jnp.sum(squares, axis=0, keepdims=True) * (1.0 / cells)
    sample = 1.0 / width_group
    mean = group_spread(own + pivot, width_group) * sample
    off = own + pivot - mean
    spread = squares - own * own + off * off
    variance = jnp.maximum(group_spread(spread, width_group) * sample, 0.0)
    scale = lax.rsqrt(variance + EPS) * gain
    offset = 0.5 * (shift - mean * scale)
    scale = 0.5 * scale
    yield
    for row in range(all_rows):
        half = field_ref[row].astype(F32) * scale + offset
        normed_ref[row + 1] = with_column_taps(half + half * jnp.tanh(half))
        if row % 2 == 1:
            yield


def clear_borders(refs):
    for ref in refs:
        border = jnp.zeros(ref.shape[1:], BF16)
        ref[0] = border
        ref[ref.shape[0] - 1] = border


def start_all(copies):
    for copy in copies:
        copy.start()


def wait_all(copies):
    for copy in copies:
        copy.wait()


def frames_body(n_height, part_ref, swapped_ref, temporal_ref, bias_ref, gain_ref, shift_ref, *refs):
    normed_out_ref, blended_out_ref, order_ref, *refs = refs
    order_ref[...] = jnp.zeros_like(order_ref)
    each, all_rows, width, channels = blended_out_ref.shape
    places = each + 2
    taps_refs, refs = refs[:places], refs[places:]
    total_refs, refs = refs[:each], refs[each:]
    raw_ref, time_ref, time_sems = refs
    n_frame = part_ref.shape[0] // n_height
    columns, rows = width // n_frame, all_rows // n_height
    depth = 3 * channels
    core = lax.axis_index("core")

    time_copies = []
    for step in range(3):
        tap = step + core * (2 - 2 * step)
        begin = pl.multiple_of(tap * 3 * depth, 3 * depth)
        time_copies.append(
            pltpu.make_async_copy(
                temporal_ref.at[pl.ds(begin, 3 * depth)], time_ref.at[step], time_sems.at[step]
            )
        )
    start_all(time_copies)
    normed_refs = [normed_out_ref.at[place] for place in range(each - 1)]
    clear_borders(list(taps_refs) + normed_refs)

    def piece_of(place, source):
        return part_ref[source, place] if place <= each else swapped_ref[source]

    def lay(place):
        for height in range(n_height):
            pieces = [
                piece_of(place, peer * n_height + height).astype(F32) for peer in range(n_frame)
            ]
            for row in range(rows):
                values = jnp.concatenate(
                    [piece[row * columns : (row + 1) * columns] for piece in pieces], axis=0
                )
                raw_ref[place, height * rows + row] = values.astype(BF16)
                taps_refs[place][height * rows + row + 1] = with_column_taps(silu(values))
            yield

    def temporal(place, step):
        if place == 0:
            time_copies[step].wait()
        return dot_pieces(taps_refs[place + step], time_ref.at[step], total_refs[place], step > 0)

    def blended_row(place):
        raw_at = place + 2 - 2 * core

        def row_of(row):
            product = total_refs[place][row * width : (row + 1) * width]
            return raw_ref[raw_at, row].astype(F32) + product + bias_ref[...]

        return row_of

    nothing = iter(())
    for place in range(3):
        interleave(lay(place), nothing, 0)
    rest = itertools.chain.from_iterable(lay(place) for place in range(3, places))
    pieces = itertools.chain.from_iterable(temporal(0, step) for step in range(3))
    interleave(pieces, rest, 1)
    for place in range(1, each):
        norm = norm_pieces(
            blended_out_ref.at[place - 1], normed_refs[place - 1], blended_row(place - 1),
            gain_ref[...], shift_ref[...],
        )
        pieces = itertools.chain.from_iterable(temporal(place, step) for step in range(3))
        interleave(pieces, norm, 1)
    row_of = blended_row(each - 1)
    for row in range(all_rows):
        blended_out_ref[each - 1, row] = row_of(row).astype(BF16)


def spatial_body(n_pair, normed_ref, blended_ref, order_ref, *refs):
    same_refs, refs = refs[:n_pair], refs[n_pair:]
    other_refs, refs = refs[:n_pair], refs[n_pair:]
    gain_ref, shift_ref, first_bias_ref, second_gain_ref, second_shift_ref, *refs = refs
    second_bias_ref, out_ref, *refs = refs
    n_height, each, rows, width, channels = out_ref.shape
    all_rows = n_height * rows
    normed_refs, refs = refs[:each], refs[each:]
    total_refs, refs = refs[:each], refs[each:]
    field_refs, refs = refs[:each], refs[each:]
    weights_ref, done_ref, out_sems = refs
    pair, core = lax.axis_index("pair"), lax.axis_index("core")
    span = same_refs[0].shape[1]

    def gather(which):
        for step in range(n_pair):
            for shard_ref, of_core in ((same_refs[step], core), (other_refs[step], 1 - core)):
                source = jnp.bitwise_xor(pair, step) * 2 + of_core
                begin = pl.multiple_of(source * span, span)
                weights_ref[which, pl.ds(begin, span)] = shard_ref[which]
                yield

    clear_borders(normed_refs)

    def first_source(place):
        return normed_ref.at[place] if place < each - 1 else normed_refs[place]

    def second_norm(place):
        def row_of(row):
            return total_refs[place][row * width : (row + 1) * width] + first_bias_ref[...]

        return norm_pieces(
            field_refs[place], normed_refs[place], row_of, second_gain_ref[...],
            second_shift_ref[...],
        )

    def finish(place):
        at = place + core * (each - 1 - 2 * place)
        for row in range(all_rows):
            product = total_refs[place][row * width : (row + 1) * width] + second_bias_ref[...]
            decoded = blended_ref[place, row].astype(F32) + product
            done_ref[place, row // rows, row % rows] = decoded.astype(BF16)
            if row % 4 == 3:
                yield
        stores.append(
            pltpu.make_async_copy(done_ref.at[place], out_ref.at[:, at], out_sems.at[place])
        )
        stores[-1].start()

    stores = []
    pending = norm_pieces(
        blended_ref.at[each - 1], normed_refs[each - 1], None, gain_ref[...], shift_ref[...]
    )
    interleave(gather(0), pending, 1)
    pending = gather(1)
    for place in range(each):
        interleave(
            dot_pieces(first_source(place), weights_ref.at[0], total_refs[place], False),
            pending, 3,
        )
        pending = second_norm(place)
    for place in range(each):
        interleave(
            dot_pieces(normed_refs[place], weights_ref.at[1], total_refs[place], False),
            pending, 3,
        )
        pending = finish(place)
    interleave(pending, iter(()), 0)
    wait_all(stores)


def route_body(room, counts_ref, route_ref):
    n_owner = counts_ref.shape[0]
    most, helper = most_and_helper(counts_ref, n_owner, room)
    route_ref[0] = most * n_owner + helper


def place_body(counts_ref, owned_ref, extra_ref, out_ref):
    count, n_owned = counts_ref[lax.axis_index("frame")], owned_ref.shape[0]
    for slot in range(out_ref.shape[0]):
        values = owned_ref[slot] if slot < n_owned else extra_ref[slot - n_owned]
        out_ref[slot] = jnp.where(slot < count, values, jnp.zeros_like(values))


def partners(size, step):
    return [(i, i ^ step) for i in range(size)]


def whole_frames(
    video, frame_counts, temporal_weight, temporal_bias, first_gain, first_shift, first_weight,
    first_bias, second_gain, second_shift, second_weight, second_bias,
):
    frames, rows, columns, channels = video.shape
    n_frame, n_pair = lax.axis_size("frame"), lax.axis_size("pair")
    n_height = 2 * n_pair
    width = columns * n_frame
    all_rows = rows * n_height
    capacity = slots_of(frames, n_frame)
    each = capacity // n_height
    extra = capacity - each * n_height
    params = pltpu.CompilerParams(vmem_limit_bytes=60 * 1024 * 1024)
    swap = [(0, 1), (1, 0)]

    picked = pl.pallas_call(
        functools.partial(pick_frames_body, capacity),
        out_shape=jax.ShapeDtypeStruct(
            (n_frame * n_height, each + 1, rows * columns, channels), BF16
        ),
        in_specs=[HBM, HBM],
        out_specs=HBM,
        scratch_shapes=[
            pltpu.VMEM((frames, rows * columns, channels), BF16),
            pltpu.VMEM((n_frame * n_height, each + 1, rows * columns, channels), BF16),
            pltpu.SMEM(frame_counts.shape, jnp.int32),
            pltpu.SemaphoreType.DMA((2,)),
            pltpu.SemaphoreType.DMA((n_frame,)),
        ],
        compiler_params=params,
        name="pick",
    )(frame_counts, video.reshape(frames, rows * columns, channels))
    parts = lax.all_to_all(picked, ("frame", "pair", "core"), split_axis=0, concat_axis=0)
    swapped = lax.ppermute(parts[:, each], "core", swap)

    own = jnp.stack([first_weight, second_weight])
    same = [own] + [
        lax.ppermute(own, "pair", partners(n_pair, step)) for step in range(1, n_pair)
    ]

    def row_of(vector):
        return vector.reshape(1, channels)

    field = (all_rows, width, channels)
    taps = (all_rows + 2, width, 3 * channels)
    total = pltpu.VMEM((all_rows * width, channels), F32)
    limit = pltpu.CompilerParams(vmem_limit_bytes=50 * 1024 * 1024)
    normed, blended, order = pl.pallas_call(
        functools.partial(frames_body, n_height),
        out_shape=(
            jax.ShapeDtypeStruct((max(each - 1, 1),) + taps, BF16),
            jax.ShapeDtypeStruct((each,) + field, BF16),
            jax.ShapeDtypeStruct((8, 128), F32),
        ),
        in_specs=[VMEM, VMEM, HBM] + [VMEM] * 3,
        out_specs=(VMEM,) * 3,
        scratch_shapes=[pltpu.VMEM(taps, BF16)] * (each + 2)
        + [total] * each
        + [
            pltpu.VMEM((each + 2,) + field, BF16),
            pltpu.VMEM((3, 9 * channels, channels), BF16),
            pltpu.SemaphoreType.DMA((3,)),
        ],
        compiler_params=limit,
        name="frames",
    )(
        parts, swapped, temporal_weight,
        row_of(temporal_bias), row_of(first_gain), row_of(first_shift),
    )
    same[1:], order = lax.optimization_barrier((same[1:], order))
    other = [lax.ppermute(shard, "core", swap) for shard in same]
    decoded = pl.pallas_call(
        functools.partial(spatial_body, n_pair),
        out_shape=jax.ShapeDtypeStruct((n_height, each, rows, width, channels), BF16),
        in_specs=[VMEM] * (9 + 2 * n_pair),
        out_specs=HBM,
        scratch_shapes=[pltpu.VMEM(taps, BF16)] * each
        + [total] * each
        + [pltpu.VMEM(field, BF16)] * each
        + [
            pltpu.VMEM((2, 9 * channels, channels), BF16),
            pltpu.VMEM((each, n_height, rows, width, channels), BF16),
            pltpu.SemaphoreType.DMA((each,)),
        ],
        compiler_params=pltpu.CompilerParams(vmem_limit_bytes=20 * 1024 * 1024),
        name="spatial",
    )(
        normed, blended, order, *same, *other,
        row_of(first_gain), row_of(first_shift), row_of(first_bias),
        row_of(second_gain), row_of(second_shift), row_of(second_bias),
    )
    owned = lax.all_to_all(decoded, ("pair", "core"), split_axis=0, concat_axis=0)
    owned = owned.reshape((n_height * each,) + owned.shape[2:])
    if extra:
        route = pl.pallas_call(
            functools.partial(route_body, each * (n_height - 2)),
            out_shape=jax.ShapeDtypeStruct((1,), jnp.int32),
            in_specs=[SMEM],
            out_specs=SMEM,
            name="route",
        )(frame_counts)

        def homeward(pairing):
            source, target = pairing % n_frame, pairing // n_frame
            if source == target:
                return jnp.zeros_like
            return lambda rows: lax.ppermute(rows, "frame", [(source, target)])

        late = lax.switch(
            route[0],
            [homeward(pairing) for pairing in range(n_frame * n_frame)],
            owned[-extra:],
        )
    else:
        late = owned[:1]
    return pl.pallas_call(
        place_body,
        out_shape=jax.ShapeDtypeStruct((capacity,) + owned.shape[1:], BF16),
        in_specs=[SMEM, VMEM, VMEM],
        out_specs=VMEM,
        compiler_params=pltpu.CompilerParams(vmem_limit_bytes=20 * 1024 * 1024),
        name="place",
    )(frame_counts, owned, late)


def split_rows(
    video,
    frame_counts,
    temporal_weight,
    temporal_bias,
    first_gain,
    first_shift,
    first_weight,
    first_bias,
    second_gain,
    second_shift,
    second_weight,
    second_bias,
):
    frames, rows, columns, channels = video.shape
    n_frame, n_pair = lax.axis_size("frame"), lax.axis_size("pair")
    width = columns * n_frame
    capacity = slots_of(frames, n_frame)
    frames_each = up_to(capacity, 2) // 2
    slots = frames_each + 2
    all_rows = 2 * rows
    edge = frames_each * width
    span = up_to(2 * frames_each, 16)
    params = pltpu.CompilerParams(vmem_limit_bytes=20 * 1024 * 1024)

    def ring(step):
        return [(i, (i + step) % n_pair) for i in range(n_pair)]

    def line(step):
        return [(i, i + step) for i in range(n_pair) if 0 <= i + step < n_pair]

    def struct(shape, dtype=BF16):
        return jax.ShapeDtypeStruct(shape, dtype)

    def row_of(vector):
        return vector.reshape(1, channels)

    pair, core = lax.axis_index("pair"), lax.axis_index("core")
    owner = lax.axis_index("frame")
    my_count = lax.dynamic_index_in_dim(frame_counts, owner, keepdims=False)
    index = jnp.stack([pair, core, my_count]).astype(jnp.int32)

    picked = pl.pallas_call(
        functools.partial(pick_body, 2, frames_each),
        out_shape=struct((n_frame * 2, slots, rows * columns, channels)),
        in_specs=[SMEM, VMEM],
        out_specs=VMEM,
        compiler_params=params,
        name="pick",
    )(frame_counts, video.reshape(frames, rows * columns, channels))
    parts = lax.all_to_all(picked, ("frame", "core"), split_axis=0, concat_axis=0)

    if first_weight.shape[0] % 16 == 0 and n_pair > 2:
        own_weights = jnp.concatenate([first_weight, second_weight], axis=0)
        same = jnp.stack(
            [own_weights]
            + [lax.ppermute(own_weights, "pair", ring(step)) for step in range(1, n_pair)]
        )
        other = lax.ppermute(same, "core", [(0, 1), (1, 0)])
    else:
        both = (first_weight, second_weight)
        same = jnp.stack([lax.all_gather(w, ("pair", "core"), tiled=True) for w in both])
        other = jnp.zeros((16, channels), BF16)

    by_place = parts.reshape(n_frame, 2, slots, rows, columns, channels)

    def edge_row(array):
        return array.transpose(1, 0, 2, 3).reshape(slots, width, channels)

    above = lax.ppermute(edge_row(by_place[:, 1, :, rows - 1]), "pair", line(1))
    below = lax.ppermute(edge_row(by_place[:, 0, :, 0]), "pair", line(-1))

    total = pl.pallas_call(
        functools.partial(temporal_body, 2, rows),
        out_shape=struct((frames_each, all_rows, width, channels), F32),
        in_specs=[VMEM] * 3,
        out_specs=VMEM,
        scratch_shapes=[pltpu.VMEM((slots, all_rows, width, 3 * channels), BF16)],
        compiler_params=params,
        name="temporal",
    )(parts, temporal_weight, row_of(temporal_bias))

    field = struct((frames_each, all_rows, width, channels))
    message = struct((edge + 3 * span, channels))
    stats_struct = struct((3 * span, channels))

    blended, down, up, stats = pl.pallas_call(
        functools.partial(borders_body, n_pair),
        out_shape=(field, message, message, stats_struct),
        in_specs=[VMEM] * 4,
        out_specs=(VMEM,) * 4,
        scratch_shapes=[pltpu.VMEM((2, slots, width, 3 * channels), BF16)],
        compiler_params=params,
        name="borders",
    )(total, above, below, temporal_weight)

    def exchange(down, up, stats):
        from_above = lax.ppermute(down, "pair", ring(1))
        from_below = lax.ppermute(up, "pair", ring(-1))
        others = [lax.ppermute(stats, "pair", ring(step)) for step in range(2, n_pair - 1)]
        return from_above, from_below, others

    def scratch():
        return [
            pltpu.VMEM((frames_each, all_rows + 2, width, 3 * channels), BF16),
            pltpu.VMEM((9 * channels, channels), BF16),
            pltpu.VMEM((frames_each, 1, channels), F32),
            pltpu.VMEM((frames_each, 1, channels), F32),
        ]

    from_above, from_below, others = exchange(down, up, stats)
    first_out, down, up, stats = pl.pallas_call(
        functools.partial(first_body, n_pair, len(others)),
        out_shape=(field, message, message, stats_struct),
        in_specs=[SMEM] + [VMEM] * (9 + len(others)),
        out_specs=(VMEM,) * 4,
        scratch_shapes=scratch(),
        compiler_params=params,
        name="first",
    )(
        index, blended, from_above, from_below, stats, *others, same, other,
        row_of(first_gain), row_of(first_shift), row_of(first_bias),
    )

    from_above, from_below, others = exchange(down, up, stats)
    half = struct((frames_each, rows, width, channels))
    kept, sent = pl.pallas_call(
        functools.partial(second_body, n_pair, len(others)),
        out_shape=(half, half),
        in_specs=[SMEM] + [VMEM] * (10 + len(others)),
        out_specs=(VMEM,) * 2,
        scratch_shapes=scratch() + [pltpu.VMEM(field.shape, BF16)],
        compiler_params=params,
        name="second",
    )(
        index, first_out, from_above, from_below, stats, *others, same, other,
        row_of(second_gain), row_of(second_shift), row_of(second_bias), blended,
    )
    received = lax.ppermute(sent, "core", [(0, 1), (1, 0)])
    early = jnp.where(core == 0, kept, received)
    late = jnp.where(core == 0, received, kept)
    return jnp.concatenate([early, late], axis=0)[:capacity]


def per_device(video, *rest):
    frames, n_frame = video.shape[0], lax.axis_size("frame")
    n_height = lax.axis_size("pair") * lax.axis_size("core")
    capacity = slots_of(frames, n_frame)
    each, extra = divmod(capacity, n_height)
    room = each * (n_height - 2)
    n_pair = lax.axis_size("pair")
    fits = each > 0 and extra <= 2 * each and n_frame > 1 and n_pair > 1
    fits = fits and n_pair & (n_pair - 1) == 0
    if fits and 2 * (each * n_height + 1) > frames and frames - capacity < n_frame * room:
        return whole_frames(video, *rest)
    return split_rows(video, *rest)


def solution(mesh):
    n_frame, n_height = mesh.devices.shape
    split = Mesh(mesh.devices.reshape(n_frame, n_height // 2, 2), ("frame", "pair", "core"))
    height = ("pair", "core")
    placed = (
        P(None, height, "frame", None),
        P(),
        P(),
        P(),
        P(),
        P(),
        P(height, None),
        P(),
        P(),
        P(),
        P(height, None),
        P(),
    )
    return jax.shard_map(
        per_device,
        mesh=split,
        in_specs=placed,
        out_specs=P("frame", height, None, None),
        check_vma=False,
    )
```

```python
import functools
import itertools

import jax
import jax.numpy as jnp
from jax import lax
from jax.experimental import pallas as pl
from jax.experimental.pallas import tpu as pltpu
from jax.sharding import Mesh, PartitionSpec as P

GROUPS = 32
EPS = 1e-06
VMEM = pl.BlockSpec(memory_space=pltpu.VMEM)
SMEM = pl.BlockSpec(memory_space=pltpu.SMEM)
HBM = pl.BlockSpec(memory_space=pl.ANY)
F32, BF16 = jnp.float32, jnp.bfloat16


def up_to(number, multiple):
    return -(-number // multiple) * multiple


def slots_of(frames, n_frame):
    return min(2 * ((frames + n_frame - 1) // n_frame), frames - n_frame + 1)


def silu(values):
    half = 0.5 * values
    return half + half * jnp.tanh(half)


def with_column_taps(values):
    axis, width = values.ndim - 2, values.shape[-2]
    column = lax.broadcasted_iota(jnp.int32, values.shape, axis)
    before = jnp.where(column == 0, 0.0, pltpu.roll(values, 1, axis))
    after = jnp.where(column == width - 1, 0.0, pltpu.roll(values, width - 1, axis))
    return jnp.concatenate([before.astype(BF16), values.astype(BF16), after.astype(BF16)], axis=-1)


def frame_offset(counts_ref, owner):
    offset = jnp.int32(0)
    for index in range(counts_ref.shape[0]):
        offset = offset + jnp.where(index < owner, counts_ref[index], 0)
    return offset


def pick_body(halves, frames_each, counts_ref, video_ref, out_ref):
    frames = video_ref.shape[0]
    slots = out_ref.shape[1]
    for owner in range(counts_ref.shape[0]):
        offset = frame_offset(counts_ref, owner)
        for half in range(halves):
            for slot in range(slots):
                frame = offset + (half * frames_each + slot - 2)
                values = video_ref[jnp.clip(frame, 0, frames - 1)]
                out_ref[owner * halves + half, slot] = jnp.where(
                    frame >= 0, values, jnp.zeros_like(values)
                )


def temporal_body(halves, rows, part_ref, weight_ref, bias_ref, total_ref, taps_ref):
    peers, slots, cells, channels = part_ref.shape
    columns = cells // rows
    frames_each, all_rows, width = total_ref.shape[:3]

    def place(slot, _):
        for half in range(halves):
            for row in range(rows):
                values = jnp.concatenate(
                    [
                        part_ref[peer * halves + half, slot].astype(F32)[
                            row * columns : (row + 1) * columns
                        ]
                        for peer in range(peers // halves)
                    ],
                    axis=0,
                )
                at = half * rows + row
                taps_ref[slot, at] = with_column_taps(silu(values))

                @pl.when(slot >= 2)
                def _():
                    total_ref[slot - 2, at] = values + bias_ref[...]

        return 0

    lax.fori_loop(0, slots, place, 0)
    depth = 3 * channels
    for row_tap in range(3):
        low, high = max(0, 1 - row_tap), min(all_rows, all_rows + 1 - row_tap)
        for time_tap in range(3):
            patches = taps_ref[
                time_tap : time_tap + frames_each, low + row_tap - 1 : high + row_tap - 1
            ]
            start = (time_tap * 3 + row_tap) * depth
            product = jnp.dot(
                patches.reshape(frames_each * (high - low) * width, depth),
                weight_ref[start : start + depth],
                preferred_element_type=F32,
            )
            total_ref[:, low:high] += product.reshape(frames_each, high - low, width, channels)


def write_stats(field_ref, stats_ref):
    frames_each, rows, width, channels = field_ref.shape
    span = stats_ref.shape[0] // 3
    sums, squares = [], []
    for frame in range(frames_each):
        values = field_ref[frame].astype(F32).reshape(rows * width, channels)
        part_sum = jnp.sum(values, axis=0, keepdims=True)
        centered = values - part_sum * (1.0 / (rows * width))
        sums.append(part_sum)
        squares.append(jnp.sum(centered * centered, axis=0, keepdims=True))
    pad = [jnp.zeros((span - 2 * frames_each, channels), F32)] if span > 2 * frames_each else []
    rest = jnp.concatenate(sums + squares + pad, axis=0)
    for piece in range(3):
        rounded = rest.astype(BF16)
        stats_ref[piece * span : (piece + 1) * span] = rounded
        rest = rest - rounded.astype(F32)


def write_messages(field_ref, down_ref, up_ref, stats_ref):
    frames_each, rows, width, channels = field_ref.shape
    write_stats(field_ref, stats_ref)
    edge = frames_each * width
    down_ref[:edge] = field_ref[:, rows - 1].reshape(edge, channels)
    up_ref[:edge] = field_ref[:, 0].reshape(edge, channels)
    down_ref[edge:] = stats_ref[...]
    up_ref[edge:] = stats_ref[...]


def borders_body(
    n_pair,
    total_ref,
    above_ref,
    below_ref,
    weight_ref,
    blended_ref,
    down_ref,
    up_ref,
    stats_ref,
    taps_ref,
):
    frames_each, rows, width, channels = total_ref.shape
    slots = above_ref.shape[0]
    depth = 3 * channels

    def place(slot, _):
        taps_ref[0, slot] = with_column_taps(silu(above_ref[slot].astype(F32)))
        taps_ref[1, slot] = with_column_taps(silu(below_ref[slot].astype(F32)))
        return 0

    lax.fori_loop(0, slots, place, 0)
    for side, row, row_tap in ((0, 0, 0), (1, rows - 1, 2)):
        summed = total_ref[:, row].reshape(frames_each * width, channels)
        for time_tap in range(3):
            patches = taps_ref[side, time_tap : time_tap + frames_each]
            start = (time_tap * 3 + row_tap) * depth
            summed = summed + jnp.dot(
                patches.reshape(frames_each * width, depth),
                weight_ref[start : start + depth],
                preferred_element_type=F32,
            )
        blended_ref[:, row] = summed.reshape(frames_each, width, channels).astype(BF16)
    blended_ref[:, 1 : rows - 1] = total_ref[:, 1 : rows - 1].astype(BF16)
    write_messages(blended_ref, down_ref, up_ref, stats_ref)


def group_total(values, width_group):
    lane = lax.broadcasted_iota(jnp.int32, values.shape, 1)
    size, step = values.shape[1], 1
    while step < width_group:
        upper = (lane // step) % 2 == 1
        values = values + jnp.where(
            upper, pltpu.roll(values, step, 1), pltpu.roll(values, size - step, 1)
        )
        step *= 2
    return values


def scale_and_offset(frames_each, cells, stats, gain_ref, shift_ref):
    channels = stats[0].shape[1]
    width_group = channels // GROUPS
    span = stats[0].shape[0] // 3
    parts = []
    for packed in stats:
        pieces = [packed[i * span : (i + 1) * span].astype(F32) for i in range(3)]
        parts.append(pieces[0] + (pieces[1] + pieces[2]))
    sums = [part[:frames_each] for part in parts]
    squares = [part[frames_each : 2 * frames_each] for part in parts]
    sample = float(cells * len(parts) * width_group)
    mean = group_total(functools.reduce(jnp.add, sums), width_group) * (1.0 / sample)
    spread = functools.reduce(jnp.add, squares)
    for part_sum in sums:
        apart = part_sum * (1.0 / cells) - mean
        spread = spread + float(cells) * apart * apart
    variance = group_total(spread, width_group) * (1.0 / sample)
    scale = lax.rsqrt(variance + EPS) * gain_ref[...]
    return scale, shift_ref[...] - mean * scale


def normed_taps(
    n_pair, index_ref, field_ref, above_ref, below_ref, stats, gain_ref, shift_ref, taps_ref,
    scale_ref, offset_ref,
):
    frames_each, rows, width, channels = field_ref.shape
    scale, offset = scale_and_offset(frames_each, rows * width, stats, gain_ref, shift_ref)
    for frame in range(frames_each):
        scale_ref[frame] = scale[frame : frame + 1]
        offset_ref[frame] = offset[frame : frame + 1]
    pair = index_ref[0]
    top = jnp.where(pair > 0, 1.0, 0.0)
    bottom = jnp.where(pair < n_pair - 1, 1.0, 0.0)

    def place(frame, _):
        scale_row, offset_row = scale_ref[frame], offset_ref[frame]
        for row in range(rows):
            values = field_ref[frame, row].astype(F32) * scale_row + offset_row
            taps_ref[frame, row + 1] = with_column_taps(silu(values))
        edge = pl.ds(pl.multiple_of(frame * width, width), width)
        values = silu(above_ref[edge].astype(F32) * scale_row + offset_row) * top
        taps_ref[frame, 0] = with_column_taps(values)
        values = silu(below_ref[edge].astype(F32) * scale_row + offset_row) * bottom
        taps_ref[frame, rows + 1] = with_column_taps(values)
        return 0

    lax.fori_loop(0, frames_each, place, 0)


def gather_weight(n_pair, which, index_ref, same_ref, other_ref, weight_ref):
    depth = weight_ref.shape[0] // (2 * n_pair)
    if same_ref.shape[0] != n_pair:
        weight_ref[...] = same_ref[which]
        return
    pair, core = index_ref[0], index_ref[1]
    for step in range(n_pair):
        source = lax.rem(pair - step + n_pair, n_pair)
        for parts_ref, of_core in ((same_ref, core), (other_ref, 1 - core)):
            shard = source * 2 + of_core
            rows = pl.ds(pl.multiple_of(shard * depth, depth), depth)
            weight_ref[rows] = parts_ref[step, which * depth : (which + 1) * depth]


def convolved(rows, row, taps_ref, weight_ref):
    frames_each, _, width, depth = taps_ref.shape
    summed = None
    for row_tap in range(3):
        patches = taps_ref[:, row + row_tap : row + row_tap + rows]
        product = jnp.dot(
            patches.reshape(frames_each * rows * width, depth),
            weight_ref[row_tap * depth : (row_tap + 1) * depth],
            preferred_element_type=F32,
        )
        summed = product if summed is None else summed + product
    return summed


def first_body(
    n_pair,
    n_others,
    index_ref,
    blended_ref,
    from_above_ref,
    from_below_ref,
    own_ref,
    *refs,
):
    others, refs = refs[:n_others], refs[n_others:]
    (
        same_ref, other_ref, gain_ref, shift_ref, bias_ref,
        out_ref, down_ref, up_ref, stats_ref,
        taps_ref, weight_ref, scale_ref, offset_ref,
    ) = refs
    frames_each, rows, width, channels = blended_ref.shape
    edge = frames_each * width
    stats = [own_ref[...], from_above_ref[edge:]]
    if n_pair > 2:
        stats.append(from_below_ref[edge:])
    stats = stats + [ref[...] for ref in others]
    normed_taps(
        n_pair, index_ref, blended_ref, from_above_ref, from_below_ref, stats,
        gain_ref, shift_ref, taps_ref, scale_ref, offset_ref,
    )
    gather_weight(n_pair, 0, index_ref, same_ref, other_ref, weight_ref)
    summed = convolved(rows, 0, taps_ref, weight_ref) + bias_ref[...]
    out_ref[...] = summed.astype(BF16).reshape(frames_each, rows, width, channels)
    write_messages(out_ref, down_ref, up_ref, stats_ref)


def second_body(
    n_pair,
    n_others,
    index_ref,
    field_ref,
    from_above_ref,
    from_below_ref,
    own_ref,
    *refs,
):
    others, refs = refs[:n_others], refs[n_others:]
    (
        same_ref, other_ref, gain_ref, shift_ref, bias_ref, blended_ref,
        kept_ref, sent_ref,
        taps_ref, weight_ref, scale_ref, offset_ref, whole_ref,
    ) = refs
    frames_each, rows, width, channels = field_ref.shape
    edge = frames_each * width
    stats = [own_ref[...], from_above_ref[edge:]]
    if n_pair > 2:
        stats.append(from_below_ref[edge:])
    stats = stats + [ref[...] for ref in others]
    normed_taps(
        n_pair, index_ref, field_ref, from_above_ref, from_below_ref, stats,
        gain_ref, shift_ref, taps_ref, scale_ref, offset_ref,
    )
    gather_weight(n_pair, 1, index_ref, same_ref, other_ref, weight_ref)
    core, count = index_ref[1], index_ref[2]
    summed = convolved(rows, 0, taps_ref, weight_ref) + bias_ref[...]
    summed = summed.reshape(frames_each, rows, width, channels) + blended_ref[...].astype(F32)
    half = rows // 2
    for frame in range(frames_each):
        live = core * frames_each + frame < count
        whole_ref[frame] = jnp.where(live, summed[frame], 0.0).astype(BF16)
    kept_ref[...] = whole_ref[:, pl.ds(core * half, half)]
    sent_ref[...] = whole_ref[:, pl.ds((1 - core) * half, half)]


def most_and_helper(counts, n_owner, room):
    most, high = jnp.int32(0), counts[0]
    for owner in range(1, n_owner):
        count = counts[owner]
        most, high = jnp.where(count > high, owner, most), jnp.maximum(count, high)
    helper, near = jnp.int32(0), jnp.int32(2 * n_owner)
    for owner in range(n_owner):
        away = jnp.where((counts[owner] > room) | (most == owner), 2 * n_owner, jnp.abs(most - owner))
        helper, near = jnp.where(away < near, owner, helper), jnp.minimum(away, near)
    return most, helper


def pick_frames_body(
    capacity, given_ref, video_ref, out_ref, held_ref, placed_ref, counts_ref, load_sems, sems
):
    read = pltpu.make_async_copy(given_ref, counts_ref, load_sems.at[0])
    load = pltpu.make_async_copy(video_ref, held_ref, load_sems.at[1])
    read.start()
    load.start()
    read.wait()
    frames, (parts, sent) = video_ref.shape[0], out_ref.shape[:2]
    n_owner = counts_ref.shape[0]
    span, each = parts // n_owner, sent - 1
    most, least = most_and_helper(counts_ref, n_owner, each * (span - 2))
    last = frame_offset(counts_ref, most) + (capacity - 2 * each)
    load.wait()
    copies = []
    for owner in range(n_owner):
        offset = frame_offset(counts_ref, owner)
        for part in range(span):
            pair, core = part // 2, part % 2
            base = offset + 2 * each * pair
            if pair == span // 2 - 1:
                base = jnp.where(least == owner, last, base)
            for place in range(sent):
                frame = base + (2 * each - 1 - place if core else place - 2)
                values = held_ref[jnp.clip(frame, 0, frames - 1)]
                if not core and place < 2:
                    values = jnp.where(frame >= 0, values, jnp.zeros_like(values))
                placed_ref[owner * span + part, place] = values
        rows = pl.ds(owner * span, span)
        copies.append(
            pltpu.make_async_copy(placed_ref.at[rows], out_ref.at[rows], sems.at[owner])
        )
        copies[-1].start()
    for copy in copies:
        copy.wait()


def group_spread(values, width_group):
    lane = lax.broadcasted_iota(jnp.int32, values.shape, 1) % width_group
    size, total = values.shape[1], values
    for step in range(1, width_group):
        total = total + jnp.where(
            lane >= step,
            pltpu.roll(values, step, 1),
            pltpu.roll(values, size - width_group + step, 1),
        )
    return total


def interleave(main, side, pace):
    for _ in main:
        for _ in range(pace):
            next(side, None)
    for _ in side:
        pass


def dot_pieces(source_ref, weight_ref, total_ref, add, parts=2):
    rows, width, depth = source_ref.shape
    part_rows = (rows - 2) // parts
    cells = part_rows * width
    for part in range(parts):
        summed = None
        for row_tap in range(3):
            low = part * part_rows + row_tap
            product = jnp.dot(
                source_ref[low : low + part_rows].reshape(cells, depth),
                weight_ref[row_tap * depth : (row_tap + 1) * depth],
                preferred_element_type=F32,
            )
            summed = product if summed is None else summed + product
            yield
        if add:
            total_ref[part * cells : (part + 1) * cells] += summed
        else:
            total_ref[part * cells : (part + 1) * cells] = summed


def norm_pieces(field_ref, normed_ref, row_of, gain, shift):
    all_rows, width, channels = field_ref.shape
    cells, width_group = all_rows * width, channels // GROUPS
    pivot = None
    sums = squares = jnp.zeros((8, channels), F32)
    for row in range(all_rows):
        if row_of is None:
            values = field_ref[row].astype(F32)
        else:
            rounded = row_of(row).astype(BF16)
            field_ref[row] = rounded
            values = rounded.astype(F32)
        if pivot is None:
            pivot = values[:1]
        apart = (values - pivot).reshape(width // 8, 8, channels)
        sums = sums + jnp.sum(apart, axis=0)
        squares = squares + jnp.sum(apart * apart, axis=0)
        if row % 4 == 3:
            yield
    own = jnp.sum(sums, axis=0, keepdims=True) * (1.0 / cells)
    squares = jnp.sum(squares, axis=0, keepdims=True) * (1.0 / cells)
    sample = 1.0 / width_group
    mean = group_spread(own + pivot, width_group) * sample
    off = own + pivot - mean
    spread = squares - own * own + off * off
    variance = jnp.maximum(group_spread(spread, width_group) * sample, 0.0)
    scale = lax.rsqrt(variance + EPS) * gain
    offset = 0.5 * (shift - mean * scale)
    scale = 0.5 * scale
    yield
    for row in range(all_rows):
        half = field_ref[row].astype(F32) * scale + offset
        normed_ref[row + 1] = with_column_taps(half + half * jnp.tanh(half))
        if row % 2 == 1:
            yield


def clear_borders(refs):
    for ref in refs:
        border = jnp.zeros(ref.shape[1:], BF16)
        ref[0] = border
        ref[ref.shape[0] - 1] = border


def start_all(copies):
    for copy in copies:
        copy.start()


def wait_all(copies):
    for copy in copies:
        copy.wait()


def frames_body(n_height, part_ref, swapped_ref, temporal_ref, bias_ref, gain_ref, shift_ref, *refs):
    normed_out_ref, blended_out_ref, order_ref, *refs = refs
    order_ref[...] = jnp.zeros_like(order_ref)
    each, all_rows, width, channels = blended_out_ref.shape
    places = each + 2
    taps_refs, refs = refs[:places], refs[places:]
    total_refs, refs = refs[:each], refs[each:]
    raw_ref, time_ref, time_sems = refs
    n_frame = part_ref.shape[0] // n_height
    columns, rows = width // n_frame, all_rows // n_height
    depth = 3 * channels
    core = lax.axis_index("core")

    time_copies = []
    for step in range(3):
        tap = step + core * (2 - 2 * step)
        begin = pl.multiple_of(tap * 3 * depth, 3 * depth)
        time_copies.append(
            pltpu.make_async_copy(
                temporal_ref.at[pl.ds(begin, 3 * depth)], time_ref.at[step], time_sems.at[step]
            )
        )
    start_all(time_copies)
    normed_refs = [normed_out_ref.at[place] for place in range(each - 1)]
    clear_borders(list(taps_refs) + normed_refs)

    def piece_of(place, source):
        return part_ref[source, place] if place <= each else swapped_ref[source]

    def lay(place):
        for height in range(n_height):
            pieces = [
                piece_of(place, peer * n_height + height).astype(F32) for peer in range(n_frame)
            ]
            for row in range(rows):
                values = jnp.concatenate(
                    [piece[row * columns : (row + 1) * columns] for piece in pieces], axis=0
                )
                raw_ref[place, height * rows + row] = values.astype(BF16)
                taps_refs[place][height * rows + row + 1] = with_column_taps(silu(values))
            yield

    def temporal(place, step):
        if place == 0:
            time_copies[step].wait()
        return dot_pieces(taps_refs[place + step], time_ref.at[step], total_refs[place], step > 0)

    def blended_row(place):
        raw_at = place + 2 - 2 * core

        def row_of(row):
            product = total_refs[place][row * width : (row + 1) * width]
            return raw_ref[raw_at, row].astype(F32) + product + bias_ref[...]

        return row_of

    nothing = iter(())
    for place in range(3):
        interleave(lay(place), nothing, 0)
    rest = itertools.chain.from_iterable(lay(place) for place in range(3, places))
    pieces = itertools.chain.from_iterable(temporal(0, step) for step in range(3))
    interleave(pieces, rest, 1)
    for place in range(1, each):
        norm = norm_pieces(
            blended_out_ref.at[place - 1], normed_refs[place - 1], blended_row(place - 1),
            gain_ref[...], shift_ref[...],
        )
        pieces = itertools.chain.from_iterable(temporal(place, step) for step in range(3))
        interleave(pieces, norm, 1)
    row_of = blended_row(each - 1)
    for row in range(all_rows):
        blended_out_ref[each - 1, row] = row_of(row).astype(BF16)


def spatial_body(n_pair, normed_ref, blended_ref, order_ref, *refs):
    same_refs, refs = refs[:n_pair], refs[n_pair:]
    other_refs, refs = refs[:n_pair], refs[n_pair:]
    gain_ref, shift_ref, first_bias_ref, second_gain_ref, second_shift_ref, *refs = refs
    second_bias_ref, out_ref, *refs = refs
    n_height, each, rows, width, channels = out_ref.shape
    all_rows = n_height * rows
    normed_refs, refs = refs[:each], refs[each:]
    total_refs, refs = refs[:each], refs[each:]
    field_refs, refs = refs[:each], refs[each:]
    weights_ref, done_ref, out_sems = refs
    pair, core = lax.axis_index("pair"), lax.axis_index("core")
    span = same_refs[0].shape[1]

    def gather(which):
        for step in range(n_pair):
            for shard_ref, of_core in ((same_refs[step], core), (other_refs[step], 1 - core)):
                source = jnp.bitwise_xor(pair, step) * 2 + of_core
                begin = pl.multiple_of(source * span, span)
                weights_ref[which, pl.ds(begin, span)] = shard_ref[which]
                yield

    clear_borders(normed_refs)

    def first_source(place):
        return normed_ref.at[place] if place < each - 1 else normed_refs[place]

    def second_norm(place):
        def row_of(row):
            return total_refs[place][row * width : (row + 1) * width] + first_bias_ref[...]

        return norm_pieces(
            field_refs[place], normed_refs[place], row_of, second_gain_ref[...],
            second_shift_ref[...],
        )

    def finish(place):
        at = place + core * (each - 1 - 2 * place)
        for row in range(all_rows):
            product = total_refs[place][row * width : (row + 1) * width] + second_bias_ref[...]
            decoded = blended_ref[place, row].astype(F32) + product
            done_ref[place, row // rows, row % rows] = decoded.astype(BF16)
            if row % 4 == 3:
                yield
        stores.append(
            pltpu.make_async_copy(done_ref.at[place], out_ref.at[:, at], out_sems.at[place])
        )
        stores[-1].start()

    stores = []
    pending = norm_pieces(
        blended_ref.at[each - 1], normed_refs[each - 1], None, gain_ref[...], shift_ref[...]
    )
    interleave(gather(0), iter(()), 0)
    for place in range(each):
        interleave(
            dot_pieces(first_source(place), weights_ref.at[0], total_refs[place], False),
            pending, 4,
        )
        pending = second_norm(place)
        if place == 0:
            pending = itertools.chain(gather(1), pending)
    for place in range(each):
        interleave(
            dot_pieces(normed_refs[place], weights_ref.at[1], total_refs[place], False),
            pending, 3,
        )
        pending = finish(place)
    interleave(pending, iter(()), 0)
    wait_all(stores)


def route_body(room, counts_ref, route_ref):
    n_owner = counts_ref.shape[0]
    most, helper = most_and_helper(counts_ref, n_owner, room)
    route_ref[0] = most * n_owner + helper


def place_body(counts_ref, owned_ref, extra_ref, out_ref):
    count, n_owned = counts_ref[lax.axis_index("frame")], owned_ref.shape[0]
    for slot in range(out_ref.shape[0]):
        values = owned_ref[slot] if slot < n_owned else extra_ref[slot - n_owned]
        out_ref[slot] = jnp.where(slot < count, values, jnp.zeros_like(values))


def partners(size, step):
    return [(i, i ^ step) for i in range(size)]


def whole_frames(
    video, frame_counts, temporal_weight, temporal_bias, first_gain, first_shift, first_weight,
    first_bias, second_gain, second_shift, second_weight, second_bias,
):
    frames, rows, columns, channels = video.shape
    n_frame, n_pair = lax.axis_size("frame"), lax.axis_size("pair")
    n_height = 2 * n_pair
    width = columns * n_frame
    all_rows = rows * n_height
    capacity = slots_of(frames, n_frame)
    each = capacity // n_height
    extra = capacity - each * n_height
    params = pltpu.CompilerParams(vmem_limit_bytes=60 * 1024 * 1024)
    swap = [(0, 1), (1, 0)]

    picked = pl.pallas_call(
        functools.partial(pick_frames_body, capacity),
        out_shape=jax.ShapeDtypeStruct(
            (n_frame * n_height, each + 1, rows * columns, channels), BF16
        ),
        in_specs=[HBM, HBM],
        out_specs=HBM,
        scratch_shapes=[
            pltpu.VMEM((frames, rows * columns, channels), BF16),
            pltpu.VMEM((n_frame * n_height, each + 1, rows * columns, channels), BF16),
            pltpu.SMEM(frame_counts.shape, jnp.int32),
            pltpu.SemaphoreType.DMA((2,)),
            pltpu.SemaphoreType.DMA((n_frame,)),
        ],
        compiler_params=params,
        name="pick",
    )(frame_counts, video.reshape(frames, rows * columns, channels))
    parts = lax.all_to_all(picked, ("frame", "pair", "core"), split_axis=0, concat_axis=0)
    swapped = lax.ppermute(parts[:, each], "core", swap)

    own = jnp.stack([first_weight, second_weight])
    same = [own] + [
        lax.ppermute(own, "pair", partners(n_pair, step)) for step in range(1, n_pair)
    ]

    def row_of(vector):
        return vector.reshape(1, channels)

    field = (all_rows, width, channels)
    taps = (all_rows + 2, width, 3 * channels)
    total = pltpu.VMEM((all_rows * width, channels), F32)
    limit = pltpu.CompilerParams(vmem_limit_bytes=50 * 1024 * 1024)
    normed, blended, order = pl.pallas_call(
        functools.partial(frames_body, n_height),
        out_shape=(
            jax.ShapeDtypeStruct((max(each - 1, 1),) + taps, BF16),
            jax.ShapeDtypeStruct((each,) + field, BF16),
            jax.ShapeDtypeStruct((8, 128), F32),
        ),
        in_specs=[VMEM, VMEM, HBM] + [VMEM] * 3,
        out_specs=(VMEM,) * 3,
        scratch_shapes=[pltpu.VMEM(taps, BF16)] * (each + 2)
        + [total] * each
        + [
            pltpu.VMEM((each + 2,) + field, BF16),
            pltpu.VMEM((3, 9 * channels, channels), BF16),
            pltpu.SemaphoreType.DMA((3,)),
        ],
        compiler_params=limit,
        name="frames",
    )(
        parts, swapped, temporal_weight,
        row_of(temporal_bias), row_of(first_gain), row_of(first_shift),
    )
    same[1:], order = lax.optimization_barrier((same[1:], order))
    other = [lax.ppermute(shard, "core", swap) for shard in same]
    decoded = pl.pallas_call(
        functools.partial(spatial_body, n_pair),
        out_shape=jax.ShapeDtypeStruct((n_height, each, rows, width, channels), BF16),
        in_specs=[VMEM] * (9 + 2 * n_pair),
        out_specs=HBM,
        scratch_shapes=[pltpu.VMEM(taps, BF16)] * each
        + [total] * each
        + [pltpu.VMEM(field, BF16)] * each
        + [
            pltpu.VMEM((2, 9 * channels, channels), BF16),
            pltpu.VMEM((each, n_height, rows, width, channels), BF16),
            pltpu.SemaphoreType.DMA((each,)),
        ],
        compiler_params=pltpu.CompilerParams(vmem_limit_bytes=20 * 1024 * 1024),
        name="spatial",
    )(
        normed, blended, order, *same, *other,
        row_of(first_gain), row_of(first_shift), row_of(first_bias),
        row_of(second_gain), row_of(second_shift), row_of(second_bias),
    )
    owned = lax.all_to_all(decoded, ("pair", "core"), split_axis=0, concat_axis=0)
    owned = owned.reshape((n_height * each,) + owned.shape[2:])
    if extra:
        route = pl.pallas_call(
            functools.partial(route_body, each * (n_height - 2)),
            out_shape=jax.ShapeDtypeStruct((1,), jnp.int32),
            in_specs=[SMEM],
            out_specs=SMEM,
            name="route",
        )(frame_counts)

        def homeward(pairing):
            source, target = pairing % n_frame, pairing // n_frame
            if source == target:
                return jnp.zeros_like
            return lambda rows: lax.ppermute(rows, "frame", [(source, target)])

        late = lax.switch(
            route[0],
            [homeward(pairing) for pairing in range(n_frame * n_frame)],
            owned[-extra:],
        )
    else:
        late = owned[:1]
    return pl.pallas_call(
        place_body,
        out_shape=jax.ShapeDtypeStruct((capacity,) + owned.shape[1:], BF16),
        in_specs=[SMEM, VMEM, VMEM],
        out_specs=VMEM,
        compiler_params=pltpu.CompilerParams(vmem_limit_bytes=20 * 1024 * 1024),
        name="place",
    )(frame_counts, owned, late)


def split_rows(
    video,
    frame_counts,
    temporal_weight,
    temporal_bias,
    first_gain,
    first_shift,
    first_weight,
    first_bias,
    second_gain,
    second_shift,
    second_weight,
    second_bias,
):
    frames, rows, columns, channels = video.shape
    n_frame, n_pair = lax.axis_size("frame"), lax.axis_size("pair")
    width = columns * n_frame
    capacity = slots_of(frames, n_frame)
    frames_each = up_to(capacity, 2) // 2
    slots = frames_each + 2
    all_rows = 2 * rows
    edge = frames_each * width
    span = up_to(2 * frames_each, 16)
    params = pltpu.CompilerParams(vmem_limit_bytes=20 * 1024 * 1024)

    def ring(step):
        return [(i, (i + step) % n_pair) for i in range(n_pair)]

    def line(step):
        return [(i, i + step) for i in range(n_pair) if 0 <= i + step < n_pair]

    def struct(shape, dtype=BF16):
        return jax.ShapeDtypeStruct(shape, dtype)

    def row_of(vector):
        return vector.reshape(1, channels)

    pair, core = lax.axis_index("pair"), lax.axis_index("core")
    owner = lax.axis_index("frame")
    my_count = lax.dynamic_index_in_dim(frame_counts, owner, keepdims=False)
    index = jnp.stack([pair, core, my_count]).astype(jnp.int32)

    picked = pl.pallas_call(
        functools.partial(pick_body, 2, frames_each),
        out_shape=struct((n_frame * 2, slots, rows * columns, channels)),
        in_specs=[SMEM, VMEM],
        out_specs=VMEM,
        compiler_params=params,
        name="pick",
    )(frame_counts, video.reshape(frames, rows * columns, channels))
    parts = lax.all_to_all(picked, ("frame", "core"), split_axis=0, concat_axis=0)

    if first_weight.shape[0] % 16 == 0 and n_pair > 2:
        own_weights = jnp.concatenate([first_weight, second_weight], axis=0)
        same = jnp.stack(
            [own_weights]
            + [lax.ppermute(own_weights, "pair", ring(step)) for step in range(1, n_pair)]
        )
        other = lax.ppermute(same, "core", [(0, 1), (1, 0)])
    else:
        both = (first_weight, second_weight)
        same = jnp.stack([lax.all_gather(w, ("pair", "core"), tiled=True) for w in both])
        other = jnp.zeros((16, channels), BF16)

    by_place = parts.reshape(n_frame, 2, slots, rows, columns, channels)

    def edge_row(array):
        return array.transpose(1, 0, 2, 3).reshape(slots, width, channels)

    above = lax.ppermute(edge_row(by_place[:, 1, :, rows - 1]), "pair", line(1))
    below = lax.ppermute(edge_row(by_place[:, 0, :, 0]), "pair", line(-1))

    total = pl.pallas_call(
        functools.partial(temporal_body, 2, rows),
        out_shape=struct((frames_each, all_rows, width, channels), F32),
        in_specs=[VMEM] * 3,
        out_specs=VMEM,
        scratch_shapes=[pltpu.VMEM((slots, all_rows, width, 3 * channels), BF16)],
        compiler_params=params,
        name="temporal",
    )(parts, temporal_weight, row_of(temporal_bias))

    field = struct((frames_each, all_rows, width, channels))
    message = struct((edge + 3 * span, channels))
    stats_struct = struct((3 * span, channels))

    blended, down, up, stats = pl.pallas_call(
        functools.partial(borders_body, n_pair),
        out_shape=(field, message, message, stats_struct),
        in_specs=[VMEM] * 4,
        out_specs=(VMEM,) * 4,
        scratch_shapes=[pltpu.VMEM((2, slots, width, 3 * channels), BF16)],
        compiler_params=params,
        name="borders",
    )(total, above, below, temporal_weight)

    def exchange(down, up, stats):
        from_above = lax.ppermute(down, "pair", ring(1))
        from_below = lax.ppermute(up, "pair", ring(-1))
        others = [lax.ppermute(stats, "pair", ring(step)) for step in range(2, n_pair - 1)]
        return from_above, from_below, others

    def scratch():
        return [
            pltpu.VMEM((frames_each, all_rows + 2, width, 3 * channels), BF16),
            pltpu.VMEM((9 * channels, channels), BF16),
            pltpu.VMEM((frames_each, 1, channels), F32),
            pltpu.VMEM((frames_each, 1, channels), F32),
        ]

    from_above, from_below, others = exchange(down, up, stats)
    first_out, down, up, stats = pl.pallas_call(
        functools.partial(first_body, n_pair, len(others)),
        out_shape=(field, message, message, stats_struct),
        in_specs=[SMEM] + [VMEM] * (9 + len(others)),
        out_specs=(VMEM,) * 4,
        scratch_shapes=scratch(),
        compiler_params=params,
        name="first",
    )(
        index, blended, from_above, from_below, stats, *others, same, other,
        row_of(first_gain), row_of(first_shift), row_of(first_bias),
    )

    from_above, from_below, others = exchange(down, up, stats)
    half = struct((frames_each, rows, width, channels))
    kept, sent = pl.pallas_call(
        functools.partial(second_body, n_pair, len(others)),
        out_shape=(half, half),
        in_specs=[SMEM] + [VMEM] * (10 + len(others)),
        out_specs=(VMEM,) * 2,
        scratch_shapes=scratch() + [pltpu.VMEM(field.shape, BF16)],
        compiler_params=params,
        name="second",
    )(
        index, first_out, from_above, from_below, stats, *others, same, other,
        row_of(second_gain), row_of(second_shift), row_of(second_bias), blended,
    )
    received = lax.ppermute(sent, "core", [(0, 1), (1, 0)])
    early = jnp.where(core == 0, kept, received)
    late = jnp.where(core == 0, received, kept)
    return jnp.concatenate([early, late], axis=0)[:capacity]


def per_device(video, *rest):
    frames, n_frame = video.shape[0], lax.axis_size("frame")
    n_height = lax.axis_size("pair") * lax.axis_size("core")
    capacity = slots_of(frames, n_frame)
    each, extra = divmod(capacity, n_height)
    room = each * (n_height - 2)
    n_pair = lax.axis_size("pair")
    fits = each > 0 and extra <= 2 * each and n_frame > 1 and n_pair > 1
    fits = fits and n_pair & (n_pair - 1) == 0
    if fits and 2 * (each * n_height + 1) > frames and frames - capacity < n_frame * room:
        return whole_frames(video, *rest)
    return split_rows(video, *rest)


def solution(mesh):
    n_frame, n_height = mesh.devices.shape
    split = Mesh(mesh.devices.reshape(n_frame, n_height // 2, 2), ("frame", "pair", "core"))
    height = ("pair", "core")
    placed = (
        P(None, height, "frame", None),
        P(),
        P(),
        P(),
        P(),
        P(),
        P(height, None),
        P(),
        P(),
        P(),
        P(height, None),
        P(),
    )
    return jax.shard_map(
        per_device,
        mesh=split,
        in_specs=placed,
        out_specs=P("frame", height, None, None),
        check_vma=False,
    )
```
